256 devices in a mesh: gx: 8 (over z_hi, core), gy: 4 (over x), gz: 8 (over z_lo, y).
Axes of the slice: x: 4, y: 4, z: 8 (z_hi: 4, z_lo: 2; z = z_hi * 2 + z_lo), core: 2. Of those that a mesh axis runs over, the one named last changes fastest.
Arguments:
- density: float32 [128, 64, 1024], P('gx', 'gy', 'gz'), may hold values from -6 to 6
- atom_site: float32 [3, 8, 4, 8, 16], P(None, 'gx', 'gy', 'gz'), may hold values from 2 to 6
- atom_charge: float32 [8, 4, 8, 16], P('gx', 'gy', 'gz'), may hold values from 2 to 8
- slot_atom: int32 [8, 4, 8, 32, 2], P('gx', 'gy', 'gz'), may hold values from 0 to 15
- slot_tile: int32 [8, 4, 8, 32, 2], P('gx', 'gy', 'gz'), may hold values from 0 to 63
- slot_shift: int32 [3, 8, 4, 8, 32, 2], P(None, 'gx', 'gy', 'gz'), may hold values from -1 to 1
Outputs:
- potential: float32 [128, 64, 1024], P('gx', 'gy', 'gz')
- residual: float32 [128, 64, 1024], P('gx', 'gy', 'gz')
The draws below stay inside these ranges and needn't reach their ends.
Inputs may be any that keep to these rules, and one draw needn't show every extreme that they name: `slot_atom`: an index into the 16 atoms of the device that holds the slot.
All inputs are finite; a program needn't handle non-finite values.
Results may differ from the reference program's by a relative error of at most 0.0003.
Values sent between devices are 32-bit elements; how exact they have to be, the bound alone decides.
No kernel may reach another device: no remote copies, remote signals or barrier semaphores. Data moves between devices by JAX's collectives and lax.ppermute only.
A program may use at most 64 MiB of HBM per device.

```python
import math
import jax
import jax.numpy as jnp
from jax import lax

CX = 16
CY = 16
CZ = 128
EDGE = 8
ATOM_DEV = 16
CAP = 2
ITERS = 9
PERIOD = 3
NX = 128
NY = 64
NZ = 1024
PLANE = 32
TILES = 64
N_GX = 8
N_GY = 4
N_GZ = 8


def set_ends(result, rng, least, top_value):
    shape = result.shape
    index_at = [jax.random.randint(jax.random.fold_in(rng, axis), (), 0, shape[axis]) for axis in range(len(shape))]
    result = result.at[tuple(index_at)].set(least)
    longest = shape.index(max(shape))
    index_at[longest] = (index_at[longest] + 1) % shape[longest]
    return result.at[tuple(index_at)].set(top_value)


def shard_levels(rng, shape, shards, least, top_value):
    def one(position, shards_of):
        steps = jax.random.uniform(jax.random.fold_in(jax.random.fold_in(rng, 6), position), (shards_of,), jnp.float32, least / len(shards), top_value / len(shards))
        return jnp.repeat(jnp.exp(steps), shape[position] // shards_of).reshape((-1,) + (1,) * (len(shape) - position - 1))

    level = one(*shards[0])
    for cut in shards[1:]:
        level = level * one(*cut)
    return level


def gaussian(stream_key, extent, deviation, most, shards=(), kind=jnp.bfloat16):
    loudness = shard_levels(stream_key, extent, shards, -0.22, 0.18) if shards else 1.0
    drawn = jax.random.normal(stream_key, extent, jnp.float32) * deviation * loudness
    return jnp.minimum(jnp.maximum(drawn, -most), most).astype(kind)


def setup_inputs(seed: int = 0) -> dict:
    key_of = jax.random.split(jax.random.key(seed), 7)
    return {
        "density": gaussian(key_of[0], (NX, NY, NZ), 1.0, 6.0, ((0, 8), (1, 4), (2, 8)), jnp.float32),
        "atom_site": jnp.clip(2.0 + 4.0 * jax.random.uniform(key_of[1], (3, N_GX, N_GY, N_GZ, ATOM_DEV), jnp.float32) ** shard_levels(key_of[1], (3, N_GX, N_GY, N_GZ, ATOM_DEV), ((1, 8), (2, 4), (3, 8)), -0.2, 0.2), 2.0, 6.0),
        "atom_charge": jnp.clip(jnp.exp(math.log(8.0) - 1.3862944 * jax.random.uniform(key_of[2], (N_GX, N_GY, N_GZ, ATOM_DEV), jnp.float32) ** shard_levels(key_of[2], (N_GX, N_GY, N_GZ, ATOM_DEV), ((0, 8), (1, 4), (2, 8)), -0.2, 0.2)), 2.0, 8.0),
        "slot_atom": set_ends(jax.random.randint(key_of[3], (N_GX, N_GY, N_GZ, PLANE, CAP), 0, ATOM_DEV), jax.random.fold_in(key_of[3], 1), 0, ATOM_DEV - 1).astype(jnp.int32),
        "slot_tile": set_ends(jax.random.randint(key_of[4], (N_GX, N_GY, N_GZ, PLANE, CAP), 0, TILES), jax.random.fold_in(key_of[4], 1), 0, TILES - 1).astype(jnp.int32),
        "slot_shift": set_ends(jax.random.randint(key_of[5], (3, N_GX, N_GY, N_GZ, PLANE, CAP), -1, 2), jax.random.fold_in(key_of[5], 1), -1, 1).astype(jnp.int32),
    }


METRIC = [[3.24, 0.972, 0.648], [0.972, 3.2157, 0.9639], [0.648, 0.9639, 2.9565]]
INVERSE = [[0.3450043297, -0.0904572938, -0.0461258313],
           [-0.0904572938, 0.3683733435, -0.1002735462],
           [-0.0461258313, -0.1002735462, 0.3810394757]]
FIRST_WEIGHTS = [6.0 / 7.0, -15.0 / 56.0, 5.0 / 63.0, -1.0 / 56.0, 2.0 / 385.0, -1.0 / 5544.0]
SECOND_WEIGHTS = [12.0 / 7.0, -15.0 / 56.0, 10.0 / 189.0, -1.0 / 112.0, 4.0 / 1925.0, -1.0 / 16632.0]
CENTER_WEIGHT = -2.0 * (12.0 / 7.0 - 15.0 / 56.0 + 10.0 / 189.0 - 1.0 / 112.0 + 4.0 / 1925.0 - 1.0 / 16632.0)
JACOBI_SCALE = 2.0 * (12.0 / 7.0 - 15.0 / 56.0 + 10.0 / 189.0 - 1.0 / 112.0 + 4.0 / 1925.0 - 1.0 / 16632.0) * (
    0.3450043297 + 0.3683733435 + 0.3810394757)
RELAX_STEP = 0.3
MIXING_STEP = 0.3
WIDTH_SQUARED = 9.0
RIDGE_SHARE = 0.01


def pseudo_blocks(site_x, site_y, site_z, weight, shift_x, shift_y, shift_z):
    edge_cells = jnp.arange(EDGE, dtype=jnp.float32)
    half_block = float(EDGE // 2)
    along_x = edge_cells[None, :] - site_x[:, None] - half_block * shift_x.astype(jnp.float32)[:, None]
    along_y = edge_cells[None, :] - site_y[:, None] - half_block * shift_y.astype(jnp.float32)[:, None]
    along_z = edge_cells[None, :] - site_z[:, None] - half_block * shift_z.astype(jnp.float32)[:, None]
    ex = along_x[:, :, None, None]
    ey = along_y[:, None, :, None]
    ez = along_z[:, None, None, :]
    radius = (METRIC[0][0] * ex * ex + METRIC[1][1] * ey * ey + METRIC[2][2] * ez * ez
              + 2.0 * METRIC[0][1] * ex * ey + 2.0 * METRIC[0][2] * ex * ez
              + 2.0 * METRIC[1][2] * ey * ez)
    return weight[:, None, None, None] * jnp.exp(-radius / WIDTH_SQUARED)


def mixing_weights(gram_sums):
    first_first = gram_sums[0]
    cross_term = gram_sums[1]
    second_second = gram_sums[2]
    first_proj = gram_sums[3]
    second_proj = gram_sums[4]
    ridge = RIDGE_SHARE * 0.5 * (first_first + second_second)
    first_first = first_first + ridge
    second_second = second_second + ridge
    determinant = first_first * second_second - cross_term * cross_term
    return ((second_second * first_proj - cross_term * second_proj) / determinant,
            (first_first * second_proj - cross_term * first_proj) / determinant)


def first_roll(field, axis):
    total = None
    for order, weight in enumerate(FIRST_WEIGHTS, start=1):
        term = weight * (jnp.roll(field, -order, axis) - jnp.roll(field, order, axis))
        total = term if total is None else total + term
    return total


def second_roll(field, axis):
    total = CENTER_WEIGHT * field
    for order, weight in enumerate(SECOND_WEIGHTS, start=1):
        total = total + weight * (jnp.roll(field, -order, axis) + jnp.roll(field, order, axis))
    return total


def apply_operator(field):
    cross = INVERSE[0][1] * first_roll(field, 1) + INVERSE[0][2] * first_roll(field, 2)
    mixed = first_roll(cross, 0) + INVERSE[1][2] * first_roll(first_roll(field, 2), 1)
    laplace = (INVERSE[0][0] * second_roll(field, 0) + INVERSE[1][1] * second_roll(field, 1)
               + INVERSE[2][2] * second_roll(field, 2) + 2.0 * mixed)
    return -laplace


def plane_charge(inputs):
    sites, charges, atoms, tiles, shifts = inputs
    plane_count = N_GY * N_GZ
    site_table = sites.reshape(3, plane_count, ATOM_DEV)
    chosen_atom = atoms.reshape(plane_count, plane_count * CAP)
    site_x = jnp.take_along_axis(site_table[0], chosen_atom, axis=1).reshape(-1)
    site_y = jnp.take_along_axis(site_table[1], chosen_atom, axis=1).reshape(-1)
    site_z = jnp.take_along_axis(site_table[2], chosen_atom, axis=1).reshape(-1)
    weight = jnp.take_along_axis(charges.reshape(plane_count, ATOM_DEV), chosen_atom, axis=1).reshape(-1)
    image_moves = shifts.reshape(3, -1)
    charge_blocks = pseudo_blocks(site_x, site_y, site_z, weight, image_moves[0], image_moves[1], image_moves[2])
    owner_rank = jnp.broadcast_to(jnp.arange(plane_count, dtype=jnp.int32)[None, :, None],
                                  (plane_count, plane_count, CAP)).reshape(-1)
    target_tile = owner_rank * TILES + tiles.reshape(-1).astype(jnp.int32)
    tile_sums = jax.ops.segment_sum(charge_blocks, target_tile, num_segments=plane_count * TILES)
    tile_grid = tile_sums.reshape(N_GY, N_GZ, CX // EDGE, CY // EDGE, CZ // EDGE, EDGE, EDGE, EDGE)
    return jnp.transpose(tile_grid, (2, 5, 0, 3, 6, 1, 4, 7)).reshape(CX, NY, NZ)


def reference(density, atom_site, atom_charge, slot_atom, slot_tile, slot_shift):
    pseudo = lax.map(plane_charge, (jnp.moveaxis(atom_site, 1, 0), atom_charge, slot_atom, slot_tile,
                                    jnp.moveaxis(slot_shift, 1, 0)))
    source = density + pseudo.reshape(NX, NY, NZ)
    potential = jnp.zeros_like(source)
    moves_x = []
    moves_f = []
    previous_potential = potential
    previous_scaled = potential
    residual = source
    for iteration in range(ITERS):
        residual = source - apply_operator(potential)
        scaled = residual / JACOBI_SCALE
        if iteration > 0:
            moves_x = (moves_x + [potential - previous_potential])[-2:]
            moves_f = (moves_f + [scaled - previous_scaled])[-2:]
        if (iteration + 1) % PERIOD == 0 and iteration > 0:
            gram_sums = jnp.stack([jnp.sum(moves_f[0] * moves_f[0]), jnp.sum(moves_f[0] * moves_f[1]),
                                   jnp.sum(moves_f[1] * moves_f[1]), jnp.sum(moves_f[0] * scaled),
                                   jnp.sum(moves_f[1] * scaled)])
            gamma_first, gamma_second = mixing_weights(gram_sums)
            updated = (potential + MIXING_STEP * scaled
                       - (moves_x[0] + MIXING_STEP * moves_f[0]) * gamma_first
                       - (moves_x[1] + MIXING_STEP * moves_f[1]) * gamma_second)
        else:
            updated = potential + RELAX_STEP * scaled
        previous_potential = potential
        previous_scaled = scaled
        potential = updated
    return potential, residual
```

```python
import functools

import jax
import jax.numpy as jnp
import numpy as np
from jax import lax
from jax.experimental import pallas as pl
from jax.experimental.pallas import tpu as pltpu
from jax.sharding import PartitionSpec as P


METRIC = np.array([[3.24, 0.972, 0.648], [0.972, 3.2157, 0.9639], [0.648, 0.9639, 2.9565]])
INVERSE = np.array(
    [
        [0.3450043297, -0.0904572938, -0.0461258313],
        [-0.0904572938, 0.3683733435, -0.1002735462],
        [-0.0461258313, -0.1002735462, 0.3810394757],
    ]
)
FIRST_WEIGHTS = np.array([6.0 / 7.0, -15.0 / 56.0, 5.0 / 63.0, -1.0 / 56.0, 2.0 / 385.0, -1.0 / 5544.0])
SECOND_WEIGHTS = 2.0 * FIRST_WEIGHTS / np.arange(1, 7)
CENTER_WEIGHT = -2.0 * SECOND_WEIGHTS.sum()
JACOBI_SCALE = float(-CENTER_WEIGHT * np.trace(INVERSE))
STEP = 0.3
WIDTH_SQUARED = 9.0
RIDGE_SHARE = 0.01
NX, NY, NZ = 128, 64, 1024
AXES = ("gx", "gy", "gz")
HI = lax.Precision.HIGHEST
LOG2E = float(np.log2(np.e))
MOMENTS = [(2, 0), (2, 1), (2, 2), (1, 2), (1, 3), (1, 8), (1, 9), (2, 6), (2, 7), (2, 8)]
MOMENTS += [(3, 4), (3, 5), (3, 6), (3, 7), (4, 2), (4, 3), (4, 4), (4, 5), (4, 6)]


def cos_sin(n, rows, columns):
    angle = 2.0 * np.pi * (np.outer(rows, columns) % n) / n
    return np.cos(angle), np.sin(angle)


def first_symbol(n):
    angle = 2.0 * np.pi * np.arange(n) / n
    return 2.0 * sum(w * np.sin((o + 1) * angle) for o, w in enumerate(FIRST_WEIGHTS))


def second_symbol(n):
    angle = 2.0 * np.pi * np.arange(n) / n
    return CENTER_WEIGHT + 2.0 * sum(w * np.cos((o + 1) * angle) for o, w in enumerate(SECOND_WEIGHTS))


@functools.lru_cache(maxsize=None)
def tables():
    eye = np.eye(32)
    freq = np.arange(128)
    c, s = cos_sin(128, freq, freq)
    t = {}
    t["z_tile"] = np.concatenate([c, -s], 0) / 32.0 / JACOBI_SCALE
    t["z_tile_back"] = np.concatenate([c, -s], 1) / 32.0
    t["twiddle"] = np.stack(cos_sin(1024, freq, np.arange(256) // 32))
    c, s = cos_sin(8, np.arange(8), np.arange(4))
    ahead = np.zeros((2, 8, 32, 384))
    into = ahead[..., :256].reshape(2, 8, 32, 4, 2, 32)
    back = np.zeros((384, 2, 8, 32))
    out = back[:256].reshape(4, 2, 32, 2, 8, 32)
    for k in range(8):
        for h in range(4):
            into[0, k, :, h, 0, :] = c[k, h] * eye
            into[1, k, :, h, 0, :] = s[k, h] * eye
            into[0, k, :, h, 1, :] = -s[k, h] * eye
            into[1, k, :, h, 1, :] = c[k, h] * eye
            out[h, 0, :, 0, k, :] = 2.0 * c[k, h] * eye
            out[h, 1, :, 0, k, :] = -2.0 * s[k, h] * eye
            out[h, 0, :, 1, k, :] = 2.0 * s[k, h] * eye
            out[h, 1, :, 1, k, :] = 2.0 * c[k, h] * eye
        ahead[0, k, :, 256:288] = (-1.0) ** k * eye
        back[256:288, 0, k, :] = (-1.0) ** k * eye
    t["z_cell"] = ahead.reshape(512, 384)
    t["z_cell_back"] = back.reshape(384, 512)
    half, b, j = np.meshgrid(np.arange(2), np.arange(4), np.arange(8), indexing="ij")
    c, s = cos_sin(64, (16 * b + 8 * half + j).reshape(-1), np.arange(64))
    c, s = c.reshape(2, 4, 8, 64) / 8.0, s.reshape(2, 4, 8, 64) / 8.0
    ahead = np.zeros((2, 2, 2, 4, 8, 2, 4, 64))
    back = np.zeros((2, 2, 64, 2, 2, 2, 4, 8))
    for f in range(2):
        ahead[:, f, 0, :, :, 0, f], ahead[:, f, 1, :, :, 0, f] = c, s
        ahead[:, f, 0, :, :, 1, f], ahead[:, f, 1, :, :, 1, f] = -s, c
        ct, st = np.moveaxis(c, 3, 0), np.moveaxis(s, 3, 0)
        back[0, f, :, :, f, 0], back[1, f, :, :, f, 0] = ct, -st
        back[0, f, :, :, f, 1], back[1, f, :, :, f, 1] = st, ct
    ahead[:, 0, 1, :, :, 0, 2], ahead[:, 0, 1, :, :, 1, 2] = c, -s
    t["y"], t["y_back"] = ahead.reshape(256, 512), back.reshape(256, 256)
    c, s = cos_sin(128, freq, freq)
    t["x"] = np.block([[c, s], [-s, c]]) / np.sqrt(128.0)
    t["x_back"] = np.block([[c, -s], [s, c]]) / np.sqrt(128.0)
    d1x, d1y, d1z = first_symbol(NX), first_symbol(NY), first_symbol(NZ)
    d2x, d2y, d2z = second_symbol(NX), second_symbol(NY), second_symbol(NZ)
    column = np.zeros((128, 128))
    column[:, 0], column[:, 1] = -INVERSE[0, 0] * d2x / JACOBI_SCALE, d1x
    rows = np.zeros((256, 512))
    for d in range(256):
        low = d % 128 + 256 * (d // 128)
        for f, kz in enumerate((low, low + 128, 512)):
            rows[d, 64 * f : 64 * f + 64] = (
                -(INVERSE[1, 1] * d2y + INVERSE[2, 2] * d2z[kz]) + 2.0 * INVERSE[1, 2] * d1y * d1z[kz]
            ) / JACOBI_SCALE
            rows[d, 256 + 64 * f : 320 + 64 * f] = (
                2.0 * (INVERSE[0, 1] * d1y + INVERSE[0, 2] * d1z[kz]) / JACOBI_SCALE
            )
    t["column"], t["rows"] = column, rows
    t["order"] = np.eye(256).reshape(4, 8, 8, 256).transpose(1, 0, 2, 3).reshape(256, 256).T
    k, j = np.repeat(np.arange(8), 8) - 3.5, np.tile(np.arange(8), 8) - 3.5
    shape = np.zeros((64, 128))
    shape[:, 0], shape[:, 1], shape[:, 2] = 1.0, j, k
    shape[:, 3] = -(METRIC[1, 1] * j * j + METRIC[2, 2] * k * k + 2.0 * METRIC[1, 2] * j * k)
    shape[:, 3] *= LOG2E / WIDTH_SQUARED
    t["shape"] = shape
    return {name: value.astype(np.float32) for name, value in t.items()}


def dot(a, b, contract=((1,), (0,))):
    return lax.dot_general(a, b, (contract, ((), ())), precision=HI, preferred_element_type=jnp.float32)


def index_of(shape, dim):
    return lax.broadcasted_iota(jnp.int32, shape, dim)


def solve(gram):
    ff, fc, cc, fs, cs = gram
    ridge = RIDGE_SHARE * 0.5 * (ff + cc)
    ff, cc = ff + ridge, cc + ridge
    determinant = ff * cc - fc * fc
    return (cc * fs - fc * cs) / determinant, (ff * cs - fc * fs) / determinant


def stack_rows(rows, count):
    at = index_of((count, 128), 0)
    stacked = jnp.zeros((count, 128), jnp.float32)
    for n, row in enumerate(rows):
        stacked = jnp.where(at == n, row, stacked)
    return stacked


def sums_on_lanes(arrays):
    rows = []
    for array in arrays:
        row = jnp.sum(array, axis=0, keepdims=True)
        rows.append(row[:, :128] + row[:, 128:])
    count = -(-len(rows) // 8) * 8
    totals = jnp.sum(stack_rows(rows, count), axis=1, keepdims=True)
    mine = index_of((count, 128), 0) == index_of((count, 128), 1)
    return jnp.sum(jnp.where(mine, totals, 0.0), axis=0, keepdims=True)


def picked(row, count):
    lane = index_of((1, 128), 1)
    return [jnp.sum(jnp.where(lane == n, row, 0.0), axis=1, keepdims=True) for n in range(count)]


def send_kernel(density, site, charge, atom, tile, shift, out):
    values = [jnp.zeros((2, 32), jnp.float32) for _ in range(4)]
    for n in range(16):
        hit = atom[...] == n
        for p in range(3):
            values[p] = jnp.where(hit, site[p, n], values[p])
        values[3] = jnp.where(hit, charge[0, n], values[3])
    for p in range(3):
        values[p] = values[p] + 4.0 * shift[p].astype(jnp.float32)
    code = tile[...]
    values.append(((code & 15) + 16 * (index_of((2, 32), 1) & 7)).astype(jnp.float32))
    values.append((code >> 4).astype(jnp.float32))
    lane = index_of((8, 128), 1)
    packed = jnp.zeros((8, 128), jnp.float32)
    for e in range(2):
        rows = [jnp.concatenate([v[e : e + 1], jnp.zeros((1, 96), jnp.float32)], 1) for v in values]
        rows = stack_rows(rows, 8)
        for b in range(4):
            moved = pltpu.roll(rows, 8 * b + 8 * e, 1)
            packed = jnp.where((lane >> 3) == 2 * b + e, moved, packed)
    for half in range(2):
        out[16 * half : 16 * half + 16, 0:8, :] = density[:, 8 * half : 8 * half + 8, :]
    out[:, 8:16, :] = jnp.broadcast_to(packed[None], (32, 8, 128))


def line_kernel(got, shape, order, z_tile, twiddle, z_cell, out, cells):
    rank = lax.axis_index("gy") * 8 + lax.axis_index("gz")
    x, half = rank & 15, rank >> 4
    own = ((x >> 3) * 2 + half).astype(jnp.float32)
    along = (x & 7).astype(jnp.float32)
    lane = index_of((8, 128), 1)
    sub = index_of((8, 512), 0)
    tile_at = index_of((128, 512), 0).astype(jnp.float32)
    scale = -LOG2E / WIDTH_SQUARED
    charge = []
    for b in range(4):
        parts = []
        for g in range(4):
            part = jnp.zeros((8, 128), jnp.float32)
            for r in range(8):
                moved = got[8 * g + r, 8:16, :]
                if r != b:
                    moved = pltpu.roll(moved, (16 * (r - b)) % 128, 1)
                part = jnp.where((lane >> 4) == r, moved, part)
            parts.append(part)
        slots = jnp.concatenate(parts, 1)
        ex = along - slots[0:1]
        vy, vz = slots[1:2] - 3.5, slots[2:3] - 3.5
        m = METRIC
        fixed = m[0, 0] * ex * ex + m[1, 1] * vy * vy + m[2, 2] * vz * vz
        fixed = fixed - 2.0 * m[0, 1] * ex * vy - 2.0 * m[0, 2] * ex * vz + 2.0 * m[1, 2] * vy * vz
        by_j = -2.0 * m[1, 1] * vy + 2.0 * m[0, 1] * ex - 2.0 * m[1, 2] * vz
        by_k = -2.0 * m[2, 2] * vz + 2.0 * m[0, 2] * ex - 2.0 * m[1, 2] * vy
        form = jnp.where(sub == 0, fixed, jnp.where(sub == 1, by_j, jnp.where(sub == 2, by_k, 0.0)))
        blocks = jnp.exp2(dot(shape[:, 0:8] * jnp.where(lane[0:1, 0:8] < 3, 1.0, 0.0), scale * form) + shape[:, 3:4])
        peak = jnp.where(slots[5:6] == own, slots[3:4], 0.0)
        placed = jnp.where(slots[4:5] == tile_at, peak, 0.0)
        charge.append(dot(placed, blocks, ((1,), (1,))))
    charge = dot(jnp.concatenate(charge, 1), order[...])
    for c in range(8):
        piece = jnp.concatenate([got[8 * b + c, 0:8, :] for b in range(4)], 0)
        cells[128 * c : 128 * c + 128, :] = jnp.transpose(jnp.concatenate([piece] * 4, 0))
    group = index_of((128, 128), 1) >> 5
    sides = []
    for side in range(2):
        total = jnp.zeros((128, 128), jnp.float32)
        for n in range(4):
            total = jnp.where(group == n, cells[pl.ds(4 * side + n, 128, stride=8), :], total)
        sides.append(total)
    field = jnp.concatenate(sides, 1) + charge
    spectrum = dot(z_tile[...], field)
    re, im = spectrum[:128], spectrum[128:]
    turned = jnp.concatenate([re * twiddle[0] + im * twiddle[1], im * twiddle[0] - re * twiddle[1]], 1)
    result = dot(turned, z_cell[...])
    last = pltpu.roll(result[:, 256:384], 32, 1)
    row, column = index_of((128, 128), 0), index_of((128, 128), 1)
    here = (row == 0) & ((column >> 5) == 1)
    out[0:128, :] = jnp.where(here, last, result[:, 0:128])
    out[128:256, :] = result[:, 128:256]


def eigenvalues(column, rows):
    rank = (lax.axis_index("gx") * 4 + lax.axis_index("gy")) * 8 + lax.axis_index("gz")
    mine = rows[pl.ds(rank, 1), :]
    return column[:, 0:1] + mine[:, 0:256] + column[:, 1:2] * mine[:, 256:512], rank


def weights_of(rank):
    field = index_of((1, 256), 1) >> 6
    first = jnp.where(field == 1, 2.0, jnp.where(field == 3, 0.0, 1.0))
    other = jnp.where(field < 2, 2.0, 0.0)
    return jnp.where(rank == 0, first, other)


def plane_kernel(got, y, x, column, rows, out_re, out_im, out):
    lam, rank = eigenvalues(column, rows)
    first = jnp.where(rank == 0, 1.0, 0.0).astype(jnp.float32)
    halves = [jnp.concatenate([got[32 * a + 16 * h : 32 * a + 16 * h + 16, :] for a in range(8)], 0) for h in range(2)]
    lines = dot(jnp.concatenate(halves, 1), y[...])
    spectrum = dot(x[...], jnp.concatenate([lines[:, :256], lines[:, 256:]], 0))
    re, im = spectrum[:128], spectrum[128:]
    re, im = (
        jnp.concatenate([re[:, :128] + first * im[:, 128:], re[:, 128:]], 1),
        jnp.concatenate([im[:, :128] - first * re[:, 128:], im[:, 128:]], 1),
    )
    out_re[...] = re
    out_im[...] = im
    a = STEP * lam
    mu = 1.0 - a
    power = (re * re + im * im) * weights_of(rank)
    products = {}
    for i in range(1, 5):
        power = power * a
        value = power
        for j in range(10):
            if j > 0:
                value = value * mu
            if (i, j) in MOMENTS:
                products[i, j] = value
            if j == max(n for m, n in MOMENTS if m == i):
                break
    row = sums_on_lanes([products[m] for m in MOMENTS])
    out[...] = jnp.broadcast_to(row, (256, 128))


def cycle_kernel(got, re_in, im_in, column, rows, x_back, y_back, out):
    sums = dict(zip(MOMENTS, picked(jnp.sum(got[...], axis=0, keepdims=True), len(MOMENTS))))
    g0, g1 = solve([sums[2, 0], sums[2, 1], sums[2, 2], -sums[1, 2], -sums[1, 3]])

    def again(i, j):
        return (
            sums[i, j + 6]
            + 2.0 * (g0 * sums[i + 1, j + 4] + g1 * sums[i + 1, j + 5])
            + g0 * g0 * sums[i + 2, j + 2]
            + 2.0 * g0 * g1 * sums[i + 2, j + 3]
            + g1 * g1 * sums[i + 2, j + 4]
        )

    h0, h1 = solve([again(2, 0), again(2, 1), again(2, 2), -again(1, 2), -again(1, 3)])
    lam, rank = eigenvalues(column, rows)
    first = jnp.where(rank == 0, 1.0, 0.0).astype(jnp.float32)
    re, im = re_in[...], im_in[...]
    a = STEP * lam
    mu = 1.0 - a
    mu2 = mu * mu
    after3 = mu * (mu2 + a * (g0 + mu * g1))
    after6 = after3 * mu * (mu2 + a * (h0 + mu * h1))
    after7 = after6 * mu
    after8 = after7 * mu
    steps = 1.0 + (1.0 - g0) * mu + (1.0 - g1) * mu2
    steps = steps + after3 * (1.0 + (1.0 - h0) * mu + (1.0 - h1) * mu2)
    steps = STEP * (steps + after6 + after7)
    power = (re * re + im * im) * weights_of(rank) * after6 * after6 * a
    low = power * mu2
    power = power * a
    row = sums_on_lanes([power, power * mu, power * mu2, low, low * mu])
    out[pl.ds(3, 256, stride=4), :] = jnp.broadcast_to(row, (256, 128))
    for f, multiplier in enumerate((steps, after7, after8)):
        fr, fi = multiplier * re, multiplier * im
        left = jnp.concatenate(
            [fr[:, :128] - first * fi[:, 128:], fi[:, :128] + first * fr[:, 128:]], 0
        )
        planes = dot(x_back[...], left)
        lines = dot(jnp.concatenate([planes[:128], planes[128:]], 1), y_back[...])
        for n in range(8):
            for h in range(2):
                out[pl.ds((32 * n + 16 * h) * 4 + f, 16, stride=4), :] = lines[
                    16 * n : 16 * n + 16, 128 * h : 128 * h + 128
                ]


def back_kernel(got, z_tile_back, twiddle, z_cell_back, out, cells):
    row = jnp.sum(got[pl.ds(3, 256, stride=4), :], axis=0, keepdims=True)
    s = picked(row, 5)
    g0, g1 = solve([s[0], s[1], s[2], -s[3], -s[4]])
    p8, s7, s8 = [got[pl.ds(f, 256, stride=4), :] for f in range(3)]
    at, column = index_of((128, 128), 0), index_of((128, 128), 1)
    spectra = [p8 + STEP * (1.0 - g1) * s8 - STEP * g0 * s7, JACOBI_SCALE * s8]
    fields = []
    for v in spectra:
        low, high = v[:128], v[128:]
        top = at == 0
        last = jnp.where(top & (column < 32), pltpu.roll(low, 96, 1), 0.0)
        low = jnp.where(top & (column < 64), jnp.where(column < 32, 0.5 * low, 0.0), low)
        result = dot(jnp.concatenate([low, high, last], 1), z_cell_back[...])
        re, im = result[:, :256], result[:, 256:]
        turned = jnp.concatenate([re * twiddle[0] - im * twiddle[1], im * twiddle[0] + re * twiddle[1]], 0)
        fields.append(dot(z_tile_back[...], turned))
    group = column >> 5
    for side in range(2):
        part = [f[:, 128 * side : 128 * side + 128] for f in fields]
        for n in range(4):
            one = part[0] if n == 0 else pltpu.roll(part[0], 128 - 32 * n, 1)
            two = part[1] if n == 1 else pltpu.roll(part[1], (160 - 32 * n) % 128, 1)
            cells[pl.ds(4 * side + n, 128, stride=8), :] = jnp.where(group == 0, one, two)
    for c in range(8):
        piece = jnp.transpose(cells[128 * c : 128 * c + 128, :])
        for b in range(4):
            for f in range(2):
                out[8 * b + c, 8 * f : 8 * f + 8, :] = piece[32 * f + 8 * b : 32 * f + 8 * b + 8]


def place_kernel(got, potential, residual):
    for h in range(2):
        for f, out in enumerate((potential, residual)):
            out[:, 8 * h : 8 * h + 8, :] = got[16 * h : 16 * h + 16, 8 * f : 8 * f + 8, :]


VMEM = pl.BlockSpec(memory_space=pltpu.VMEM)
SMEM = pl.BlockSpec(memory_space=pltpu.SMEM)


def call(kernel, out_shapes, specs, scratch=(), name=None):
    shapes = [jax.ShapeDtypeStruct(s, jnp.float32) for s in out_shapes]
    single = len(shapes) == 1
    return pl.pallas_call(
        kernel,
        out_shape=shapes[0] if single else shapes,
        in_specs=specs,
        out_specs=VMEM if single else [VMEM] * len(shapes),
        scratch_shapes=list(scratch),
        compiler_params=pltpu.CompilerParams(vmem_limit_bytes=48 * 1024 * 1024),
        name=name,
    )


def exchanged(array, axes):
    return lax.all_to_all(array, axes, 0, 0, tiled=True)


def per_device(density, atom_site, atom_charge, slot_atom, slot_tile, slot_shift):
    t = {name: jnp.asarray(value) for name, value in tables().items()}
    message = call(send_kernel, [(32, 16, 128)], [VMEM, SMEM, SMEM, VMEM, VMEM, VMEM], name="send")(
        density,
        atom_site.reshape(3, 16),
        atom_charge.reshape(1, 16),
        slot_atom.reshape(32, 2).T,
        slot_tile.reshape(32, 2).T,
        jnp.swapaxes(slot_shift.reshape(3, 32, 2), 1, 2),
    )
    got = exchanged(message, ("gy", "gz"))
    message = call(line_kernel, [(256, 128)], [VMEM] * 6, [pltpu.VMEM((1024, 128), jnp.float32)], "line")(
        got, t["shape"], t["order"], t["z_tile"], t["twiddle"], t["z_cell"]
    )
    got = exchanged(message, AXES)
    re, im, message = call(plane_kernel, [(128, 256), (128, 256), (256, 128)], [VMEM] * 5, name="plane")(
        got, t["y"], t["x"], t["column"], t["rows"]
    )
    got = exchanged(message, AXES)
    message = call(cycle_kernel, [(1024, 128)], [VMEM] * 7, name="cycle")(
        got, re, im, t["column"], t["rows"], t["x_back"], t["y_back"]
    )
    got = exchanged(message.reshape(256, 4, 128), AXES).reshape(1024, 128)
    message = call(back_kernel, [(32, 16, 128)], [VMEM] * 4, [pltpu.VMEM((1024, 128), jnp.float32)], "back")(
        got, t["z_tile_back"], t["twiddle"], t["z_cell_back"]
    )
    got = exchanged(message, ("gy", "gz"))
    potential, residual = call(place_kernel, [(16, 16, 128)] * 2, [VMEM], name="place")(got)
    return potential, residual


def solution(mesh):
    return jax.shard_map(
        per_device,
        mesh=mesh,
        in_specs=(
            P("gx", "gy", "gz"),
            P(None, "gx", "gy", "gz", None),
            P("gx", "gy", "gz", None),
            P("gx", "gy", "gz", None, None),
            P("gx", "gy", "gz", None, None),
            P(None, "gx", "gy", "gz", None, None),
        ),
        out_specs=(P("gx", "gy", "gz"), P("gx", "gy", "gz")),
        check_vma=False,
    )
```

```python
import functools

import jax
import jax.numpy as jnp
import numpy as np
from jax import lax
from jax.experimental import pallas as pl
from jax.experimental.pallas import tpu as pltpu
from jax.sharding import PartitionSpec as P


METRIC = np.array([[3.24, 0.972, 0.648], [0.972, 3.2157, 0.9639], [0.648, 0.9639, 2.9565]])
INVERSE = np.array(
    [
        [0.3450043297, -0.0904572938, -0.0461258313],
        [-0.0904572938, 0.3683733435, -0.1002735462],
        [-0.0461258313, -0.1002735462, 0.3810394757],
    ]
)
FIRST_WEIGHTS = np.array([6.0 / 7.0, -15.0 / 56.0, 5.0 / 63.0, -1.0 / 56.0, 2.0 / 385.0, -1.0 / 5544.0])
SECOND_WEIGHTS = 2.0 * FIRST_WEIGHTS / np.arange(1, 7)
CENTER_WEIGHT = -2.0 * SECOND_WEIGHTS.sum()
JACOBI_SCALE = float(-CENTER_WEIGHT * np.trace(INVERSE))
STEP = 0.3
WIDTH_SQUARED = 9.0
RIDGE_SHARE = 0.01
NX, NY, NZ = 128, 64, 1024
AXES = ("gx", "gy", "gz")
HI = lax.Precision.HIGHEST
LOG2E = float(np.log2(np.e))
MOMENTS = [(2, 0), (2, 1), (2, 2), (1, 2), (1, 3), (1, 8), (1, 9), (2, 6), (2, 7), (2, 8)]
MOMENTS += [(3, 4), (3, 5), (3, 6), (3, 7), (4, 2), (4, 3), (4, 4), (4, 5), (4, 6)]


def cos_sin(n, rows, columns):
    angle = 2.0 * np.pi * (np.outer(rows, columns) % n) / n
    return np.cos(angle), np.sin(angle)


def first_symbol(n):
    angle = 2.0 * np.pi * np.arange(n) / n
    return 2.0 * sum(w * np.sin((o + 1) * angle) for o, w in enumerate(FIRST_WEIGHTS))


def second_symbol(n):
    angle = 2.0 * np.pi * np.arange(n) / n
    return CENTER_WEIGHT + 2.0 * sum(w * np.cos((o + 1) * angle) for o, w in enumerate(SECOND_WEIGHTS))


@functools.lru_cache(maxsize=None)
def tables():
    eye = np.eye(32)
    freq = np.arange(128)
    c, s = cos_sin(128, freq, freq)
    t = {}
    t["z_tile"] = np.concatenate([c, -s], 0) / 32.0 / JACOBI_SCALE
    t["z_tile_back"] = np.concatenate([c, -s], 1) / 32.0
    t["twiddle"] = np.stack(cos_sin(1024, freq, np.arange(256) // 32))
    c, s = cos_sin(8, np.arange(8), np.arange(4))
    ahead = np.zeros((2, 8, 32, 384))
    into = ahead[..., :256].reshape(2, 8, 32, 4, 2, 32)
    back = np.zeros((384, 2, 8, 32))
    out = back[:256].reshape(4, 2, 32, 2, 8, 32)
    for k in range(8):
        for h in range(4):
            into[0, k, :, h, 0, :] = c[k, h] * eye
            into[1, k, :, h, 0, :] = s[k, h] * eye
            into[0, k, :, h, 1, :] = -s[k, h] * eye
            into[1, k, :, h, 1, :] = c[k, h] * eye
            out[h, 0, :, 0, k, :] = 2.0 * c[k, h] * eye
            out[h, 1, :, 0, k, :] = -2.0 * s[k, h] * eye
            out[h, 0, :, 1, k, :] = 2.0 * s[k, h] * eye
            out[h, 1, :, 1, k, :] = 2.0 * c[k, h] * eye
        ahead[0, k, :, 256:288] = (-1.0) ** k * eye
        back[256:288, 0, k, :] = (-1.0) ** k * eye
    t["z_cell"] = ahead.reshape(512, 384)
    t["z_cell_back"] = back.reshape(384, 512)
    half, b, j = np.meshgrid(np.arange(2), np.arange(4), np.arange(8), indexing="ij")
    c, s = cos_sin(64, (16 * b + 8 * half + j).reshape(-1), np.arange(64))
    c, s = c.reshape(2, 4, 8, 64) / 8.0, s.reshape(2, 4, 8, 64) / 8.0
    ahead = np.zeros((2, 2, 2, 4, 8, 2, 4, 64))
    for f in range(2):
        ahead[:, f, 0, :, :, 0, f], ahead[:, f, 1, :, :, 0, f] = c, s
        ahead[:, f, 0, :, :, 1, f], ahead[:, f, 1, :, :, 1, f] = -s, c
    ahead[:, 0, 1, :, :, 0, 2], ahead[:, 0, 1, :, :, 1, 2] = c, -s
    t["y"] = ahead.reshape(256, 512)
    c, s = cos_sin(64, np.arange(64), np.arange(64))
    c, s = c.reshape(64, 4, 16) / 8.0, s.reshape(64, 4, 16) / 8.0
    back = np.zeros((2, 2, 2, 64, 4, 2, 2, 2, 16))
    for odd in range(2):
        for f in range(2):
            back[odd, 0, f, :, :, f, 0, odd], back[odd, 1, f, :, :, f, 0, odd] = c, -s
            back[odd, 0, f, :, :, f, 1, odd], back[odd, 1, f, :, :, f, 1, odd] = s, c
    t["y_back"] = back.reshape(512, 512)
    c, s = cos_sin(128, freq, freq)
    t["x"] = np.block([[c, s], [-s, c]]) / np.sqrt(128.0)
    back = np.block([[c, -s], [s, c]]) / np.sqrt(128.0)
    t["x_back"] = back.reshape(2, 64, 2, 256).transpose(2, 0, 1, 3).reshape(256, 256)
    d1x, d1y, d1z = first_symbol(NX), first_symbol(NY), first_symbol(NZ)
    d2x, d2y, d2z = second_symbol(NX), second_symbol(NY), second_symbol(NZ)
    column = np.zeros((128, 128))
    column[:, 0], column[:, 1] = -INVERSE[0, 0] * d2x / JACOBI_SCALE, d1x
    rows = np.zeros((256, 512))
    for d in range(256):
        low = d % 128 + 256 * (d // 128)
        for f, kz in enumerate((low, low + 128, 512)):
            rows[d, 64 * f : 64 * f + 64] = (
                -(INVERSE[1, 1] * d2y + INVERSE[2, 2] * d2z[kz]) + 2.0 * INVERSE[1, 2] * d1y * d1z[kz]
            ) / JACOBI_SCALE
            rows[d, 256 + 64 * f : 320 + 64 * f] = (
                2.0 * (INVERSE[0, 1] * d1y + INVERSE[0, 2] * d1z[kz]) / JACOBI_SCALE
            )
    t["column"], t["rows"] = column, rows
    t["order"] = np.eye(256).reshape(4, 8, 8, 256).transpose(1, 0, 2, 3).reshape(256, 256).T
    k, j = np.repeat(np.arange(8), 8) - 3.5, np.tile(np.arange(8), 8) - 3.5
    shape = np.zeros((64, 128))
    shape[:, 0], shape[:, 1], shape[:, 2] = 1.0, j, k
    shape[:, 3] = -(METRIC[1, 1] * j * j + METRIC[2, 2] * k * k + 2.0 * METRIC[1, 2] * j * k)
    shape[:, 3] *= LOG2E / WIDTH_SQUARED
    t["shape"] = shape
    return {name: value.astype(np.float32) for name, value in t.items()}


def dot(a, b, contract=((1,), (0,))):
    return lax.dot_general(a, b, (contract, ((), ())), precision=HI, preferred_element_type=jnp.float32)


def index_of(shape, dim):
    return lax.broadcasted_iota(jnp.int32, shape, dim)


def solve(gram):
    ff, fc, cc, fs, cs = gram
    ridge = RIDGE_SHARE * 0.5 * (ff + cc)
    ff, cc = ff + ridge, cc + ridge
    determinant = ff * cc - fc * fc
    return (cc * fs - fc * cs) / determinant, (ff * cs - fc * fs) / determinant


def stack_rows(rows, count):
    at = index_of((count, 128), 0)
    stacked = jnp.zeros((count, 128), jnp.float32)
    for n, row in enumerate(rows):
        stacked = jnp.where(at == n, row, stacked)
    return stacked


def sums_on_lanes(arrays):
    rows = []
    for array in arrays:
        row = jnp.sum(array, axis=0, keepdims=True)
        rows.append(row[:, :128] + row[:, 128:])
    count = -(-len(rows) // 8) * 8
    totals = jnp.sum(stack_rows(rows, count), axis=1, keepdims=True)
    mine = index_of((count, 128), 0) == index_of((count, 128), 1)
    return jnp.sum(jnp.where(mine, totals, 0.0), axis=0, keepdims=True)


def picked(row, count):
    lane = index_of((1, 128), 1)
    return [jnp.sum(jnp.where(lane == n, row, 0.0), axis=1, keepdims=True) for n in range(count)]


def send_kernel(density, *refs):
    held, out, slots, done = refs[:5], refs[5], refs[6:11], refs[11]
    copies = [pltpu.make_async_copy(a, b, done.at[n]) for n, (a, b) in enumerate(zip(held, slots))]
    for half in range(2):
        into = out.at[16 * half : 16 * half + 16, 0:8, :]
        copies.append(pltpu.make_async_copy(density.at[:, 8 * half : 8 * half + 8, :], into, done.at[5 + half]))
    for copy in copies:
        copy.start()
    for copy in copies[:5]:
        copy.wait()
    site, charge, atom, tile, shift = slots
    values = [jnp.zeros((2, 32), jnp.float32) for _ in range(4)]
    for n in range(16):
        hit = atom[...] == n
        for p in range(3):
            values[p] = jnp.where(hit, site[p, 0, n], values[p])
        values[3] = jnp.where(hit, charge[0, n], values[3])
    for p in range(3):
        values[p] = values[p] + 4.0 * shift[p].astype(jnp.float32)
    code = tile[...]
    values.append(((code & 15) + 16 * (index_of((2, 32), 1) & 7)).astype(jnp.float32))
    values.append((code >> 4).astype(jnp.float32))
    lane = index_of((8, 128), 1)
    packed = jnp.zeros((8, 128), jnp.float32)
    for e in range(2):
        rows = [jnp.concatenate([v[e : e + 1], jnp.zeros((1, 96), jnp.float32)], 1) for v in values]
        rows = stack_rows(rows, 8)
        for b in range(4):
            moved = pltpu.roll(rows, 8 * b + 8 * e, 1)
            packed = jnp.where((lane >> 3) == 2 * b + e, moved, packed)
    out[:, 8:16, :] = jnp.broadcast_to(packed[None], (32, 8, 128))
    for copy in copies[5:]:
        copy.wait()


def line_kernel(got, shape, order, z_tile, twiddle, z_cell, out, cells):
    rank = lax.axis_index("gy") * 8 + lax.axis_index("gz")
    x, half = rank & 15, rank >> 4
    own = ((x >> 3) * 2 + half).astype(jnp.float32)
    along = (x & 7).astype(jnp.float32)
    lane = index_of((8, 128), 1)
    sub = index_of((8, 512), 0)
    tile_at = index_of((128, 512), 0).astype(jnp.float32)
    scale = -LOG2E / WIDTH_SQUARED
    charge = []
    for b in range(4):
        parts = []
        for g in range(4):
            part = jnp.zeros((8, 128), jnp.float32)
            for r in range(8):
                moved = got[8 * g + r, 8:16, :]
                if r != b:
                    moved = pltpu.roll(moved, (16 * (r - b)) % 128, 1)
                part = jnp.where((lane >> 4) == r, moved, part)
            parts.append(part)
        slots = jnp.concatenate(parts, 1)
        ex = along - slots[0:1]
        vy, vz = slots[1:2] - 3.5, slots[2:3] - 3.5
        m = METRIC
        fixed = m[0, 0] * ex * ex + m[1, 1] * vy * vy + m[2, 2] * vz * vz
        fixed = fixed - 2.0 * m[0, 1] * ex * vy - 2.0 * m[0, 2] * ex * vz + 2.0 * m[1, 2] * vy * vz
        by_j = -2.0 * m[1, 1] * vy + 2.0 * m[0, 1] * ex - 2.0 * m[1, 2] * vz
        by_k = -2.0 * m[2, 2] * vz + 2.0 * m[0, 2] * ex - 2.0 * m[1, 2] * vy
        form = jnp.where(sub == 0, fixed, jnp.where(sub == 1, by_j, jnp.where(sub == 2, by_k, 0.0)))
        blocks = jnp.exp2(dot(shape[:, 0:8] * jnp.where(lane[0:1, 0:8] < 3, 1.0, 0.0), scale * form) + shape[:, 3:4])
        peak = jnp.where(slots[5:6] == own, slots[3:4], 0.0)
        placed = jnp.where(slots[4:5] == tile_at, peak, 0.0)
        charge.append(dot(placed, blocks, ((1,), (1,))))
    charge = dot(jnp.concatenate(charge, 1), order[...])
    for c in range(8):
        piece = jnp.concatenate([got[8 * b + c, 0:8, :] for b in range(4)], 0)
        cells[128 * c : 128 * c + 128, :] = jnp.transpose(jnp.concatenate([piece] * 4, 0))
    group = index_of((128, 128), 1) >> 5
    sides = []
    for side in range(2):
        total = jnp.zeros((128, 128), jnp.float32)
        for n in range(4):
            total = jnp.where(group == n, cells[pl.ds(4 * side + n, 128, stride=8), :], total)
        sides.append(total)
    field = jnp.concatenate(sides, 1) + charge
    spectrum = dot(z_tile[...], field)
    re, im = spectrum[:128], spectrum[128:]
    turned = jnp.concatenate([re * twiddle[0] + im * twiddle[1], im * twiddle[0] - re * twiddle[1]], 1)
    result = dot(turned, z_cell[...])
    last = pltpu.roll(result[:, 256:384], 32, 1)
    row, column = index_of((128, 128), 0), index_of((128, 128), 1)
    here = (row == 0) & ((column >> 5) == 1)
    out[0:128, :] = jnp.where(here, last, result[:, 0:128])
    out[128:256, :] = result[:, 128:256]


def eigenvalues(column, rows):
    rank = (lax.axis_index("gx") * 4 + lax.axis_index("gy")) * 8 + lax.axis_index("gz")
    mine = rows[pl.ds(rank, 1), :]
    return column[:, 0:1] + mine[:, 0:256] + column[:, 1:2] * mine[:, 256:512], rank


def weights_of(rank):
    field = index_of((1, 256), 1) >> 6
    first = jnp.where(field == 1, 2.0, jnp.where(field == 3, 0.0, 1.0))
    other = jnp.where(field < 2, 2.0, 0.0)
    return jnp.where(rank == 0, first, other)


def plane_kernel(got, y, x, column, rows, out_re, out_im, out):
    lam, rank = eigenvalues(column, rows)
    first = jnp.where(rank == 0, 1.0, 0.0).astype(jnp.float32)
    halves = [jnp.concatenate([got[32 * a + 16 * h : 32 * a + 16 * h + 16, :] for a in range(8)], 0) for h in range(2)]
    lines = dot(jnp.concatenate(halves, 1), y[...])
    spectrum = dot(x[...], jnp.concatenate([lines[:, :256], lines[:, 256:]], 0))
    re, im = spectrum[:128], spectrum[128:]
    re, im = (
        jnp.concatenate([re[:, :128] + first * im[:, 128:], re[:, 128:]], 1),
        jnp.concatenate([im[:, :128] - first * re[:, 128:], im[:, 128:]], 1),
    )
    out_re[...] = re
    out_im[...] = im
    a = STEP * lam
    mu = 1.0 - a
    power = (re * re + im * im) * weights_of(rank)
    products = {}
    for i in range(1, 5):
        power = power * a
        value = power
        for j in range(10):
            if j > 0:
                value = value * mu
            if (i, j) in MOMENTS:
                products[i, j] = value
            if j == max(n for m, n in MOMENTS if m == i):
                break
    row = sums_on_lanes([products[m] for m in MOMENTS])
    out[...] = jnp.broadcast_to(row, (256, 128))


def cycle_kernel(got, re_in, im_in, column, rows, x_back, y_back, out):
    sums = dict(zip(MOMENTS, picked(jnp.sum(got[...], axis=0, keepdims=True), len(MOMENTS))))
    g0, g1 = solve([sums[2, 0], sums[2, 1], sums[2, 2], -sums[1, 2], -sums[1, 3]])

    def again(i, j):
        return (
            sums[i, j + 6]
            + 2.0 * (g0 * sums[i + 1, j + 4] + g1 * sums[i + 1, j + 5])
            + g0 * g0 * sums[i + 2, j + 2]
            + 2.0 * g0 * g1 * sums[i + 2, j + 3]
            + g1 * g1 * sums[i + 2, j + 4]
        )

    h0, h1 = solve([again(2, 0), again(2, 1), again(2, 2), -again(1, 2), -again(1, 3)])
    lam, rank = eigenvalues(column, rows)
    first = jnp.where(rank == 0, 1.0, 0.0).astype(jnp.float32)
    re, im = re_in[...], im_in[...]
    a = STEP * lam
    mu = 1.0 - a
    mu2 = mu * mu
    after3 = mu * (mu2 + a * (g0 + mu * g1))
    after6 = after3 * mu * (mu2 + a * (h0 + mu * h1))
    after7 = after6 * mu
    after8 = after7 * mu
    steps = 1.0 + (1.0 - g0) * mu + (1.0 - g1) * mu2
    steps = steps + after3 * (1.0 + (1.0 - h0) * mu + (1.0 - h1) * mu2)
    steps = STEP * (steps + after6 + after7)
    power = (re * re + im * im) * weights_of(rank) * after6 * after6 * a
    low = power * mu2
    power = power * a
    row = sums_on_lanes([power, power * mu, power * mu2, low, low * mu])
    out[pl.ds(3, 256, stride=4), :] = jnp.broadcast_to(row, (256, 128))
    columns = []
    for multiplier in (steps, after7, after8):
        fr, fi = multiplier * re, multiplier * im
        columns.append(
            jnp.concatenate([fr[:, :128] - first * fi[:, 128:], fi[:, :128] + first * fr[:, 128:]], 0)
        )
    planes = dot(x_back[...], jnp.concatenate(columns, 1))
    lines = [
        jnp.concatenate([planes[64 * n : 64 * n + 64, 128 * f : 128 * f + 128] for n in range(4)], 1) for f in range(3)
    ]
    lines = dot(jnp.concatenate(lines, 0), y_back[...])
    for f in range(3):
        for n in range(8):
            for b in range(4):
                out[pl.ds((32 * n + 8 * b) * 4 + f, 8, stride=4), :] = lines[
                    64 * f + 8 * n : 64 * f + 8 * n + 8, 128 * b : 128 * b + 128
                ]


def back_kernel(got, z_tile_back, twiddle, z_cell_back, out, cells):
    row = jnp.sum(got[pl.ds(3, 256, stride=4), :], axis=0, keepdims=True)
    s = picked(row, 5)
    g0, g1 = solve([s[0], s[1], s[2], -s[3], -s[4]])
    p8, s7, s8 = [got[pl.ds(f, 256, stride=4), :] for f in range(3)]
    at, column = index_of((128, 128), 0), index_of((128, 128), 1)
    spectra = [p8 + STEP * (1.0 - g1) * s8 - STEP * g0 * s7, JACOBI_SCALE * s8]
    fields = []
    for v in spectra:
        low, high = v[:128], v[128:]
        top = at == 0
        last = jnp.where(top & (column < 32), pltpu.roll(low, 96, 1), 0.0)
        low = jnp.where(top & (column < 64), jnp.where(column < 32, 0.5 * low, 0.0), low)
        result = dot(jnp.concatenate([low, high, last], 1), z_cell_back[...])
        re, im = result[:, :256], result[:, 256:]
        turned = jnp.concatenate([re * twiddle[0] - im * twiddle[1], im * twiddle[0] + re * twiddle[1]], 0)
        fields.append(dot(z_tile_back[...], turned))
    group = column >> 5
    for side in range(2):
        part = [f[:, 128 * side : 128 * side + 128] for f in fields]
        for n in range(4):
            one = part[0] if n == 0 else pltpu.roll(part[0], 128 - 32 * n, 1)
            two = part[1] if n == 1 else pltpu.roll(part[1], (160 - 32 * n) % 128, 1)
            cells[pl.ds(4 * side + n, 128, stride=8), :] = jnp.where(group == 0, one, two)
    for c in range(8):
        piece = jnp.transpose(cells[128 * c : 128 * c + 128, :])
        out[c] = piece[0:64]


def place_kernel(got, potential, residual, done):
    copies = [
        pltpu.make_async_copy(got.at[:, f], out, done.at[f]) for f, out in enumerate((potential, residual))
    ]
    for copy in copies:
        copy.start()
    for copy in copies:
        copy.wait()


VMEM = pl.BlockSpec(memory_space=pltpu.VMEM)
HBM = pl.BlockSpec(memory_space=pltpu.HBM)


def call(kernel, out_shapes, specs, scratch=(), name=None, result=VMEM, limit=16):
    shapes = [jax.ShapeDtypeStruct(s, jnp.float32) for s in out_shapes]
    single = len(shapes) == 1
    return pl.pallas_call(
        kernel,
        out_shape=shapes[0] if single else shapes,
        in_specs=specs,
        out_specs=result if single else [result] * len(shapes),
        scratch_shapes=list(scratch),
        compiler_params=pltpu.CompilerParams(vmem_limit_bytes=limit * 1024 * 1024),
        name=name,
    )


def exchanged(array, axes):
    return lax.all_to_all(array, axes, 0, 0, tiled=True)


def per_device(density, atom_site, atom_charge, slot_atom, slot_tile, slot_shift):
    t = {name: jnp.asarray(value) for name, value in tables().items()}
    scratch = [
        pltpu.SMEM((3, 1, 16), jnp.float32),
        pltpu.SMEM((1, 16), jnp.float32),
        pltpu.VMEM((2, 32), jnp.int32),
        pltpu.VMEM((2, 32), jnp.int32),
        pltpu.VMEM((3, 2, 32), jnp.int32),
        pltpu.SemaphoreType.DMA((7,)),
    ]
    message = call(send_kernel, [(32, 16, 128)], [HBM] * 6, scratch, name="send", limit=63)(
        density,
        atom_site.reshape(3, 1, 16),
        atom_charge.reshape(1, 16),
        slot_atom.reshape(32, 2).T,
        slot_tile.reshape(32, 2).T,
        jnp.swapaxes(slot_shift.reshape(3, 32, 2), 1, 2),
    )
    got = exchanged(message, ("gy", "gz"))
    message = call(line_kernel, [(256, 128)], [VMEM] * 6, [pltpu.VMEM((1024, 128), jnp.float32)], "line")(
        got, t["shape"], t["order"], t["z_tile"], t["twiddle"], t["z_cell"]
    )
    got = exchanged(message, AXES)
    re, im, message = call(plane_kernel, [(128, 256), (128, 256), (256, 128)], [VMEM] * 5, name="plane")(
        got, t["y"], t["x"], t["column"], t["rows"]
    )
    got = exchanged(message, AXES)
    message = call(cycle_kernel, [(1024, 128)], [VMEM] * 7, name="cycle")(
        got, re, im, t["column"], t["rows"], t["x_back"], t["y_back"]
    )
    got = exchanged(message.reshape(256, 4, 128), AXES).reshape(1024, 128)
    message = call(back_kernel, [(8, 64, 128)], [VMEM] * 4, [pltpu.VMEM((1024, 128), jnp.float32)], "back")(
        got, t["z_tile_back"], t["twiddle"], t["z_cell_back"]
    )
    got = exchanged(message, "gz").reshape(8, 2, 2, 16, 128)
    place = call(place_kernel, [(8, 2, 16, 128)] * 2, [VMEM], [pltpu.SemaphoreType.DMA((2,))], "place", HBM, 63)
    return tuple(out.reshape(16, 16, 128) for out in place(got))


def solution(mesh):
    return jax.shard_map(
        per_device,
        mesh=mesh,
        in_specs=(
            P("gx", "gy", "gz"),
            P(None, "gx", "gy", "gz", None),
            P("gx", "gy", "gz", None),
            P("gx", "gy", "gz", None, None),
            P("gx", "gy", "gz", None, None),
            P(None, "gx", "gy", "gz", None, None),
        ),
        out_specs=(P("gx", "gy", "gz"), P("gx", "gy", "gz")),
        check_vma=False,
    )
```

```python
import functools

import jax
import jax.numpy as jnp
import numpy as np
from jax import lax
from jax.experimental import pallas as pl
from jax.experimental.pallas import tpu as pltpu
from jax.sharding import PartitionSpec as P


METRIC = np.array([[3.24, 0.972, 0.648], [0.972, 3.2157, 0.9639], [0.648, 0.9639, 2.9565]])
INVERSE = np.array(
    [
        [0.3450043297, -0.0904572938, -0.0461258313],
        [-0.0904572938, 0.3683733435, -0.1002735462],
        [-0.0461258313, -0.1002735462, 0.3810394757],
    ]
)
FIRST_WEIGHTS = np.array([6.0 / 7.0, -15.0 / 56.0, 5.0 / 63.0, -1.0 / 56.0, 2.0 / 385.0, -1.0 / 5544.0])
SECOND_WEIGHTS = 2.0 * FIRST_WEIGHTS / np.arange(1, 7)
CENTER_WEIGHT = -2.0 * SECOND_WEIGHTS.sum()
JACOBI_SCALE = float(-CENTER_WEIGHT * np.trace(INVERSE))
STEP = 0.3
WIDTH_SQUARED = 9.0
RIDGE_SHARE = 0.01
NX, NY, NZ = 128, 64, 1024
AXES = ("gx", "gy", "gz")
HI = lax.Precision.HIGHEST
LOG2E = float(np.log2(np.e))
NODES = 16
LARGEST = STEP * 2.3721


def cos_sin(n, rows, columns):
    angle = 2.0 * np.pi * (np.outer(rows, columns) % n) / n
    return np.cos(angle), np.sin(angle)


def first_symbol(n):
    angle = 2.0 * np.pi * np.arange(n) / n
    return 2.0 * sum(w * np.sin((o + 1) * angle) for o, w in enumerate(FIRST_WEIGHTS))


def second_symbol(n):
    angle = 2.0 * np.pi * np.arange(n) / n
    return CENTER_WEIGHT + 2.0 * sum(w * np.cos((o + 1) * angle) for o, w in enumerate(SECOND_WEIGHTS))


@functools.lru_cache(maxsize=None)
def tables():
    eye = np.eye(32)
    freq = np.arange(128)
    c, s = cos_sin(128, freq, freq)
    t = {}
    t["z_tile"] = np.concatenate([c, -s], 0) / 32.0 / JACOBI_SCALE
    t["z_tile_back"] = np.concatenate([c, -s], 1) / 32.0
    t["twiddle"] = np.stack(cos_sin(1024, freq, np.arange(256) // 32))
    c, s = cos_sin(8, np.arange(4), np.arange(4))
    half_eye = np.eye(16)
    for odd, name in enumerate(("z_even", "z_odd")):
        ahead = np.zeros((2, 4, 32, 2, 2, 32))
        back = np.zeros((2, 2, 2, 16, 2, 4, 2, 16))
        for k in range(4):
            for n in range(2):
                cc, ss = c[k, 2 * n + odd], s[k, 2 * n + odd]
                ahead[0, k, :, n, 0], ahead[1, k, :, n, 0] = cc * eye, ss * eye
                ahead[0, k, :, n, 1], ahead[1, k, :, n, 1] = -ss * eye, cc * eye
                for x in range(2):
                    back[x, n, 0, :, 0, k, x], back[x, n, 1, :, 0, k, x] = 2.0 * cc * half_eye, -2.0 * ss * half_eye
                    back[x, n, 0, :, 1, k, x], back[x, n, 1, :, 1, k, x] = 2.0 * ss * half_eye, 2.0 * cc * half_eye
        t[name], t[name + "_back"] = ahead.reshape(256, 128), back.reshape(128, 256)
    last = np.zeros((2, 2, 2, 16, 4, 2, 16))
    for k in range(4):
        for x in range(2):
            last[x, 0, 1, :, k, x] = (-1.0) ** k * half_eye
    t["z_last_back"] = last.reshape(128, 128)
    half, b, j = np.meshgrid(np.arange(2), np.arange(4), np.arange(8), indexing="ij")
    c, s = cos_sin(64, (16 * b + 8 * half + j).reshape(-1), np.arange(64))
    c, s = c.reshape(2, 4, 8, 64) / 8.0, s.reshape(2, 4, 8, 64) / 8.0
    ahead = np.zeros((2, 2, 2, 4, 8, 2, 4, 64))
    for f in range(2):
        ahead[:, f, 0, :, :, 0, f], ahead[:, f, 1, :, :, 0, f] = c, s
        ahead[:, f, 0, :, :, 1, f], ahead[:, f, 1, :, :, 1, f] = -s, c
    ahead[:, 0, 1, :, :, 0, 2], ahead[:, 0, 1, :, :, 1, 2] = c, -s
    t["y"] = ahead.reshape(256, 512)
    c, s = cos_sin(64, np.arange(64), np.arange(64))
    c, s = c.reshape(64, 4, 16) / 8.0, s.reshape(64, 4, 16) / 8.0
    back = np.zeros((2, 2, 64, 4, 2, 2, 16))
    for f in range(2):
        back[0, f, :, :, f, 0], back[1, f, :, :, f, 0] = c, -s
        back[0, f, :, :, f, 1], back[1, f, :, :, f, 1] = s, c
    t["y_back"] = back.reshape(256, 256)
    c, s = cos_sin(128, freq, freq)
    t["x"] = np.block([[c, s], [-s, c]]) / np.sqrt(128.0)
    back = np.block([[c, -s], [s, c]]) / np.sqrt(128.0)
    t["x_back"] = back.reshape(2, 64, 2, 256).transpose(2, 0, 1, 3).reshape(256, 256)
    d1x, d1y, d1z = first_symbol(NX), first_symbol(NY), first_symbol(NZ)
    d2x, d2y, d2z = second_symbol(NX), second_symbol(NY), second_symbol(NZ)
    column = np.zeros((128, 128))
    column[:, 0], column[:, 1] = -INVERSE[0, 0] * d2x / JACOBI_SCALE, d1x
    rows = np.zeros((256, 512))
    for d in range(256):
        low = d % 128 + 128 * (d // 128)
        for f, kz in enumerate((low, low + 256, 512)):
            rows[d, 64 * f : 64 * f + 64] = (
                -(INVERSE[1, 1] * d2y + INVERSE[2, 2] * d2z[kz]) + 2.0 * INVERSE[1, 2] * d1y * d1z[kz]
            ) / JACOBI_SCALE
            rows[d, 256 + 64 * f : 320 + 64 * f] = (
                2.0 * (INVERSE[0, 1] * d1y + INVERSE[0, 2] * d1z[kz]) / JACOBI_SCALE
            )
    t["column"], t["rows"] = column, rows
    angle = (np.arange(NODES) + 0.5) * np.pi / NODES
    nodes = np.zeros((136, 128))
    nodes[:NODES, :NODES] = 2.0 / NODES * np.cos(np.outer(np.arange(NODES), angle))
    nodes[0, :NODES] = 1.0 / NODES
    nodes[128, :NODES] = 0.5 * LARGEST * (1.0 + np.cos(angle))
    t["nodes"] = nodes
    t["order"] = np.eye(256).reshape(4, 8, 8, 256).transpose(1, 0, 2, 3).reshape(256, 256).T
    k, j = np.repeat(np.arange(8), 8) - 3.5, np.tile(np.arange(8), 8) - 3.5
    shape = np.zeros((64, 128))
    shape[:, 0], shape[:, 1], shape[:, 2] = 1.0, j, k
    shape[:, 3] = -(METRIC[1, 1] * j * j + METRIC[2, 2] * k * k + 2.0 * METRIC[1, 2] * j * k)
    shape[:, 3] *= LOG2E / WIDTH_SQUARED
    t["shape"] = shape
    return {name: value.astype(np.float32) for name, value in t.items()}


def dot(a, b, contract=((1,), (0,))):
    return lax.dot_general(a, b, (contract, ((), ())), precision=HI, preferred_element_type=jnp.float32)


def index_of(shape, dim):
    return lax.broadcasted_iota(jnp.int32, shape, dim)


def solve(gram):
    ff, fc, cc, fs, cs = gram
    ridge = RIDGE_SHARE * 0.5 * (ff + cc)
    ff, cc = ff + ridge, cc + ridge
    determinant = ff * cc - fc * fc
    return (cc * fs - fc * cs) / determinant, (ff * cs - fc * fs) / determinant


def stack_rows(rows, count):
    at = index_of((count, 128), 0)
    stacked = jnp.zeros((count, 128), jnp.float32)
    for n, row in enumerate(rows):
        stacked = jnp.where(at == n, row, stacked)
    return stacked


def sums_on_lanes(arrays):
    rows = []
    for array in arrays:
        row = jnp.sum(array, axis=0, keepdims=True)
        rows.append(row[:, :128] + row[:, 128:])
    count = -(-len(rows) // 8) * 8
    totals = jnp.sum(stack_rows(rows, count), axis=1, keepdims=True)
    mine = index_of((count, 128), 0) == index_of((count, 128), 1)
    return jnp.sum(jnp.where(mine, totals, 0.0), axis=0, keepdims=True)


def in_three(array):
    high = array.astype(jnp.bfloat16)
    rest = array - high.astype(jnp.float32)
    middle = rest.astype(jnp.bfloat16)
    return high, middle, (rest - middle.astype(jnp.float32)).astype(jnp.bfloat16)


def exact_dot(a, b, contract):
    return lax.dot_general(a, b, (contract, ((), ())), preferred_element_type=jnp.float32)


def send_kernel(density, *refs):
    held, out, slots, done = refs[:5], refs[5], refs[6:11], refs[11]
    copies = [pltpu.make_async_copy(a, b, done.at[n]) for n, (a, b) in enumerate(zip(held, slots))]
    for half in range(2):
        into = out.at[16 * half : 16 * half + 16, 0:8, :]
        copies.append(pltpu.make_async_copy(density.at[:, 8 * half : 8 * half + 8, :], into, done.at[5 + half]))
    for copy in copies:
        copy.start()
    for copy in copies[:5]:
        copy.wait()
    site, charge, atom, tile, shift = slots
    values = [jnp.zeros((2, 32), jnp.float32) for _ in range(4)]
    for n in range(16):
        hit = atom[...] == n
        for p in range(3):
            values[p] = jnp.where(hit, site[p, 0, n], values[p])
        values[3] = jnp.where(hit, charge[0, n], values[3])
    for p in range(3):
        values[p] = values[p] + 4.0 * shift[p].astype(jnp.float32)
    code = tile[...]
    values.append(((code & 15) + 16 * (index_of((2, 32), 1) & 7)).astype(jnp.float32))
    values.append((code >> 4).astype(jnp.float32))
    lane = index_of((8, 128), 1)
    packed = jnp.zeros((8, 128), jnp.float32)
    for e in range(2):
        rows = [jnp.concatenate([v[e : e + 1], jnp.zeros((1, 96), jnp.float32)], 1) for v in values]
        rows = stack_rows(rows, 8)
        for b in range(4):
            moved = pltpu.roll(rows, 8 * b + 8 * e, 1)
            packed = jnp.where((lane >> 3) == 2 * b + e, moved, packed)
    out[:, 8:16, :] = jnp.broadcast_to(packed[None], (32, 8, 128))
    for copy in copies[5:]:
        copy.wait()


def line_kernel(got, shape, order, z_tile, twiddle, z_even, z_odd, out, cells):
    rank = lax.axis_index("gy") * 8 + lax.axis_index("gz")
    x, half = rank & 15, rank >> 4
    own = ((x >> 3) * 2 + half).astype(jnp.float32)
    along = (x & 7).astype(jnp.float32)
    lane = index_of((8, 128), 1)
    sub = index_of((8, 512), 0)
    tile_at = index_of((128, 512), 0).astype(jnp.float32)
    scale = -LOG2E / WIDTH_SQUARED
    charge = []
    for b in range(4):
        parts = []
        for g in range(4):
            part = jnp.zeros((8, 128), jnp.float32)
            for r in range(8):
                moved = got[8 * g + r, 8:16, :]
                if r != b:
                    moved = pltpu.roll(moved, (16 * (r - b)) % 128, 1)
                part = jnp.where((lane >> 4) == r, moved, part)
            parts.append(part)
        slots = jnp.concatenate(parts, 1)
        ex = along - slots[0:1]
        vy, vz = slots[1:2] - 3.5, slots[2:3] - 3.5
        m = METRIC
        fixed = m[0, 0] * ex * ex + m[1, 1] * vy * vy + m[2, 2] * vz * vz
        fixed = fixed - 2.0 * m[0, 1] * ex * vy - 2.0 * m[0, 2] * ex * vz + 2.0 * m[1, 2] * vy * vz
        by_j = -2.0 * m[1, 1] * vy + 2.0 * m[0, 1] * ex - 2.0 * m[1, 2] * vz
        by_k = -2.0 * m[2, 2] * vz + 2.0 * m[0, 2] * ex - 2.0 * m[1, 2] * vy
        form = jnp.where(sub == 0, fixed, jnp.where(sub == 1, by_j, jnp.where(sub == 2, by_k, 0.0)))
        blocks = jnp.exp2(dot(shape[:, 0:8] * jnp.where(lane[0:1, 0:8] < 3, 1.0, 0.0), scale * form) + shape[:, 3:4])
        peak = jnp.where(slots[5:6] == own, slots[3:4], 0.0)
        placed = jnp.where(slots[4:5] == tile_at, 1.0, 0.0).astype(jnp.bfloat16)
        parts = jnp.concatenate(in_three(blocks * peak), 0)
        charge.append(exact_dot(placed, parts, ((1,), (1,))))
    charge = [c[:, 0:64] + c[:, 64:128] + c[:, 128:192] for c in charge]
    charge = jnp.concatenate(in_three(jnp.concatenate(charge, 1)), 1)
    charge = exact_dot(charge, jnp.concatenate([order[...]] * 3, 0), ((1,), (0,)))
    for c in range(8):
        piece = jnp.concatenate([got[8 * b + c, 0:8, :] for b in range(4)], 0)
        cells[128 * c : 128 * c + 128, :] = jnp.transpose(jnp.concatenate([piece] * 4, 0))
    group = index_of((128, 128), 1) >> 5
    sides = []
    for side in range(2):
        total = jnp.zeros((128, 128), jnp.float32)
        for n in range(4):
            total = jnp.where(group == n, cells[pl.ds(4 * side + n, 128, stride=8), :], total)
        sides.append(total)
    field = jnp.concatenate(sides, 1) + charge
    spectrum = dot(z_tile[...], field)
    re, im = spectrum[:128], spectrum[128:]
    re, im = re * twiddle[0] + im * twiddle[1], im * twiddle[0] - re * twiddle[1]
    even = jnp.concatenate([re[:, :128] + re[:, 128:], im[:, :128] + im[:, 128:]], 1)
    odd = jnp.concatenate([re[:, :128] - re[:, 128:], im[:, :128] - im[:, 128:]], 1)
    out[0:128, :] = dot(even, z_even[...])
    out[128:256, :] = dot(odd, z_odd[...])
    last = jnp.where((lane >> 5) & 1 == 0, even[0:8, 0:128], -even[0:8, 0:128])
    last = last + pltpu.roll(last, 64, 1)
    last = last + pltpu.roll(last, 32, 1)
    here = (index_of((8, 128), 0) == 0) & ((lane >> 5) == 1)
    out[0:8, :] = jnp.where(here, last, out[0:8, :])


def eigenvalues(column, rows):
    rank = (lax.axis_index("gx") * 4 + lax.axis_index("gy")) * 8 + lax.axis_index("gz")
    mine = rows[pl.ds(rank, 1), :]
    return column[:, 0:1] + mine[:, 0:256] + column[:, 1:2] * mine[:, 256:512], rank


def weights_of(rank):
    field = index_of((1, 256), 1) >> 6
    first = jnp.where(field == 1, 2.0, jnp.where(field == 3, 0.0, 1.0))
    other = jnp.where(field < 2, 2.0, 0.0)
    return jnp.where(rank == 0, first, other)


def plane_kernel(got, y, x, column, rows, out_re, out_im, out):
    lam, rank = eigenvalues(column, rows)
    first = jnp.where(rank == 0, 1.0, 0.0).astype(jnp.float32)
    halves = [jnp.concatenate([got[32 * a + 16 * h : 32 * a + 16 * h + 16, :] for a in range(8)], 0) for h in range(2)]
    lines = dot(jnp.concatenate(halves, 1), y[...])
    spectrum = dot(x[...], jnp.concatenate([lines[:, :256], lines[:, 256:]], 0))
    re, im = spectrum[:128], spectrum[128:]
    re, im = (
        jnp.concatenate([re[:, :128] + first * im[:, 128:], re[:, 128:]], 1),
        jnp.concatenate([im[:, :128] - first * re[:, 128:], im[:, 128:]], 1),
    )
    out_re[...] = re
    out_im[...] = im
    a = STEP * lam
    power = (re * re + im * im) * weights_of(rank) * a
    double = a * (4.0 / LARGEST) - 2.0
    moments = [power, 0.5 * double * power]
    while len(moments) < NODES:
        moments.append(double * moments[-1] - moments[-2])
    out[...] = jnp.broadcast_to(sums_on_lanes(moments), (256, 128))


def cycle_kernel(got, re_in, im_in, column, rows, nodes, x_back, y_back, out):
    moments = jnp.sum(got[...], axis=0, keepdims=True)
    weight = dot(jnp.broadcast_to(moments, (8, 128)), nodes[0:128, :])[0:1]
    node = nodes[128:129, :]
    lam, rank = eigenvalues(column, rows)
    first = jnp.where(rank == 0, 1.0, 0.0).astype(jnp.float32)
    fine = STEP * lam
    sides = [(node, 1.0 - node), (fine, 1.0 - fine)]
    scaled, potential = [1.0, 1.0], 0.0
    for cycle in range(3):
        a, mu = sides[0]
        low = weight * scaled[0] * scaled[0]
        products = [low * a, low * a * mu, low * a * mu * mu, -low * mu * mu, -low * mu * mu * mu]
        g0, g1 = solve([jnp.sum(p, axis=1, keepdims=True) for p in products])
        a, mu = sides[1]
        potential = potential + STEP * scaled[1] * (1.0 + mu * ((1.0 - g0) + (1.0 - g1) * mu))
        if cycle < 2:
            scaled = [s * mu * (mu * mu + a * (g0 + mu * g1)) for s, (a, mu) in zip(scaled, sides)]
    residual = JACOBI_SCALE * scaled[1] * mu * mu
    re, im = re_in[...], im_in[...]
    columns = []
    for multiplier in (potential, residual):
        fr, fi = multiplier * re, multiplier * im
        columns.append(
            jnp.concatenate([fr[:, :128] - first * fi[:, 128:], fi[:, :128] + first * fr[:, 128:]], 0)
        )
    planes = dot(x_back[...], jnp.concatenate(columns, 1))
    lines = []
    for f in range(2):
        for odd in range(2):
            at = 128 * odd
            pair = [planes[at + n : at + n + 64, 128 * f : 128 * f + 128] for n in (0, 64)]
            lines.append(jnp.concatenate(pair, 1))
    lines = dot(jnp.concatenate(lines, 0), y_back[...])
    left = index_of((64, 128), 1) < 64
    for f in range(2):
        for b in range(4):
            side = slice(128 * (b // 2), 128 * (b // 2) + 128)
            even, odd = lines[128 * f : 128 * f + 64, side], lines[128 * f + 64 : 128 * f + 128, side]
            if b % 2 == 0:
                odd = pltpu.roll(odd, 64, 1)
            else:
                even = pltpu.roll(even, 64, 1)
            message = jnp.where(left, even, odd)
            for n in range(8):
                out[pl.ds((32 * n + 8 * b) * 2 + f, 8, stride=2), :] = message[8 * n : 8 * n + 8]


def back_kernel(got, z_tile_back, twiddle, z_even_back, z_odd_back, z_last_back, out, cells):
    spectra = [got[pl.ds(f, 256, stride=2), :] for f in range(2)]
    low = jnp.concatenate([v[:128] for v in spectra], 0)
    high = jnp.concatenate([v[128:] for v in spectra], 0)
    top = index_of((256, 128), 0) & 127 == 0
    part = (index_of((256, 128), 1) & 63) >> 4
    last = jnp.where(top & (part == 1), low, 0.0)
    low = jnp.where(top & (part < 2), jnp.where(part == 0, 0.5 * low, 0.0), low)
    last = dot(jnp.concatenate([last[0:8], last[128:136]], 0), z_last_back[...])
    even, odd = dot(low, z_even_back[...]), dot(high, z_odd_back[...])
    turned = []
    for f in range(2):
        e, o = even[128 * f : 128 * f + 128], odd[128 * f : 128 * f + 128]
        real = jnp.concatenate([e[0:8, :128] + last[8 * f : 8 * f + 8], e[8:, :128]], 0)
        re = jnp.concatenate([real + o[:, :128], real - o[:, :128]], 1)
        im = jnp.concatenate([e[:, 128:] + o[:, 128:], e[:, 128:] - o[:, 128:]], 1)
        turned.append(
            jnp.concatenate([re * twiddle[0] - im * twiddle[1], im * twiddle[0] + re * twiddle[1]], 0)
        )
    fields = dot(z_tile_back[...], jnp.concatenate(turned, 1))
    group = index_of((128, 128), 1) >> 5
    for side in range(2):
        one = fields[:, 128 * side : 128 * side + 128]
        two = fields[:, 256 + 128 * side : 384 + 128 * side]
        for n in range(4):
            lower = one if n == 0 else pltpu.roll(one, 128 - 32 * n, 1)
            upper = two if n == 1 else pltpu.roll(two, (160 - 32 * n) % 128, 1)
            cells[pl.ds(4 * side + n, 128, stride=8), :] = jnp.where(group == 0, lower, upper)
    for c in range(8):
        out[c] = jnp.transpose(cells[128 * c : 128 * c + 128, :])[0:64]


def place_kernel(got, potential, residual, done):
    copies = [
        pltpu.make_async_copy(got.at[:, f], out, done.at[f]) for f, out in enumerate((potential, residual))
    ]
    for copy in copies:
        copy.start()
    for copy in copies:
        copy.wait()


VMEM = pl.BlockSpec(memory_space=pltpu.VMEM)
HBM = pl.BlockSpec(memory_space=pltpu.HBM)


def call(kernel, out_shapes, specs, scratch=(), name=None, result=VMEM, limit=16):
    shapes = [jax.ShapeDtypeStruct(s, jnp.float32) for s in out_shapes]
    single = len(shapes) == 1
    return pl.pallas_call(
        kernel,
        out_shape=shapes[0] if single else shapes,
        in_specs=specs,
        out_specs=result if single else [result] * len(shapes),
        scratch_shapes=list(scratch),
        compiler_params=pltpu.CompilerParams(vmem_limit_bytes=limit * 1024 * 1024),
        name=name,
    )


def exchanged(array, axes):
    return lax.all_to_all(array, axes, 0, 0, tiled=True)


def per_device(density, atom_site, atom_charge, slot_atom, slot_tile, slot_shift):
    t = {name: jnp.asarray(value) for name, value in tables().items()}
    scratch = [
        pltpu.SMEM((3, 1, 16), jnp.float32),
        pltpu.SMEM((1, 16), jnp.float32),
        pltpu.VMEM((2, 32), jnp.int32),
        pltpu.VMEM((2, 32), jnp.int32),
        pltpu.VMEM((3, 2, 32), jnp.int32),
        pltpu.SemaphoreType.DMA((7,)),
    ]
    message = call(send_kernel, [(32, 16, 128)], [HBM] * 6, scratch, name="send", limit=63)(
        density,
        atom_site.reshape(3, 1, 16),
        atom_charge.reshape(1, 16),
        slot_atom.reshape(32, 2).T,
        slot_tile.reshape(32, 2).T,
        jnp.swapaxes(slot_shift.reshape(3, 32, 2), 1, 2),
    )
    got = exchanged(message, ("gy", "gz"))
    cells = [pltpu.VMEM((1024, 128), jnp.float32)]
    message = call(line_kernel, [(256, 128)], [VMEM] * 7, cells, "line")(
        got, t["shape"], t["order"].astype(jnp.bfloat16), t["z_tile"], t["twiddle"], t["z_even"], t["z_odd"]
    )
    got = exchanged(message, AXES)
    re, im, message = call(plane_kernel, [(128, 256), (128, 256), (256, 128)], [VMEM] * 5, name="plane")(
        got, t["y"], t["x"], t["column"], t["rows"]
    )
    got = exchanged(message, AXES)
    message = call(cycle_kernel, [(512, 128)], [VMEM] * 8, name="cycle")(
        got, re, im, t["column"], t["rows"], t["nodes"], t["x_back"], t["y_back"]
    )
    got = exchanged(message.reshape(256, 2, 128), AXES).reshape(512, 128)
    message = call(back_kernel, [(8, 64, 128)], [VMEM] * 6, cells, "back")(
        got, t["z_tile_back"], t["twiddle"], t["z_even_back"], t["z_odd_back"], t["z_last_back"]
    )
    got = exchanged(message, "gz").reshape(8, 2, 2, 16, 128)
    place = call(place_kernel, [(8, 2, 16, 128)] * 2, [VMEM], [pltpu.SemaphoreType.DMA((2,))], "place", HBM)
    return tuple(out.reshape(16, 16, 128) for out in place(got))


def solution(mesh):
    return jax.shard_map(
        per_device,
        mesh=mesh,
        in_specs=(
            P("gx", "gy", "gz"),
            P(None, "gx", "gy", "gz", None),
            P("gx", "gy", "gz", None),
            P("gx", "gy", "gz", None, None),
            P("gx", "gy", "gz", None, None),
            P(None, "gx", "gy", "gz", None, None),
        ),
        out_specs=(P("gx", "gy", "gz"), P("gx", "gy", "gz")),
        check_vma=False,
    )
```

```python
import functools

import jax
import jax.numpy as jnp
import ml_dtypes
import numpy as np
from jax import lax
from jax.experimental import pallas as pl
from jax.experimental.pallas import tpu as pltpu
from jax.sharding import PartitionSpec as P


METRIC = np.array([[3.24, 0.972, 0.648], [0.972, 3.2157, 0.9639], [0.648, 0.9639, 2.9565]])
INVERSE = np.array(
    [
        [0.3450043297, -0.0904572938, -0.0461258313],
        [-0.0904572938, 0.3683733435, -0.1002735462],
        [-0.0461258313, -0.1002735462, 0.3810394757],
    ]
)
FIRST_WEIGHTS = np.array([6.0 / 7.0, -15.0 / 56.0, 5.0 / 63.0, -1.0 / 56.0, 2.0 / 385.0, -1.0 / 5544.0])
SECOND_WEIGHTS = 2.0 * FIRST_WEIGHTS / np.arange(1, 7)
CENTER_WEIGHT = -2.0 * SECOND_WEIGHTS.sum()
JACOBI_SCALE = float(-CENTER_WEIGHT * np.trace(INVERSE))
STEP = 0.3
WIDTH_SQUARED = 9.0
RIDGE_SHARE = 0.01
NX, NY, NZ = 128, 64, 1024
AXES = ("gx", "gy", "gz")
HI = lax.Precision.HIGHEST
LOG2E = float(np.log2(np.e))
NODES = 16
LARGEST = STEP * 2.3721


def cos_sin(n, rows, columns):
    angle = 2.0 * np.pi * (np.outer(rows, columns) % n) / n
    return np.cos(angle), np.sin(angle)


def first_symbol(n):
    angle = 2.0 * np.pi * np.arange(n) / n
    return 2.0 * sum(w * np.sin((o + 1) * angle) for o, w in enumerate(FIRST_WEIGHTS))


def second_symbol(n):
    angle = 2.0 * np.pi * np.arange(n) / n
    return CENTER_WEIGHT + 2.0 * sum(w * np.cos((o + 1) * angle) for o, w in enumerate(SECOND_WEIGHTS))


def halves_of(table):
    high = table.astype(ml_dtypes.bfloat16)
    return high, (table - high.astype(np.float64)).astype(ml_dtypes.bfloat16)


ON_THE_RIGHT = ("z_even", "z_odd", "y", "y_back", "z_even_back", "z_odd_back", "z_last_back")
ON_THE_LEFT = ("z_tile", "x", "x_back", "z_tile_back")


@functools.lru_cache(maxsize=None)
def tables():
    eye = np.eye(32)
    freq = np.arange(128)
    c, s = cos_sin(128, freq, freq)
    t = {}
    t["z_tile"] = np.concatenate([c, -s], 0) / 32.0 / JACOBI_SCALE
    t["z_tile_back"] = np.concatenate([c, -s], 1) / 32.0
    t["twiddle"] = np.stack(cos_sin(1024, freq, np.arange(256) // 32))
    c, s = cos_sin(8, np.arange(4), np.arange(4))
    half_eye = np.eye(16)
    for odd, name in enumerate(("z_even", "z_odd")):
        ahead = np.zeros((2, 4, 32, 2, 2, 32))
        back = np.zeros((2, 2, 2, 16, 2, 4, 2, 16))
        for k in range(4):
            for n in range(2):
                cc, ss = c[k, 2 * n + odd], s[k, 2 * n + odd]
                ahead[0, k, :, n, 0], ahead[1, k, :, n, 0] = cc * eye, ss * eye
                ahead[0, k, :, n, 1], ahead[1, k, :, n, 1] = -ss * eye, cc * eye
                for x in range(2):
                    back[x, n, 0, :, 0, k, x], back[x, n, 1, :, 0, k, x] = 2.0 * cc * half_eye, -2.0 * ss * half_eye
                    back[x, n, 0, :, 1, k, x], back[x, n, 1, :, 1, k, x] = 2.0 * ss * half_eye, 2.0 * cc * half_eye
        t[name], t[name + "_back"] = ahead.reshape(256, 128), back.reshape(128, 256)
    last = np.zeros((2, 2, 2, 16, 4, 2, 16))
    for k in range(4):
        for x in range(2):
            last[x, 0, 1, :, k, x] = (-1.0) ** k * half_eye
    t["z_last_back"] = last.reshape(128, 128)
    half, b, j = np.meshgrid(np.arange(2), np.arange(4), np.arange(8), indexing="ij")
    c, s = cos_sin(64, (16 * b + 8 * half + j).reshape(-1), np.arange(64))
    c, s = c.reshape(2, 4, 8, 64) / 8.0, s.reshape(2, 4, 8, 64) / 8.0
    ahead = np.zeros((2, 2, 2, 4, 8, 2, 4, 64))
    for f in range(2):
        ahead[:, f, 0, :, :, 0, f], ahead[:, f, 1, :, :, 0, f] = c, s
        ahead[:, f, 0, :, :, 1, f], ahead[:, f, 1, :, :, 1, f] = -s, c
    ahead[:, 0, 1, :, :, 0, 2], ahead[:, 0, 1, :, :, 1, 2] = c, -s
    t["y"] = ahead.reshape(256, 512)
    c, s = cos_sin(64, np.arange(64), np.arange(64))
    c, s = c.reshape(64, 4, 16) / 8.0, s.reshape(64, 4, 16) / 8.0
    back = np.zeros((2, 2, 64, 4, 2, 2, 16))
    for f in range(2):
        back[0, f, :, :, f, 0], back[1, f, :, :, f, 0] = c, -s
        back[0, f, :, :, f, 1], back[1, f, :, :, f, 1] = s, c
    t["y_back"] = back.reshape(256, 256)
    c, s = cos_sin(128, freq, freq)
    t["x"] = np.block([[c, s], [-s, c]]) / np.sqrt(128.0)
    back = np.block([[c, -s], [s, c]]) / np.sqrt(128.0)
    t["x_back"] = back.reshape(2, 64, 2, 256).transpose(2, 0, 1, 3).reshape(256, 256)
    d1x, d1y, d1z = first_symbol(NX), first_symbol(NY), first_symbol(NZ)
    d2x, d2y, d2z = second_symbol(NX), second_symbol(NY), second_symbol(NZ)
    column = np.zeros((128, 128))
    column[:, 0], column[:, 1] = -INVERSE[0, 0] * d2x / JACOBI_SCALE, d1x
    rows = np.zeros((256, 512))
    for d in range(256):
        low = d % 128 + 128 * (d // 128)
        for f, kz in enumerate((low, low + 256, 512)):
            rows[d, 64 * f : 64 * f + 64] = (
                -(INVERSE[1, 1] * d2y + INVERSE[2, 2] * d2z[kz]) + 2.0 * INVERSE[1, 2] * d1y * d1z[kz]
            ) / JACOBI_SCALE
            rows[d, 256 + 64 * f : 320 + 64 * f] = (
                2.0 * (INVERSE[0, 1] * d1y + INVERSE[0, 2] * d1z[kz]) / JACOBI_SCALE
            )
    t["column"], t["rows"] = column, rows
    angle = (np.arange(NODES) + 0.5) * np.pi / NODES
    nodes = np.zeros((136, 128))
    nodes[:NODES, :NODES] = 2.0 / NODES * np.cos(np.outer(np.arange(NODES), angle))
    nodes[0, :NODES] = 1.0 / NODES
    nodes[128, :NODES] = 0.5 * LARGEST * (1.0 + np.cos(angle))
    t["nodes"] = nodes
    t["order"] = np.eye(256).reshape(4, 8, 8, 256).transpose(1, 0, 2, 3).reshape(256, 256).T
    for name in ON_THE_RIGHT:
        high, low = halves_of(t[name])
        t[name] = np.concatenate([high, low, high], 0)
    for name in ON_THE_LEFT:
        high, low = halves_of(t[name])
        t[name] = np.concatenate([high, low, high], 1)
    t["order"] = t["order"].astype(ml_dtypes.bfloat16)
    return {n: v if v.dtype == ml_dtypes.bfloat16 else v.astype(np.float32) for n, v in t.items()}


def dot(a, b, contract=((1,), (0,))):
    return lax.dot_general(a, b, (contract, ((), ())), precision=HI, preferred_element_type=jnp.float32)


def index_of(shape, dim):
    return lax.broadcasted_iota(jnp.int32, shape, dim)


def solve(gram):
    ff, fc, cc, fs, cs = gram
    ridge = RIDGE_SHARE * 0.5 * (ff + cc)
    ff, cc = ff + ridge, cc + ridge
    determinant = ff * cc - fc * fc
    return (cc * fs - fc * cs) / determinant, (ff * cs - fc * fs) / determinant


def stack_rows(rows, count):
    at = index_of((count, 128), 0)
    stacked = jnp.zeros((count, 128), jnp.float32)
    for n, row in enumerate(rows):
        stacked = jnp.where(at == n, row, stacked)
    return stacked


def sums_on_lanes(arrays):
    rows = []
    for array in arrays:
        row = jnp.sum(array, axis=0, keepdims=True)
        rows.append(row[:, :128] + row[:, 128:])
    count = -(-len(rows) // 8) * 8
    totals = jnp.sum(stack_rows(rows, count), axis=1, keepdims=True)
    mine = index_of((count, 128), 0) == index_of((count, 128), 1)
    return jnp.sum(jnp.where(mine, totals, 0.0), axis=0, keepdims=True)


def in_three(array):
    high = array.astype(jnp.bfloat16)
    rest = array - high.astype(jnp.float32)
    middle = rest.astype(jnp.bfloat16)
    return high, middle, (rest - middle.astype(jnp.float32)).astype(jnp.bfloat16)


def exact_dot(a, b, contract=((1,), (0,))):
    return lax.dot_general(a, b, (contract, ((), ())), preferred_element_type=jnp.float32)


def in_two(array, axis):
    high = array.astype(jnp.bfloat16)
    low = (array - high.astype(jnp.float32)).astype(jnp.bfloat16)
    return jnp.concatenate([high, high, low], axis)


def times(data, table):
    return exact_dot(in_two(data, 1), table[...])


def applied(table, data):
    return exact_dot(table[...], in_two(data, 0))


def send_kernel(density, *refs):
    held, out, slots, done = refs[:5], refs[5], refs[6:11], refs[11]
    copies = [pltpu.make_async_copy(a, b, done.at[n]) for n, (a, b) in enumerate(zip(held, slots))]
    for half in range(2):
        into = out.at[16 * half : 16 * half + 16, 0:8, :]
        copies.append(pltpu.make_async_copy(density.at[:, 8 * half : 8 * half + 8, :], into, done.at[5 + half]))
    for copy in copies:
        copy.start()
    for copy in copies[:5]:
        copy.wait()
    site, charge, atom, tile, shift = slots
    values = [jnp.zeros((2, 32), jnp.float32) for _ in range(4)]
    for n in range(16):
        hit = atom[...] == n
        for p in range(3):
            values[p] = jnp.where(hit, site[p, 0, n], values[p])
        values[3] = jnp.where(hit, charge[0, n], values[3])
    for p in range(3):
        values[p] = values[p] + 4.0 * shift[p].astype(jnp.float32)
    code = tile[...]
    values.append(((code & 15) + 16 * (index_of((2, 32), 1) & 7)).astype(jnp.float32))
    values.append((code >> 4).astype(jnp.float32))
    lane = index_of((8, 128), 1)
    packed = jnp.zeros((8, 128), jnp.float32)
    for e in range(2):
        rows = [jnp.concatenate([v[e : e + 1], jnp.zeros((1, 96), jnp.float32)], 1) for v in values]
        rows = stack_rows(rows, 8)
        for b in range(4):
            moved = pltpu.roll(rows, 8 * b + 8 * e, 1)
            packed = jnp.where((lane >> 3) == 2 * b + e, moved, packed)
    out[:, 8:16, :] = jnp.broadcast_to(packed[None], (32, 8, 128))
    for copy in copies[5:]:
        copy.wait()


def line_kernel(got, order, z_tile, twiddle, z_even, z_odd, out, cells):
    rank = lax.axis_index("gy") * 8 + lax.axis_index("gz")
    x, half = rank & 15, rank >> 4
    own = ((x >> 3) * 2 + half).astype(jnp.float32)
    along = (x & 7).astype(jnp.float32)
    lane = index_of((8, 128), 1)
    at_j = index_of((8, 512), 0).astype(jnp.float32) - 3.5
    tile_at = index_of((128, 512), 0).astype(jnp.float32)
    scale = -LOG2E / WIDTH_SQUARED
    charge = []
    for b in range(4):
        parts = []
        for g in range(4):
            part = jnp.zeros((8, 128), jnp.float32)
            for r in range(8):
                moved = got[8 * g + r, 8:16, :]
                if r != b:
                    moved = pltpu.roll(moved, (16 * (r - b)) % 128, 1)
                part = jnp.where((lane >> 4) == r, moved, part)
            parts.append(part)
        slots = jnp.concatenate(parts, 1)
        ex = along - slots[0:1]
        vy, vz = slots[1:2] - 3.5, slots[2:3] - 3.5
        m = METRIC
        fixed = m[0, 0] * ex * ex + m[1, 1] * vy * vy + m[2, 2] * vz * vz
        fixed = fixed - 2.0 * m[0, 1] * ex * vy - 2.0 * m[0, 2] * ex * vz + 2.0 * m[1, 2] * vy * vz
        by_j = -2.0 * m[1, 1] * vy + 2.0 * m[0, 1] * ex - 2.0 * m[1, 2] * vz
        by_k = -2.0 * m[2, 2] * vz + 2.0 * m[0, 2] * ex - 2.0 * m[1, 2] * vy
        exponents = []
        for k in range(8):
            at_k = k - 3.5
            row = scale * (fixed + at_k * by_k + m[2, 2] * at_k * at_k)
            exponents.append(row + at_j * (scale * by_j + 2.0 * scale * m[1, 2] * at_k + scale * m[1, 1] * at_j))
        blocks = jnp.exp2(jnp.concatenate(exponents, 0))
        peak = jnp.where(slots[5:6] == own, slots[3:4], 0.0)
        placed = jnp.where(slots[4:5] == tile_at, 1.0, 0.0).astype(jnp.bfloat16)
        parts = jnp.concatenate(in_three(blocks * peak), 0)
        charge.append(exact_dot(placed, parts, ((1,), (1,))))
    charge = [c[:, 0:64] + c[:, 64:128] + c[:, 128:192] for c in charge]
    charge = jnp.concatenate(in_three(jnp.concatenate(charge, 1)), 1)
    charge = exact_dot(charge, jnp.concatenate([order[...]] * 3, 0))
    for c in range(8):
        piece = jnp.concatenate([got[8 * b + c, 0:8, :] for b in range(4)], 0)
        cells[128 * c : 128 * c + 128, :] = jnp.transpose(jnp.concatenate([piece] * 4, 0))
    group = index_of((128, 128), 1) >> 5
    sides = []
    for side in range(2):
        total = jnp.zeros((128, 128), jnp.float32)
        for n in range(4):
            total = jnp.where(group == n, cells[pl.ds(4 * side + n, 128, stride=8), :], total)
        sides.append(total)
    field = jnp.concatenate(sides, 1) + charge
    spectrum = applied(z_tile, field)
    re, im = spectrum[:128], spectrum[128:]
    re, im = re * twiddle[0] + im * twiddle[1], im * twiddle[0] - re * twiddle[1]
    even = jnp.concatenate([re[:, :128] + re[:, 128:], im[:, :128] + im[:, 128:]], 1)
    odd = jnp.concatenate([re[:, :128] - re[:, 128:], im[:, :128] - im[:, 128:]], 1)
    out[0:128, :] = times(even, z_even)
    out[128:256, :] = times(odd, z_odd)
    last = jnp.where((lane >> 5) & 1 == 0, even[0:8, 0:128], -even[0:8, 0:128])
    last = last + pltpu.roll(last, 64, 1)
    last = last + pltpu.roll(last, 32, 1)
    here = (index_of((8, 128), 0) == 0) & ((lane >> 5) == 1)
    out[0:8, :] = jnp.where(here, last, out[0:8, :])


def eigenvalues(column, rows):
    rank = (lax.axis_index("gx") * 4 + lax.axis_index("gy")) * 8 + lax.axis_index("gz")
    mine = rows[pl.ds(rank, 1), :]
    return column[:, 0:1] + mine[:, 0:256] + column[:, 1:2] * mine[:, 256:512], rank


def weights_of(rank):
    field = index_of((1, 256), 1) >> 6
    first = jnp.where(field == 1, 2.0, jnp.where(field == 3, 0.0, 1.0))
    other = jnp.where(field < 2, 2.0, 0.0)
    return jnp.where(rank == 0, first, other)


def plane_kernel(got, y, x, column, rows, out_re, out_im, out):
    lam, rank = eigenvalues(column, rows)
    first = jnp.where(rank == 0, 1.0, 0.0).astype(jnp.float32)
    halves = [jnp.concatenate([got[32 * a + 16 * h : 32 * a + 16 * h + 16, :] for a in range(8)], 0) for h in range(2)]
    lines = times(jnp.concatenate(halves, 1), y)
    spectrum = applied(x, jnp.concatenate([lines[:, :256], lines[:, 256:]], 0))
    re, im = spectrum[:128], spectrum[128:]
    re, im = (
        jnp.concatenate([re[:, :128] + first * im[:, 128:], re[:, 128:]], 1),
        jnp.concatenate([im[:, :128] - first * re[:, 128:], im[:, 128:]], 1),
    )
    out_re[...] = re
    out_im[...] = im
    a = STEP * lam
    power = (re * re + im * im) * weights_of(rank) * a
    double = a * (4.0 / LARGEST) - 2.0
    moments = [power, 0.5 * double * power]
    while len(moments) < NODES:
        moments.append(double * moments[-1] - moments[-2])
    out[...] = jnp.broadcast_to(sums_on_lanes(moments), (256, 128))


def cycle_kernel(got, re_in, im_in, column, rows, nodes, x_back, y_back, out):
    moments = jnp.sum(got[...], axis=0, keepdims=True)
    weight = dot(jnp.broadcast_to(moments, (8, 128)), nodes[0:128, :])[0:1]
    node = nodes[128:129, :]
    lam, rank = eigenvalues(column, rows)
    first = jnp.where(rank == 0, 1.0, 0.0).astype(jnp.float32)
    fine = STEP * lam
    sides = [(node, 1.0 - node), (fine, 1.0 - fine)]
    scaled, potential = [1.0, 1.0], 0.0
    for cycle in range(3):
        a, mu = sides[0]
        low = weight * scaled[0] * scaled[0]
        products = [low * a, low * a * mu, low * a * mu * mu, -low * mu * mu, -low * mu * mu * mu]
        g0, g1 = solve([jnp.sum(p, axis=1, keepdims=True) for p in products])
        a, mu = sides[1]
        potential = potential + STEP * scaled[1] * (1.0 + mu * ((1.0 - g0) + (1.0 - g1) * mu))
        if cycle < 2:
            scaled = [s * mu * (mu * mu + a * (g0 + mu * g1)) for s, (a, mu) in zip(scaled, sides)]
    residual = JACOBI_SCALE * scaled[1] * mu * mu
    re, im = re_in[...], im_in[...]
    columns = []
    for multiplier in (potential, residual):
        fr, fi = multiplier * re, multiplier * im
        columns.append(
            jnp.concatenate([fr[:, :128] - first * fi[:, 128:], fi[:, :128] + first * fr[:, 128:]], 0)
        )
    planes = applied(x_back, jnp.concatenate(columns, 1))
    lines = []
    for f in range(2):
        for odd in range(2):
            at = 128 * odd
            pair = [planes[at + n : at + n + 64, 128 * f : 128 * f + 128] for n in (0, 64)]
            lines.append(jnp.concatenate(pair, 1))
    lines = times(jnp.concatenate(lines, 0), y_back)
    left = index_of((64, 128), 1) < 64
    for f in range(2):
        for b in range(4):
            side = slice(128 * (b // 2), 128 * (b // 2) + 128)
            even, odd = lines[128 * f : 128 * f + 64, side], lines[128 * f + 64 : 128 * f + 128, side]
            if b % 2 == 0:
                odd = pltpu.roll(odd, 64, 1)
            else:
                even = pltpu.roll(even, 64, 1)
            message = jnp.where(left, even, odd)
            for n in range(8):
                out[pl.ds((32 * n + 8 * b) * 2 + f, 8, stride=2), :] = message[8 * n : 8 * n + 8]


def back_kernel(got, z_tile_back, twiddle, z_even_back, z_odd_back, z_last_back, out, cells):
    spectra = [got[pl.ds(f, 256, stride=2), :] for f in range(2)]
    low = jnp.concatenate([v[:128] for v in spectra], 0)
    high = jnp.concatenate([v[128:] for v in spectra], 0)
    top = index_of((256, 128), 0) & 127 == 0
    part = (index_of((256, 128), 1) & 63) >> 4
    last = jnp.where(top & (part == 1), low, 0.0)
    low = jnp.where(top & (part < 2), jnp.where(part == 0, 0.5 * low, 0.0), low)
    last = times(jnp.concatenate([last[0:8], last[128:136]], 0), z_last_back)
    even, odd = times(low, z_even_back), times(high, z_odd_back)
    turned = []
    for f in range(2):
        e, o = even[128 * f : 128 * f + 128], odd[128 * f : 128 * f + 128]
        real = jnp.concatenate([e[0:8, :128] + last[8 * f : 8 * f + 8], e[8:, :128]], 0)
        re = jnp.concatenate([real + o[:, :128], real - o[:, :128]], 1)
        im = jnp.concatenate([e[:, 128:] + o[:, 128:], e[:, 128:] - o[:, 128:]], 1)
        turned.append(
            jnp.concatenate([re * twiddle[0] - im * twiddle[1], im * twiddle[0] + re * twiddle[1]], 0)
        )
    fields = applied(z_tile_back, jnp.concatenate(turned, 1))
    group = index_of((128, 128), 1) >> 5
    for side in range(2):
        one = fields[:, 128 * side : 128 * side + 128]
        two = fields[:, 256 + 128 * side : 384 + 128 * side]
        for n in range(4):
            lower = one if n == 0 else pltpu.roll(one, 128 - 32 * n, 1)
            upper = two if n == 1 else pltpu.roll(two, (160 - 32 * n) % 128, 1)
            cells[pl.ds(4 * side + n, 128, stride=8), :] = jnp.where(group == 0, lower, upper)
    for c in range(8):
        out[c] = jnp.transpose(cells[128 * c : 128 * c + 128, :])[0:64]


def place_kernel(got, potential, residual, done):
    copies = [
        pltpu.make_async_copy(got.at[:, f], out, done.at[f]) for f, out in enumerate((potential, residual))
    ]
    for copy in copies:
        copy.start()
    for copy in copies:
        copy.wait()


VMEM = pl.BlockSpec(memory_space=pltpu.VMEM)
HBM = pl.BlockSpec(memory_space=pltpu.HBM)


def call(kernel, out_shapes, specs, scratch=(), name=None, result=VMEM, limit=16):
    shapes = [jax.ShapeDtypeStruct(s, jnp.float32) for s in out_shapes]
    single = len(shapes) == 1
    return pl.pallas_call(
        kernel,
        out_shape=shapes[0] if single else shapes,
        in_specs=specs,
        out_specs=result if single else [result] * len(shapes),
        scratch_shapes=list(scratch),
        compiler_params=pltpu.CompilerParams(vmem_limit_bytes=limit * 1024 * 1024),
        name=name,
    )


def exchanged(array, axes):
    return lax.all_to_all(array, axes, 0, 0, tiled=True)


def per_device(density, atom_site, atom_charge, slot_atom, slot_tile, slot_shift):
    t = {name: jnp.asarray(value) for name, value in tables().items()}
    scratch = [
        pltpu.SMEM((3, 1, 16), jnp.float32),
        pltpu.SMEM((1, 16), jnp.float32),
        pltpu.VMEM((2, 32), jnp.int32),
        pltpu.VMEM((2, 32), jnp.int32),
        pltpu.VMEM((3, 2, 32), jnp.int32),
        pltpu.SemaphoreType.DMA((7,)),
    ]
    message = call(send_kernel, [(32, 16, 128)], [HBM] * 6, scratch, name="send", limit=63)(
        density,
        atom_site.reshape(3, 1, 16),
        atom_charge.reshape(1, 16),
        slot_atom.reshape(32, 2).T,
        slot_tile.reshape(32, 2).T,
        jnp.swapaxes(slot_shift.reshape(3, 32, 2), 1, 2),
    )
    got = exchanged(message, ("gy", "gz"))
    cells = [pltpu.VMEM((1024, 128), jnp.float32)]
    message = call(line_kernel, [(256, 128)], [VMEM] * 6, cells, "line")(
        got, t["order"], t["z_tile"], t["twiddle"], t["z_even"], t["z_odd"]
    )
    got = exchanged(message, AXES)
    re, im, message = call(plane_kernel, [(128, 256), (128, 256), (256, 128)], [VMEM] * 5, name="plane")(
        got, t["y"], t["x"], t["column"], t["rows"]
    )
    got = exchanged(message, AXES)
    message = call(cycle_kernel, [(512, 128)], [VMEM] * 8, name="cycle")(
        got, re, im, t["column"], t["rows"], t["nodes"], t["x_back"], t["y_back"]
    )
    got = exchanged(message.reshape(256, 2, 128), AXES).reshape(512, 128)
    message = call(back_kernel, [(8, 64, 128)], [VMEM] * 6, cells, "back")(
        got, t["z_tile_back"], t["twiddle"], t["z_even_back"], t["z_odd_back"], t["z_last_back"]
    )
    got = exchanged(message, "gz").reshape(8, 2, 2, 16, 128)
    place = call(place_kernel, [(8, 2, 16, 128)] * 2, [VMEM], [pltpu.SemaphoreType.DMA((2,))], "place", HBM)
    return tuple(out.reshape(16, 16, 128) for out in place(got))


def solution(mesh):
    return jax.shard_map(
        per_device,
        mesh=mesh,
        in_specs=(
            P("gx", "gy", "gz"),
            P(None, "gx", "gy", "gz", None),
            P("gx", "gy", "gz", None),
            P("gx", "gy", "gz", None, None),
            P("gx", "gy", "gz", None, None),
            P(None, "gx", "gy", "gz", None, None),
        ),
        out_specs=(P("gx", "gy", "gz"), P("gx", "gy", "gz")),
        check_vma=False,
    )
```

```python
import functools

import jax
import jax.numpy as jnp
import ml_dtypes
import numpy as np
from jax import lax
from jax.experimental import pallas as pl
from jax.experimental.pallas import tpu as pltpu
from jax.sharding import PartitionSpec as P


METRIC = np.array([[3.24, 0.972, 0.648], [0.972, 3.2157, 0.9639], [0.648, 0.9639, 2.9565]])
INVERSE = np.array(
    [
        [0.3450043297, -0.0904572938, -0.0461258313],
        [-0.0904572938, 0.3683733435, -0.1002735462],
        [-0.0461258313, -0.1002735462, 0.3810394757],
    ]
)
FIRST_WEIGHTS = np.array([6.0 / 7.0, -15.0 / 56.0, 5.0 / 63.0, -1.0 / 56.0, 2.0 / 385.0, -1.0 / 5544.0])
SECOND_WEIGHTS = 2.0 * FIRST_WEIGHTS / np.arange(1, 7)
CENTER_WEIGHT = -2.0 * SECOND_WEIGHTS.sum()
JACOBI_SCALE = float(-CENTER_WEIGHT * np.trace(INVERSE))
STEP = 0.3
WIDTH_SQUARED = 9.0
RIDGE_SHARE = 0.01
NX, NY, NZ = 128, 64, 1024
AXES = ("gx", "gy", "gz")
HI = lax.Precision.HIGHEST
LOG2E = float(np.log2(np.e))
NODES = 16
LARGEST = STEP * 2.3721


def cos_sin(n, rows, columns):
    angle = 2.0 * np.pi * (np.outer(rows, columns) % n) / n
    return np.cos(angle), np.sin(angle)


def first_symbol(n):
    angle = 2.0 * np.pi * np.arange(n) / n
    return 2.0 * sum(w * np.sin((o + 1) * angle) for o, w in enumerate(FIRST_WEIGHTS))


def second_symbol(n):
    angle = 2.0 * np.pi * np.arange(n) / n
    return CENTER_WEIGHT + 2.0 * sum(w * np.cos((o + 1) * angle) for o, w in enumerate(SECOND_WEIGHTS))


def halves_of(table):
    high = table.astype(ml_dtypes.bfloat16)
    return high, (table - high.astype(np.float64)).astype(ml_dtypes.bfloat16)


ON_THE_RIGHT = ("z_even", "z_odd", "y", "y_back", "z_even_back", "z_odd_back", "z_last_back")
ON_THE_LEFT = ("z_tile", "x", "x_back", "z_tile_back")


@functools.lru_cache(maxsize=None)
def tables():
    eye = np.eye(32)
    freq = np.arange(128)
    c, s = cos_sin(128, freq, freq)
    t = {}
    t["z_tile"] = np.concatenate([c, -s], 0) / 32.0 / JACOBI_SCALE
    t["z_tile_back"] = np.concatenate([c, -s], 1) / 32.0
    t["twiddle"] = np.stack(cos_sin(1024, freq, np.arange(256) // 32))
    c, s = cos_sin(8, np.arange(4), np.arange(4))
    half_eye = np.eye(16)
    for odd, name in enumerate(("z_even", "z_odd")):
        ahead = np.zeros((2, 4, 32, 2, 2, 32))
        back = np.zeros((2, 2, 2, 16, 2, 4, 2, 16))
        for k in range(4):
            for n in range(2):
                cc, ss = c[k, 2 * n + odd], s[k, 2 * n + odd]
                ahead[0, k, :, n, 0], ahead[1, k, :, n, 0] = cc * eye, ss * eye
                ahead[0, k, :, n, 1], ahead[1, k, :, n, 1] = -ss * eye, cc * eye
                for x in range(2):
                    back[x, n, 0, :, 0, k, x], back[x, n, 1, :, 0, k, x] = 2.0 * cc * half_eye, -2.0 * ss * half_eye
                    back[x, n, 0, :, 1, k, x], back[x, n, 1, :, 1, k, x] = 2.0 * ss * half_eye, 2.0 * cc * half_eye
        t[name], t[name + "_back"] = ahead.reshape(256, 128), back.reshape(128, 256)
    last = np.zeros((2, 2, 2, 16, 4, 2, 16))
    for k in range(4):
        for x in range(2):
            last[x, 0, 1, :, k, x] = (-1.0) ** k * half_eye
    t["z_last_back"] = last.reshape(128, 128)
    half, b, j = np.meshgrid(np.arange(2), np.arange(4), np.arange(8), indexing="ij")
    c, s = cos_sin(64, (16 * b + 8 * half + j).reshape(-1), np.arange(64))
    c, s = c.reshape(2, 4, 8, 64) / 8.0, s.reshape(2, 4, 8, 64) / 8.0
    ahead = np.zeros((2, 2, 2, 4, 8, 2, 4, 64))
    for f in range(2):
        ahead[:, f, 0, :, :, 0, f], ahead[:, f, 1, :, :, 0, f] = c, s
        ahead[:, f, 0, :, :, 1, f], ahead[:, f, 1, :, :, 1, f] = -s, c
    ahead[:, 0, 1, :, :, 0, 2], ahead[:, 0, 1, :, :, 1, 2] = c, -s
    t["y"] = ahead.reshape(256, 512)
    c, s = cos_sin(64, np.arange(64), np.arange(64))
    c, s = c.reshape(64, 4, 16) / 8.0, s.reshape(64, 4, 16) / 8.0
    back = np.zeros((2, 2, 64, 4, 2, 2, 16))
    for f in range(2):
        back[0, f, :, :, f, 0], back[1, f, :, :, f, 0] = c, -s
        back[0, f, :, :, f, 1], back[1, f, :, :, f, 1] = s, c
    t["y_back"] = back.reshape(256, 256)
    c, s = cos_sin(128, freq, freq)
    t["x"] = np.block([[c, s], [-s, c]]) / np.sqrt(128.0)
    back = np.block([[c, -s], [s, c]]) / np.sqrt(128.0)
    t["x_back"] = back.reshape(2, 64, 2, 256).transpose(2, 0, 1, 3).reshape(256, 256)
    d1x, d1y, d1z = first_symbol(NX), first_symbol(NY), first_symbol(NZ)
    d2x, d2y, d2z = second_symbol(NX), second_symbol(NY), second_symbol(NZ)
    column = np.zeros((128, 128))
    column[:, 0], column[:, 1] = -INVERSE[0, 0] * d2x / JACOBI_SCALE, d1x
    by_ky = np.zeros((8, 256))
    by_ky[0] = np.tile(-INVERSE[1, 1] * d2y / JACOBI_SCALE, 4)
    by_ky[1] = np.tile(2.0 * INVERSE[1, 2] * d1y / JACOBI_SCALE, 4)
    by_ky[2] = np.tile(2.0 * INVERSE[0, 1] * d1y / JACOBI_SCALE, 4)
    by_kz = np.zeros((256, 128))
    low = np.arange(256)
    for f, kz in enumerate((low, low + 256, 0 * low + 512)):
        by_kz[:, 2 * f], by_kz[:, 2 * f + 1] = -INVERSE[2, 2] * d2z[kz] / JACOBI_SCALE, d1z[kz]
    t["column"], t["by_ky"], t["by_kz"] = column, by_ky, by_kz
    angle = (np.arange(NODES) + 0.5) * np.pi / NODES
    nodes = np.zeros((136, 128))
    nodes[:NODES, :NODES] = 2.0 / NODES * np.cos(np.outer(np.arange(NODES), angle))
    nodes[0, :NODES] = 1.0 / NODES
    nodes[128, :NODES] = 0.5 * LARGEST * (1.0 + np.cos(angle))
    t["nodes"] = nodes
    t["order"] = np.eye(256).reshape(4, 8, 8, 256).transpose(1, 0, 2, 3).reshape(256, 256).T
    for name in ON_THE_RIGHT:
        high, low = halves_of(t[name])
        t[name] = np.concatenate([high, low], 0)
    for name in ON_THE_LEFT:
        high, low = halves_of(t[name])
        t[name] = np.concatenate([high, low], 1)
    t["order"] = t["order"].astype(ml_dtypes.bfloat16)
    return {n: v if v.dtype == ml_dtypes.bfloat16 else v.astype(np.float32) for n, v in t.items()}


def dot(a, b, contract=((1,), (0,))):
    return lax.dot_general(a, b, (contract, ((), ())), precision=HI, preferred_element_type=jnp.float32)


def index_of(shape, dim):
    return lax.broadcasted_iota(jnp.int32, shape, dim)


def solve(gram):
    ff, fc, cc, fs, cs = gram
    ridge = RIDGE_SHARE * 0.5 * (ff + cc)
    ff, cc = ff + ridge, cc + ridge
    determinant = ff * cc - fc * fc
    return (cc * fs - fc * cs) / determinant, (ff * cs - fc * fs) / determinant


def stack_rows(rows, count):
    at = index_of((count, 128), 0)
    stacked = jnp.zeros((count, 128), jnp.float32)
    for n, row in enumerate(rows):
        stacked = jnp.where(at == n, row, stacked)
    return stacked


def sums_on_lanes(arrays):
    rows = []
    for array in arrays:
        row = jnp.sum(array, axis=0, keepdims=True)
        rows.append(row[:, :128] + row[:, 128:])
    count = -(-len(rows) // 8) * 8
    totals = jnp.sum(stack_rows(rows, count), axis=1, keepdims=True)
    mine = index_of((count, 128), 0) == index_of((count, 128), 1)
    return jnp.sum(jnp.where(mine, totals, 0.0), axis=0, keepdims=True)


def in_three(array):
    high = array.astype(jnp.bfloat16)
    rest = array - high.astype(jnp.float32)
    middle = rest.astype(jnp.bfloat16)
    return high, middle, (rest - middle.astype(jnp.float32)).astype(jnp.bfloat16)


def exact_dot(a, b, contract=((1,), (0,))):
    return lax.dot_general(a, b, (contract, ((), ())), preferred_element_type=jnp.float32)


def in_two(array, axis):
    high = array.astype(jnp.bfloat16)
    low = (array - high.astype(jnp.float32)).astype(jnp.bfloat16)
    return jnp.concatenate([high, high, low], axis)


def times(data, table):
    return exact_dot(in_two(data, 1), jnp.concatenate([table[...], table[0 : table.shape[0] // 2, :]], 0))


def applied(table, data):
    return exact_dot(jnp.concatenate([table[...], table[:, 0 : table.shape[1] // 2]], 1), in_two(data, 0))


def send_kernel(density, *refs):
    held, out, slots, done = refs[:5], refs[5], refs[6:11], refs[11]
    copies = [pltpu.make_async_copy(a, b, done.at[n]) for n, (a, b) in enumerate(zip(held, slots))]
    for half in range(2):
        into = out.at[16 * half : 16 * half + 16, 0:8, :]
        copies.append(pltpu.make_async_copy(density.at[:, 8 * half : 8 * half + 8, :], into, done.at[5 + half]))
    for copy in copies:
        copy.start()
    for copy in copies[:5]:
        copy.wait()
    site, charge, atom, tile, shift = slots
    values = [jnp.zeros((2, 32), jnp.float32) for _ in range(4)]
    for n in range(16):
        hit = atom[...] == n
        for p in range(3):
            values[p] = jnp.where(hit, site[p, 0, n], values[p])
        values[3] = jnp.where(hit, charge[0, n], values[3])
    for p in range(3):
        values[p] = values[p] + 4.0 * shift[p].astype(jnp.float32)
    code = tile[...]
    values.append(((code & 15) + 16 * (index_of((2, 32), 1) & 7)).astype(jnp.float32))
    values.append((code >> 4).astype(jnp.float32))
    lane = index_of((8, 128), 1)
    packed = jnp.zeros((8, 128), jnp.float32)
    for e in range(2):
        rows = [jnp.concatenate([v[e : e + 1], jnp.zeros((1, 96), jnp.float32)], 1) for v in values]
        rows = stack_rows(rows, 8)
        for b in range(4):
            moved = pltpu.roll(rows, 8 * b + 8 * e, 1)
            packed = jnp.where((lane >> 3) == 2 * b + e, moved, packed)
    out[:, 8:16, :] = jnp.broadcast_to(packed[None], (32, 8, 128))
    for copy in copies[5:]:
        copy.wait()


def line_kernel(got, order, z_tile, twiddle, z_even, z_odd, out, cells):
    rank = lax.axis_index("gy") * 8 + lax.axis_index("gz")
    x, half = rank & 15, rank >> 4
    own = ((x >> 3) * 2 + half).astype(jnp.float32)
    along = (x & 7).astype(jnp.float32)
    lane = index_of((8, 128), 1)
    at_j = index_of((8, 512), 0).astype(jnp.float32) - 3.5
    tile_at = index_of((128, 512), 0).astype(jnp.float32)
    scale = -LOG2E / WIDTH_SQUARED
    charge = []
    for b in range(4):
        parts = []
        for g in range(4):
            part = jnp.zeros((8, 128), jnp.float32)
            for r in range(8):
                moved = got[8 * g + r, 8:16, :]
                if r != b:
                    moved = pltpu.roll(moved, (16 * (r - b)) % 128, 1)
                part = jnp.where((lane >> 4) == r, moved, part)
            parts.append(part)
        slots = jnp.concatenate(parts, 1)
        ex = along - slots[0:1]
        vy, vz = slots[1:2] - 3.5, slots[2:3] - 3.5
        m = METRIC
        fixed = m[0, 0] * ex * ex + m[1, 1] * vy * vy + m[2, 2] * vz * vz
        fixed = fixed - 2.0 * m[0, 1] * ex * vy - 2.0 * m[0, 2] * ex * vz + 2.0 * m[1, 2] * vy * vz
        by_j = -2.0 * m[1, 1] * vy + 2.0 * m[0, 1] * ex - 2.0 * m[1, 2] * vz
        by_k = -2.0 * m[2, 2] * vz + 2.0 * m[0, 2] * ex - 2.0 * m[1, 2] * vy
        exponents = []
        for k in range(8):
            at_k = k - 3.5
            row = scale * (fixed + at_k * by_k + m[2, 2] * at_k * at_k)
            exponents.append(row + at_j * (scale * by_j + 2.0 * scale * m[1, 2] * at_k + scale * m[1, 1] * at_j))
        blocks = jnp.exp2(jnp.concatenate(exponents, 0))
        peak = jnp.where(slots[5:6] == own, slots[3:4], 0.0)
        placed = jnp.where(slots[4:5] == tile_at, 1.0, 0.0).astype(jnp.bfloat16)
        parts = jnp.concatenate(in_three(blocks * peak), 0)
        charge.append(exact_dot(placed, parts, ((1,), (1,))))
    charge = [c[:, 0:64] + c[:, 64:128] + c[:, 128:192] for c in charge]
    charge = jnp.concatenate(in_three(jnp.concatenate(charge, 1)), 1)
    charge = exact_dot(charge, jnp.concatenate([order[...]] * 3, 0))
    for c in range(8):
        piece = jnp.concatenate([got[8 * b + c, 0:8, :] for b in range(4)], 0)
        cells[128 * c : 128 * c + 128, :] = jnp.transpose(jnp.concatenate([piece] * 4, 0))
    group = index_of((128, 128), 1) >> 5
    sides = []
    for side in range(2):
        total = jnp.zeros((128, 128), jnp.float32)
        for n in range(4):
            total = jnp.where(group == n, cells[pl.ds(4 * side + n, 128, stride=8), :], total)
        sides.append(total)
    field = jnp.concatenate(sides, 1) + charge
    spectrum = applied(z_tile, field)
    re, im = spectrum[:128], spectrum[128:]
    re, im = re * twiddle[0] + im * twiddle[1], im * twiddle[0] - re * twiddle[1]
    even = jnp.concatenate([re[:, :128] + re[:, 128:], im[:, :128] + im[:, 128:]], 1)
    odd = jnp.concatenate([re[:, :128] - re[:, 128:], im[:, :128] - im[:, 128:]], 1)
    out[0:128, :] = times(even, z_even)
    out[128:256, :] = times(odd, z_odd)
    last = jnp.where((lane >> 5) & 1 == 0, even[0:8, 0:128], -even[0:8, 0:128])
    last = last + pltpu.roll(last, 64, 1)
    last = last + pltpu.roll(last, 32, 1)
    here = (index_of((8, 128), 0) == 0) & ((lane >> 5) == 1)
    out[0:8, :] = jnp.where(here, last, out[0:8, :])


def own_rank():
    return (lax.axis_index("gx") * 4 + lax.axis_index("gy")) * 8 + lax.axis_index("gz")


def eigenvalues(column, by_ky, by_kz):
    rank = own_rank()
    mine = by_kz[pl.ds(rank, 1), :]
    field = index_of((1, 256), 1) >> 6
    second, first = [
        jnp.where(field == 0, mine[:, n : n + 1], jnp.where(field == 1, mine[:, n + 2 : n + 3], mine[:, n + 4 : n + 5]))
        for n in range(2)
    ]
    row = by_ky[0:1, :] + second + by_ky[1:2, :] * first
    other = by_ky[2:3, :] + (2.0 * INVERSE[0, 2] / JACOBI_SCALE) * first
    return column[:, 0:1] + row + column[:, 1:2] * other, rank


def weights_of(rank):
    field = index_of((1, 256), 1) >> 6
    first = jnp.where(field == 1, 2.0, jnp.where(field == 3, 0.0, 1.0))
    other = jnp.where(field < 2, 2.0, 0.0)
    return jnp.where(rank == 0, first, other)


def plane_kernel(got, y, x, column, by_ky, by_kz, out_re, out_im, out_a, out):
    lam, rank = eigenvalues(column, by_ky, by_kz)
    first = jnp.where(rank == 0, 1.0, 0.0).astype(jnp.float32)
    halves = [jnp.concatenate([got[32 * a + 16 * h : 32 * a + 16 * h + 16, :] for a in range(8)], 0) for h in range(2)]
    lines = times(jnp.concatenate(halves, 1), y)
    spectrum = applied(x, jnp.concatenate([lines[:, :256], lines[:, 256:]], 0))
    re, im = spectrum[:128], spectrum[128:]
    re, im = (
        jnp.concatenate([re[:, :128] + first * im[:, 128:], re[:, 128:]], 1),
        jnp.concatenate([im[:, :128] - first * re[:, 128:], im[:, 128:]], 1),
    )
    out_re[...] = re
    out_im[...] = im
    a = STEP * lam
    out_a[...] = a
    power = (re * re + im * im) * weights_of(rank) * a
    double = a * (4.0 / LARGEST) - 2.0
    moments = [power, 0.5 * double * power]
    while len(moments) < NODES:
        moments.append(double * moments[-1] - moments[-2])
    out[...] = jnp.broadcast_to(sums_on_lanes(moments), (256, 128))


def cycle_kernel(got, re_in, im_in, a_in, nodes, x_back, y_back, out):
    moments = jnp.sum(got[...], axis=0, keepdims=True)
    weight = dot(jnp.broadcast_to(moments, (8, 128)), nodes[0:128, :])[0:1]
    node = nodes[128:129, :]
    fine = a_in[...]
    first = jnp.where(own_rank() == 0, 1.0, 0.0).astype(jnp.float32)
    sides = [(node, 1.0 - node), (fine, 1.0 - fine)]
    scaled, potential = [1.0, 1.0], 0.0
    for cycle in range(3):
        a, mu = sides[0]
        low = weight * scaled[0] * scaled[0]
        products = [low * a, low * a * mu, low * a * mu * mu, -low * mu * mu, -low * mu * mu * mu]
        g0, g1 = solve([jnp.sum(p, axis=1, keepdims=True) for p in products])
        a, mu = sides[1]
        potential = potential + STEP * scaled[1] * (1.0 + mu * ((1.0 - g0) + (1.0 - g1) * mu))
        if cycle < 2:
            scaled = [s * mu * (mu * mu + a * (g0 + mu * g1)) for s, (a, mu) in zip(scaled, sides)]
    residual = JACOBI_SCALE * scaled[1] * mu * mu
    re, im = re_in[...], im_in[...]
    columns = []
    for multiplier in (potential, residual):
        fr, fi = multiplier * re, multiplier * im
        columns.append(
            jnp.concatenate([fr[:, :128] - first * fi[:, 128:], fi[:, :128] + first * fr[:, 128:]], 0)
        )
    planes = applied(x_back, jnp.concatenate(columns, 1))
    lines = []
    for f in range(2):
        for odd in range(2):
            at = 128 * odd
            pair = [planes[at + n : at + n + 64, 128 * f : 128 * f + 128] for n in (0, 64)]
            lines.append(jnp.concatenate(pair, 1))
    lines = times(jnp.concatenate(lines, 0), y_back)
    left = index_of((64, 128), 1) < 64
    for f in range(2):
        for b in range(4):
            side = slice(128 * (b // 2), 128 * (b // 2) + 128)
            even, odd = lines[128 * f : 128 * f + 64, side], lines[128 * f + 64 : 128 * f + 128, side]
            if b % 2 == 0:
                odd = pltpu.roll(odd, 64, 1)
            else:
                even = pltpu.roll(even, 64, 1)
            message = jnp.where(left, even, odd)
            for n in range(8):
                out[pl.ds((32 * n + 8 * b) * 2 + f, 8, stride=2), :] = message[8 * n : 8 * n + 8]


def back_kernel(got, z_tile_back, twiddle, z_even_back, z_odd_back, z_last_back, out, cells):
    spectra = [got[pl.ds(f, 256, stride=2), :] for f in range(2)]
    low = jnp.concatenate([v[:128] for v in spectra], 0)
    high = jnp.concatenate([v[128:] for v in spectra], 0)
    top = index_of((256, 128), 0) & 127 == 0
    part = (index_of((256, 128), 1) & 63) >> 4
    last = jnp.where(top & (part == 1), low, 0.0)
    low = jnp.where(top & (part < 2), jnp.where(part == 0, 0.5 * low, 0.0), low)
    last = times(jnp.concatenate([last[0:8], last[128:136]], 0), z_last_back)
    even, odd = times(low, z_even_back), times(high, z_odd_back)
    turned = []
    for f in range(2):
        e, o = even[128 * f : 128 * f + 128], odd[128 * f : 128 * f + 128]
        real = jnp.concatenate([e[0:8, :128] + last[8 * f : 8 * f + 8], e[8:, :128]], 0)
        re = jnp.concatenate([real + o[:, :128], real - o[:, :128]], 1)
        im = jnp.concatenate([e[:, 128:] + o[:, 128:], e[:, 128:] - o[:, 128:]], 1)
        turned.append(
            jnp.concatenate([re * twiddle[0] - im * twiddle[1], im * twiddle[0] + re * twiddle[1]], 0)
        )
    fields = applied(z_tile_back, jnp.concatenate(turned, 1))
    group = index_of((128, 128), 1) >> 5
    for side in range(2):
        one = fields[:, 128 * side : 128 * side + 128]
        two = fields[:, 256 + 128 * side : 384 + 128 * side]
        for n in range(4):
            lower = one if n == 0 else pltpu.roll(one, 128 - 32 * n, 1)
            upper = two if n == 1 else pltpu.roll(two, (160 - 32 * n) % 128, 1)
            cells[pl.ds(4 * side + n, 128, stride=8), :] = jnp.where(group == 0, lower, upper)
    for c in range(8):
        out[c] = jnp.transpose(cells[128 * c : 128 * c + 128, :])[0:64]


def place_kernel(got, potential, residual, done):
    copies = [
        pltpu.make_async_copy(got.at[:, f], out, done.at[f]) for f, out in enumerate((potential, residual))
    ]
    for copy in copies:
        copy.start()
    for copy in copies:
        copy.wait()


VMEM = pl.BlockSpec(memory_space=pltpu.VMEM)
HBM = pl.BlockSpec(memory_space=pltpu.HBM)


def call(kernel, out_shapes, specs, scratch=(), name=None, result=VMEM, limit=16):
    shapes = [jax.ShapeDtypeStruct(s, jnp.float32) for s in out_shapes]
    single = len(shapes) == 1
    return pl.pallas_call(
        kernel,
        out_shape=shapes[0] if single else shapes,
        in_specs=specs,
        out_specs=result if single else [result] * len(shapes),
        scratch_shapes=list(scratch),
        compiler_params=pltpu.CompilerParams(vmem_limit_bytes=limit * 1024 * 1024),
        name=name,
    )


def exchanged(array, axes):
    return lax.all_to_all(array, axes, 0, 0, tiled=True)


def per_device(density, atom_site, atom_charge, slot_atom, slot_tile, slot_shift):
    t = {name: jnp.asarray(value) for name, value in tables().items()}
    scratch = [
        pltpu.SMEM((3, 1, 16), jnp.float32),
        pltpu.SMEM((1, 16), jnp.float32),
        pltpu.VMEM((2, 32), jnp.int32),
        pltpu.VMEM((2, 32), jnp.int32),
        pltpu.VMEM((3, 2, 32), jnp.int32),
        pltpu.SemaphoreType.DMA((7,)),
    ]
    message = call(send_kernel, [(32, 16, 128)], [HBM] * 6, scratch, name="send", limit=63)(
        density,
        atom_site.reshape(3, 1, 16),
        atom_charge.reshape(1, 16),
        slot_atom.reshape(32, 2).T,
        slot_tile.reshape(32, 2).T,
        jnp.swapaxes(slot_shift.reshape(3, 32, 2), 1, 2),
    )
    got = exchanged(message, ("gy", "gz"))
    cells = [pltpu.VMEM((1024, 128), jnp.float32)]
    message = call(line_kernel, [(256, 128)], [VMEM] * 6, cells, "line")(
        got, t["order"], t["z_tile"], t["twiddle"], t["z_even"], t["z_odd"]
    )
    got = exchanged(message, AXES)
    re, im, a, message = call(plane_kernel, [(128, 256)] * 3 + [(256, 128)], [VMEM] * 6, name="plane")(
        got, t["y"], t["x"], t["column"], t["by_ky"], t["by_kz"]
    )
    got = exchanged(message, AXES)
    message = call(cycle_kernel, [(512, 128)], [VMEM] * 7, name="cycle")(
        got, re, im, a, t["nodes"], t["x_back"], t["y_back"]
    )
    got = exchanged(message.reshape(256, 2, 128), AXES).reshape(512, 128)
    message = call(back_kernel, [(8, 64, 128)], [VMEM] * 6, cells, "back")(
        got, t["z_tile_back"], t["twiddle"], t["z_even_back"], t["z_odd_back"], t["z_last_back"]
    )
    got = exchanged(message, "gz").reshape(8, 2, 2, 16, 128)
    place = call(place_kernel, [(8, 2, 16, 128)] * 2, [VMEM], [pltpu.SemaphoreType.DMA((2,))], "place", HBM)
    return tuple(out.reshape(16, 16, 128) for out in place(got))


def solution(mesh):
    return jax.shard_map(
        per_device,
        mesh=mesh,
        in_specs=(
            P("gx", "gy", "gz"),
            P(None, "gx", "gy", "gz", None),
            P("gx", "gy", "gz", None),
            P("gx", "gy", "gz", None, None),
            P("gx", "gy", "gz", None, None),
            P(None, "gx", "gy", "gz", None, None),
        ),
        out_specs=(P("gx", "gy", "gz"), P("gx", "gy", "gz")),
        check_vma=False,
    )
```

```python
import functools

import jax
import jax.numpy as jnp
import ml_dtypes
import numpy as np
from jax import lax
from jax.experimental import pallas as pl
from jax.experimental.pallas import tpu as pltpu
from jax.sharding import PartitionSpec as P


METRIC = np.array([[3.24, 0.972, 0.648], [0.972, 3.2157, 0.9639], [0.648, 0.9639, 2.9565]])
INVERSE = np.array(
    [
        [0.3450043297, -0.0904572938, -0.0461258313],
        [-0.0904572938, 0.3683733435, -0.1002735462],
        [-0.0461258313, -0.1002735462, 0.3810394757],
    ]
)
FIRST_WEIGHTS = np.array([6.0 / 7.0, -15.0 / 56.0, 5.0 / 63.0, -1.0 / 56.0, 2.0 / 385.0, -1.0 / 5544.0])
SECOND_WEIGHTS = 2.0 * FIRST_WEIGHTS / np.arange(1, 7)
CENTER_WEIGHT = -2.0 * SECOND_WEIGHTS.sum()
JACOBI_SCALE = float(-CENTER_WEIGHT * np.trace(INVERSE))
STEP = 0.3
WIDTH_SQUARED = 9.0
RIDGE_SHARE = 0.01
NX, NY, NZ = 128, 64, 1024
AXES = ("gx", "gy", "gz")
HI = lax.Precision.HIGHEST
LOG2E = float(np.log2(np.e))
NODES = 16
LARGEST = STEP * 2.3721


def cos_sin(n, rows, columns):
    angle = 2.0 * np.pi * (np.outer(rows, columns) % n) / n
    return np.cos(angle), np.sin(angle)


def first_symbol(n):
    angle = 2.0 * np.pi * np.arange(n) / n
    return 2.0 * sum(w * np.sin((o + 1) * angle) for o, w in enumerate(FIRST_WEIGHTS))


def second_symbol(n):
    angle = 2.0 * np.pi * np.arange(n) / n
    return CENTER_WEIGHT + 2.0 * sum(w * np.cos((o + 1) * angle) for o, w in enumerate(SECOND_WEIGHTS))


def halves_of(table):
    high = table.astype(ml_dtypes.bfloat16)
    return high, (table - high.astype(np.float64)).astype(ml_dtypes.bfloat16)


ON_THE_RIGHT = ("z_even", "z_odd", "y", "y_back", "z_even_back", "z_odd_back", "z_last_back")
ON_THE_LEFT = ("z_tile", "x", "x_back", "z_tile_back")


@functools.lru_cache(maxsize=None)
def tables():
    eye = np.eye(32)
    freq = np.arange(128)
    c, s = cos_sin(128, freq, freq)
    t = {}
    t["z_tile"] = np.concatenate([c, -s], 0) / 32.0 / JACOBI_SCALE
    t["z_tile_back"] = np.concatenate([c, -s], 1) / 32.0
    t["twiddle"] = np.stack(cos_sin(1024, freq, np.arange(256) // 32))
    c, s = cos_sin(8, np.arange(4), np.arange(4))
    half_eye = np.eye(16)
    for odd, name in enumerate(("z_even", "z_odd")):
        ahead = np.zeros((2, 4, 32, 2, 2, 32))
        back = np.zeros((2, 2, 2, 16, 2, 4, 2, 16))
        for k in range(4):
            for n in range(2):
                cc, ss = c[k, 2 * n + odd], s[k, 2 * n + odd]
                ahead[0, k, :, n, 0], ahead[1, k, :, n, 0] = cc * eye, ss * eye
                ahead[0, k, :, n, 1], ahead[1, k, :, n, 1] = -ss * eye, cc * eye
                for x in range(2):
                    back[x, n, 0, :, 0, k, x], back[x, n, 1, :, 0, k, x] = 2.0 * cc * half_eye, -2.0 * ss * half_eye
                    back[x, n, 0, :, 1, k, x], back[x, n, 1, :, 1, k, x] = 2.0 * ss * half_eye, 2.0 * cc * half_eye
        t[name], t[name + "_back"] = ahead.reshape(256, 128), back.reshape(128, 256)
    last = np.zeros((2, 2, 2, 16, 4, 2, 16))
    for k in range(4):
        for x in range(2):
            last[x, 0, 1, :, k, x] = (-1.0) ** k * half_eye
    t["z_last_back"] = last.reshape(128, 128)
    half, b, j = np.meshgrid(np.arange(2), np.arange(4), np.arange(8), indexing="ij")
    c, s = cos_sin(64, (16 * b + 8 * half + j).reshape(-1), np.arange(64))
    c, s = c.reshape(2, 4, 8, 64) / 8.0, s.reshape(2, 4, 8, 64) / 8.0
    ahead = np.zeros((2, 2, 2, 4, 8, 2, 4, 64))
    for f in range(2):
        ahead[:, f, 0, :, :, 0, f], ahead[:, f, 1, :, :, 0, f] = c, s
        ahead[:, f, 0, :, :, 1, f], ahead[:, f, 1, :, :, 1, f] = -s, c
    ahead[:, 0, 1, :, :, 0, 2], ahead[:, 0, 1, :, :, 1, 2] = c, -s
    t["y"] = ahead.reshape(256, 512)
    c, s = cos_sin(64, np.arange(64), np.arange(64))
    c, s = c.reshape(64, 4, 16) / 8.0, s.reshape(64, 4, 16) / 8.0
    back = np.zeros((2, 2, 64, 4, 2, 2, 16))
    for f in range(2):
        back[0, f, :, :, f, 0], back[1, f, :, :, f, 0] = c, -s
        back[0, f, :, :, f, 1], back[1, f, :, :, f, 1] = s, c
    t["y_back"] = back.reshape(256, 256)
    c, s = cos_sin(128, freq, freq)
    t["x"] = np.block([[c, s], [-s, c]]) / np.sqrt(128.0)
    back = np.block([[c, -s], [s, c]]) / np.sqrt(128.0)
    t["x_back"] = back.reshape(2, 64, 2, 256).transpose(2, 0, 1, 3).reshape(256, 256)
    d1x, d1y, d1z = first_symbol(NX), first_symbol(NY), first_symbol(NZ)
    d2x, d2y, d2z = second_symbol(NX), second_symbol(NY), second_symbol(NZ)
    column = np.zeros((128, 128))
    column[:, 0], column[:, 1] = -INVERSE[0, 0] * d2x / JACOBI_SCALE, d1x
    by_ky = np.zeros((8, 256))
    by_ky[0] = np.tile(-INVERSE[1, 1] * d2y / JACOBI_SCALE, 4)
    by_ky[1] = np.tile(2.0 * INVERSE[1, 2] * d1y / JACOBI_SCALE, 4)
    by_ky[2] = np.tile(2.0 * INVERSE[0, 1] * d1y / JACOBI_SCALE, 4)
    by_kz = np.zeros((256, 128))
    low = np.arange(256)
    for f, kz in enumerate((low, low + 256, 0 * low + 512)):
        by_kz[:, 2 * f], by_kz[:, 2 * f + 1] = -INVERSE[2, 2] * d2z[kz] / JACOBI_SCALE, d1z[kz]
    t["column"], t["by_ky"], t["by_kz"] = column, by_ky, by_kz
    angle = (np.arange(NODES) + 0.5) * np.pi / NODES
    nodes = np.zeros((136, 128))
    nodes[:NODES, :NODES] = 2.0 / NODES * np.cos(np.outer(np.arange(NODES), angle))
    nodes[0, :NODES] = 1.0 / NODES
    nodes[128, :NODES] = 0.5 * LARGEST * (1.0 + np.cos(angle))
    t["nodes"] = nodes
    for name in ON_THE_RIGHT:
        high, low = halves_of(t[name])
        t[name] = np.concatenate([high, low], 0)
    for name in ON_THE_LEFT:
        high, low = halves_of(t[name])
        t[name] = np.concatenate([high, low], 1)
    return {n: v if v.dtype == ml_dtypes.bfloat16 else v.astype(np.float32) for n, v in t.items()}


def dot(a, b, contract=((1,), (0,))):
    return lax.dot_general(a, b, (contract, ((), ())), precision=HI, preferred_element_type=jnp.float32)


def index_of(shape, dim):
    return lax.broadcasted_iota(jnp.int32, shape, dim)


def solve(gram):
    ff, fc, cc, fs, cs = gram
    ridge = RIDGE_SHARE * 0.5 * (ff + cc)
    ff, cc = ff + ridge, cc + ridge
    determinant = ff * cc - fc * fc
    return (cc * fs - fc * cs) / determinant, (ff * cs - fc * fs) / determinant


def stack_rows(rows, count):
    at = index_of((count, 128), 0)
    stacked = jnp.zeros((count, 128), jnp.float32)
    for n, row in enumerate(rows):
        stacked = jnp.where(at == n, row, stacked)
    return stacked


def sums_on_lanes(arrays):
    rows = []
    for array in arrays:
        row = jnp.sum(array, axis=0, keepdims=True)
        rows.append(row[:, :128] + row[:, 128:])
    count = -(-len(rows) // 8) * 8
    totals = jnp.sum(stack_rows(rows, count), axis=1, keepdims=True)
    mine = index_of((count, 128), 0) == index_of((count, 128), 1)
    return jnp.sum(jnp.where(mine, totals, 0.0), axis=0, keepdims=True)


def in_three(array):
    high = array.astype(jnp.bfloat16)
    rest = array - high.astype(jnp.float32)
    middle = rest.astype(jnp.bfloat16)
    return high, middle, (rest - middle.astype(jnp.float32)).astype(jnp.bfloat16)


def exact_dot(a, b, contract=((1,), (0,))):
    return lax.dot_general(a, b, (contract, ((), ())), preferred_element_type=jnp.float32)


def in_two(array, axis):
    high = array.astype(jnp.bfloat16)
    low = (array - high.astype(jnp.float32)).astype(jnp.bfloat16)
    return jnp.concatenate([high, high, low], axis)


def times(data, table):
    return exact_dot(in_two(data, 1), jnp.concatenate([table[...], table[0 : table.shape[0] // 2, :]], 0))


def applied(table, data):
    return exact_dot(jnp.concatenate([table[...], table[:, 0 : table.shape[1] // 2]], 1), in_two(data, 0))


def blank_kernel(out):
    out[...] = jnp.zeros((8, 128), jnp.float32)


def slots_kernel(blank, site, charge, atom, tile, shift, out):
    values = [jnp.zeros((2, 32), jnp.float32) for _ in range(4)]
    for n in range(16):
        hit = atom[...] == n
        for p in range(3):
            values[p] = jnp.where(hit, site[p, :, n : n + 1], values[p])
        values[3] = jnp.where(hit, charge[:, n : n + 1], values[3])
    for p in range(3):
        values[p] = values[p] + 4.0 * shift[p].astype(jnp.float32)
    code = tile[...]
    values.append(((code & 15) + 16 * (index_of((2, 32), 1) & 7)).astype(jnp.float32))
    values.append((code >> 4).astype(jnp.float32))
    lane = index_of((8, 128), 1)
    packed = blank[...]
    for e in range(2):
        rows = [jnp.concatenate([v[e : e + 1], jnp.zeros((1, 96), jnp.float32)], 1) for v in values]
        rows = stack_rows(rows, 8)
        for b in range(4):
            moved = pltpu.roll(rows, 8 * b + 8 * e, 1)
            packed = jnp.where((lane >> 3) == 2 * b + e, moved, packed)
    out[...] = packed


def send_kernel(density, packed, out):
    for half in range(2):
        out[16 * half : 16 * half + 16, 0:8, :] = density[:, 8 * half : 8 * half + 8, :]
    out[:, 8:16, :] = jnp.broadcast_to(packed[...][None], (32, 8, 128))


def line_kernel(got, z_tile, twiddle, z_even, z_odd, out, cells):
    rank = lax.axis_index("gy") * 8 + lax.axis_index("gz")
    x, half = rank & 15, rank >> 4
    own = ((x >> 3) * 2 + half).astype(jnp.float32)
    along = (x & 7).astype(jnp.float32)
    lane = index_of((8, 128), 1)
    at_j = index_of((8, 512), 0).astype(jnp.float32) - 3.5
    tile_at = index_of((128, 512), 0).astype(jnp.float32)
    scale = -LOG2E / WIDTH_SQUARED
    charge = []
    for b in range(4):
        parts = []
        for g in range(4):
            part = jnp.zeros((8, 128), jnp.float32)
            for r in range(8):
                moved = got[8 * g + r, 8:16, :]
                if r != b:
                    moved = pltpu.roll(moved, (16 * (r - b)) % 128, 1)
                part = jnp.where((lane >> 4) == r, moved, part)
            parts.append(part)
        slots = jnp.concatenate(parts, 1)
        ex = along - slots[0:1]
        vy, vz = slots[1:2] - 3.5, slots[2:3] - 3.5
        m = METRIC
        fixed = m[0, 0] * ex * ex + m[1, 1] * vy * vy + m[2, 2] * vz * vz
        fixed = fixed - 2.0 * m[0, 1] * ex * vy - 2.0 * m[0, 2] * ex * vz + 2.0 * m[1, 2] * vy * vz
        by_j = -2.0 * m[1, 1] * vy + 2.0 * m[0, 1] * ex - 2.0 * m[1, 2] * vz
        by_k = -2.0 * m[2, 2] * vz + 2.0 * m[0, 2] * ex - 2.0 * m[1, 2] * vy
        exponents = []
        for k in range(8):
            at_k = k - 3.5
            row = scale * (fixed + at_k * by_k + m[2, 2] * at_k * at_k)
            exponents.append(row + at_j * (scale * by_j + 2.0 * scale * m[1, 2] * at_k + scale * m[1, 1] * at_j))
        blocks = jnp.exp2(jnp.concatenate(exponents, 0))
        peak = jnp.where(slots[5:6] == own, slots[3:4], 0.0)
        placed = jnp.where(slots[4:5] == tile_at, 1.0, 0.0).astype(jnp.bfloat16)
        parts = jnp.concatenate(in_three(blocks * peak), 0)
        sums = exact_dot(parts, placed, ((1,), (1,)))
        charge.append(sums[0:64] + sums[64:128] + sums[128:192])
    charge = [charge[b][8 * k : 8 * k + 8] for k in range(8) for b in range(4)]
    charge = [jnp.transpose(jnp.concatenate(charge[16 * n : 16 * n + 16], 0)) for n in range(2)]
    charge = jnp.concatenate(charge, 1)
    for c in range(8):
        piece = jnp.concatenate([got[8 * b + c, 0:8, :] for b in range(4)], 0)
        cells[128 * c : 128 * c + 128, :] = jnp.transpose(jnp.concatenate([piece] * 4, 0))
    group = index_of((128, 128), 1) >> 5
    sides = []
    for side in range(2):
        total = jnp.zeros((128, 128), jnp.float32)
        for n in range(4):
            total = jnp.where(group == n, cells[pl.ds(4 * side + n, 128, stride=8), :], total)
        sides.append(total)
    field = jnp.concatenate(sides, 1) + charge
    spectrum = applied(z_tile, field)
    re, im = spectrum[:128], spectrum[128:]
    re, im = re * twiddle[0] + im * twiddle[1], im * twiddle[0] - re * twiddle[1]
    even = jnp.concatenate([re[:, :128] + re[:, 128:], im[:, :128] + im[:, 128:]], 1)
    odd = jnp.concatenate([re[:, :128] - re[:, 128:], im[:, :128] - im[:, 128:]], 1)
    out[0:128, :] = times(even, z_even)
    out[128:256, :] = times(odd, z_odd)
    last = jnp.where((lane >> 5) & 1 == 0, even[0:8, 0:128], -even[0:8, 0:128])
    last = last + pltpu.roll(last, 64, 1)
    last = last + pltpu.roll(last, 32, 1)
    here = (index_of((8, 128), 0) == 0) & ((lane >> 5) == 1)
    out[0:8, :] = jnp.where(here, last, out[0:8, :])


def own_rank():
    return (lax.axis_index("gx") * 4 + lax.axis_index("gy")) * 8 + lax.axis_index("gz")


def eigenvalues(column, by_ky, by_kz):
    rank = own_rank()
    mine = by_kz[pl.ds(rank, 1), :]
    field = index_of((1, 256), 1) >> 6
    second, first = [
        jnp.where(field == 0, mine[:, n : n + 1], jnp.where(field == 1, mine[:, n + 2 : n + 3], mine[:, n + 4 : n + 5]))
        for n in range(2)
    ]
    row = by_ky[0:1, :] + second + by_ky[1:2, :] * first
    other = by_ky[2:3, :] + (2.0 * INVERSE[0, 2] / JACOBI_SCALE) * first
    return column[:, 0:1] + row + column[:, 1:2] * other, rank


def weights_of(rank):
    field = index_of((1, 256), 1) >> 6
    first = jnp.where(field == 1, 2.0, jnp.where(field == 3, 0.0, 1.0))
    other = jnp.where(field < 2, 2.0, 0.0)
    return jnp.where(rank == 0, first, other)


def plane_kernel(got, y, x, column, by_ky, by_kz, out_re, out_im, out_a, out):
    lam, rank = eigenvalues(column, by_ky, by_kz)
    first = jnp.where(rank == 0, 1.0, 0.0).astype(jnp.float32)
    halves = [jnp.concatenate([got[32 * a + 16 * h : 32 * a + 16 * h + 16, :] for a in range(8)], 0) for h in range(2)]
    lines = times(jnp.concatenate(halves, 1), y)
    spectrum = applied(x, jnp.concatenate([lines[:, :256], lines[:, 256:]], 0))
    re, im = spectrum[:128], spectrum[128:]
    re, im = (
        jnp.concatenate([re[:, :128] + first * im[:, 128:], re[:, 128:]], 1),
        jnp.concatenate([im[:, :128] - first * re[:, 128:], im[:, 128:]], 1),
    )
    out_re[...] = re
    out_im[...] = im
    a = STEP * lam
    out_a[...] = a
    power = (re * re + im * im) * weights_of(rank) * a
    double = a * (4.0 / LARGEST) - 2.0
    moments = [power, 0.5 * double * power]
    while len(moments) < NODES:
        moments.append(double * moments[-1] - moments[-2])
    out[...] = jnp.broadcast_to(sums_on_lanes(moments), (256, 128))


def cycle_kernel(got, re_in, im_in, a_in, nodes, x_back, y_back, out):
    moments = jnp.sum(got[...], axis=0, keepdims=True)
    weight = dot(jnp.broadcast_to(moments, (8, 128)), nodes[0:128, :])[0:1]
    node = nodes[128:129, :]
    fine = a_in[...]
    first = jnp.where(own_rank() == 0, 1.0, 0.0).astype(jnp.float32)
    sides = [(node, 1.0 - node), (fine, 1.0 - fine)]
    scaled, potential = [1.0, 1.0], 0.0
    for cycle in range(3):
        a, mu = sides[0]
        low = weight * scaled[0] * scaled[0]
        products = [low * a, low * a * mu, low * a * mu * mu, -low * mu * mu, -low * mu * mu * mu]
        g0, g1 = solve([jnp.sum(p, axis=1, keepdims=True) for p in products])
        a, mu = sides[1]
        potential = potential + STEP * scaled[1] * (1.0 + mu * ((1.0 - g0) + (1.0 - g1) * mu))
        if cycle < 2:
            scaled = [s * mu * (mu * mu + a * (g0 + mu * g1)) for s, (a, mu) in zip(scaled, sides)]
    residual = JACOBI_SCALE * scaled[1] * mu * mu
    re, im = re_in[...], im_in[...]
    columns = []
    for multiplier in (potential, residual):
        fr, fi = multiplier * re, multiplier * im
        columns.append(
            jnp.concatenate([fr[:, :128] - first * fi[:, 128:], fi[:, :128] + first * fr[:, 128:]], 0)
        )
    planes = applied(x_back, jnp.concatenate(columns, 1))
    lines = []
    for f in range(2):
        for odd in range(2):
            at = 128 * odd
            pair = [planes[at + n : at + n + 64, 128 * f : 128 * f + 128] for n in (0, 64)]
            lines.append(jnp.concatenate(pair, 1))
    lines = times(jnp.concatenate(lines, 0), y_back)
    left = index_of((64, 128), 1) < 64
    for f in range(2):
        for b in range(4):
            side = slice(128 * (b // 2), 128 * (b // 2) + 128)
            even, odd = lines[128 * f : 128 * f + 64, side], lines[128 * f + 64 : 128 * f + 128, side]
            if b % 2 == 0:
                odd = pltpu.roll(odd, 64, 1)
            else:
                even = pltpu.roll(even, 64, 1)
            message = jnp.where(left, even, odd)
            for n in range(8):
                out[pl.ds((32 * n + 8 * b) * 2 + f, 8, stride=2), :] = message[8 * n : 8 * n + 8]


def back_kernel(got, z_tile_back, twiddle, z_even_back, z_odd_back, z_last_back, out, cells):
    spectra = [got[pl.ds(f, 256, stride=2), :] for f in range(2)]
    low = jnp.concatenate([v[:128] for v in spectra], 0)
    high = jnp.concatenate([v[128:] for v in spectra], 0)
    top = index_of((256, 128), 0) & 127 == 0
    part = (index_of((256, 128), 1) & 63) >> 4
    last = jnp.where(top & (part == 1), low, 0.0)
    low = jnp.where(top & (part < 2), jnp.where(part == 0, 0.5 * low, 0.0), low)
    last = times(jnp.concatenate([last[0:8], last[128:136]], 0), z_last_back)
    even, odd = times(low, z_even_back), times(high, z_odd_back)
    turned = []
    for f in range(2):
        e, o = even[128 * f : 128 * f + 128], odd[128 * f : 128 * f + 128]
        real = jnp.concatenate([e[0:8, :128] + last[8 * f : 8 * f + 8], e[8:, :128]], 0)
        re = jnp.concatenate([real + o[:, :128], real - o[:, :128]], 1)
        im = jnp.concatenate([e[:, 128:] + o[:, 128:], e[:, 128:] - o[:, 128:]], 1)
        turned.append(
            jnp.concatenate([re * twiddle[0] - im * twiddle[1], im * twiddle[0] + re * twiddle[1]], 0)
        )
    fields = applied(z_tile_back, jnp.concatenate(turned, 1))
    group = index_of((128, 128), 1) >> 5
    for side in range(2):
        one = fields[:, 128 * side : 128 * side + 128]
        two = fields[:, 256 + 128 * side : 384 + 128 * side]
        for n in range(4):
            lower = one if n == 0 else pltpu.roll(one, 128 - 32 * n, 1)
            upper = two if n == 1 else pltpu.roll(two, (160 - 32 * n) % 128, 1)
            cells[pl.ds(4 * side + n, 128, stride=8), :] = jnp.where(group == 0, lower, upper)
    for c in range(8):
        out[c] = jnp.transpose(cells[128 * c : 128 * c + 128, :])[0:64]


def place_kernel(got, potential, residual, done):
    copies = [
        pltpu.make_async_copy(got.at[:, f], out, done.at[f]) for f, out in enumerate((potential, residual))
    ]
    for copy in copies:
        copy.start()
    for copy in copies:
        copy.wait()


VMEM = pl.BlockSpec(memory_space=pltpu.VMEM)
HBM = pl.BlockSpec(memory_space=pltpu.HBM)
SMEM = pl.BlockSpec(memory_space=pltpu.SMEM)


def call(kernel, out_shapes, specs, scratch=(), name=None, result=VMEM, limit=16, cost=None):
    shapes = [jax.ShapeDtypeStruct(s, jnp.float32) for s in out_shapes]
    single = len(shapes) == 1
    return pl.pallas_call(
        kernel,
        out_shape=shapes[0] if single else shapes,
        in_specs=specs,
        out_specs=result if single else [result] * len(shapes),
        scratch_shapes=list(scratch),
        compiler_params=pltpu.CompilerParams(vmem_limit_bytes=limit * 1024 * 1024),
        name=name,
        cost_estimate=cost and pl.CostEstimate(flops=cost, bytes_accessed=cost, transcendentals=0),
    )


def exchanged(array, axes):
    return lax.all_to_all(array, axes, 0, 0, tiled=True)


def per_device(density, atom_site, atom_charge, slot_atom, slot_tile, slot_shift):
    t = {name: jnp.asarray(value) for name, value in tables().items()}
    packed = call(slots_kernel, [(8, 128)], [VMEM] * 6, name="slots")(
        call(blank_kernel, [(8, 128)], [], name="blank", cost=10**8)(),
        atom_site.reshape(3, 1, 16),
        atom_charge.reshape(1, 16),
        slot_atom.reshape(32, 2).T,
        slot_tile.reshape(32, 2).T,
        jnp.swapaxes(slot_shift.reshape(3, 32, 2), 1, 2),
    )
    message = call(send_kernel, [(32, 16, 128)], [VMEM] * 2, name="send")(density, packed)
    got = exchanged(message, ("gy", "gz"))
    cells = [pltpu.VMEM((1024, 128), jnp.float32)]
    message = call(line_kernel, [(256, 128)], [VMEM] * 5, cells, "line")(
        got, t["z_tile"], t["twiddle"], t["z_even"], t["z_odd"]
    )
    got = exchanged(message, AXES)
    re, im, a, message = call(plane_kernel, [(128, 256)] * 3 + [(256, 128)], [VMEM] * 6, name="plane")(
        got, t["y"], t["x"], t["column"], t["by_ky"], t["by_kz"]
    )
    got = exchanged(message, AXES)
    message = call(cycle_kernel, [(512, 128)], [VMEM] * 7, name="cycle")(
        got, re, im, a, t["nodes"], t["x_back"], t["y_back"]
    )
    got = exchanged(message.reshape(256, 2, 128), AXES).reshape(512, 128)
    message = call(back_kernel, [(8, 64, 128)], [VMEM] * 6, cells, "back")(
        got, t["z_tile_back"], t["twiddle"], t["z_even_back"], t["z_odd_back"], t["z_last_back"]
    )
    got = exchanged(message, "gz").reshape(8, 2, 2, 16, 128)
    place = call(place_kernel, [(8, 2, 16, 128)] * 2, [VMEM], [pltpu.SemaphoreType.DMA((2,))], "place", HBM)
    return tuple(out.reshape(16, 16, 128) for out in place(got))


def solution(mesh):
    return jax.shard_map(
        per_device,
        mesh=mesh,
        in_specs=(
            P("gx", "gy", "gz"),
            P(None, "gx", "gy", "gz", None),
            P("gx", "gy", "gz", None),
            P("gx", "gy", "gz", None, None),
            P("gx", "gy", "gz", None, None),
            P(None, "gx", "gy", "gz", None, None),
        ),
        out_specs=(P("gx", "gy", "gz"), P("gx", "gy", "gz")),
        check_vma=False,
    )
```

```python
import functools

import jax
import jax.numpy as jnp
import ml_dtypes
import numpy as np
from jax import lax
from jax.experimental import pallas as pl
from jax.experimental.pallas import tpu as pltpu
from jax.sharding import PartitionSpec as P


METRIC = np.array([[3.24, 0.972, 0.648], [0.972, 3.2157, 0.9639], [0.648, 0.9639, 2.9565]])
INVERSE = np.array(
    [
        [0.3450043297, -0.0904572938, -0.0461258313],
        [-0.0904572938, 0.3683733435, -0.1002735462],
        [-0.0461258313, -0.1002735462, 0.3810394757],
    ]
)
FIRST_WEIGHTS = np.array([6.0 / 7.0, -15.0 / 56.0, 5.0 / 63.0, -1.0 / 56.0, 2.0 / 385.0, -1.0 / 5544.0])
SECOND_WEIGHTS = 2.0 * FIRST_WEIGHTS / np.arange(1, 7)
CENTER_WEIGHT = -2.0 * SECOND_WEIGHTS.sum()
JACOBI_SCALE = float(-CENTER_WEIGHT * np.trace(INVERSE))
STEP = 0.3
WIDTH_SQUARED = 9.0
RIDGE_SHARE = 0.01
NX, NY, NZ = 128, 64, 1024
AXES = ("gx", "gy", "gz")
HI = lax.Precision.HIGHEST
LOG2E = float(np.log2(np.e))
NODES = 16
LARGEST = STEP * 2.3721


def cos_sin(n, rows, columns):
    angle = 2.0 * np.pi * (np.outer(rows, columns) % n) / n
    return np.cos(angle), np.sin(angle)


def first_symbol(n):
    angle = 2.0 * np.pi * np.arange(n) / n
    return 2.0 * sum(w * np.sin((o + 1) * angle) for o, w in enumerate(FIRST_WEIGHTS))


def second_symbol(n):
    angle = 2.0 * np.pi * np.arange(n) / n
    return CENTER_WEIGHT + 2.0 * sum(w * np.cos((o + 1) * angle) for o, w in enumerate(SECOND_WEIGHTS))


def halves_of(table):
    high = table.astype(ml_dtypes.bfloat16)
    return high, (table - high.astype(np.float64)).astype(ml_dtypes.bfloat16)


ON_THE_RIGHT = ("z_even", "z_odd", "y", "y_back", "z_even_back", "z_odd_back", "z_last_back")
ON_THE_LEFT = ("z_tile", "x_even", "x_odd", "x_even_back", "x_odd_back", "z_tile_back")


@functools.lru_cache(maxsize=None)
def tables():
    eye = np.eye(32)
    freq = np.arange(128)
    c, s = cos_sin(128, freq, freq)
    t = {}
    t["z_tile"] = np.concatenate([c, -s], 0) / 32.0 / JACOBI_SCALE
    t["z_tile_back"] = np.concatenate([c, -s], 1) / 32.0
    t["twiddle"] = np.stack(cos_sin(1024, freq, np.arange(256) // 32))
    c, s = cos_sin(8, np.arange(4), np.arange(4))
    half_eye = np.eye(16)
    for odd, name in enumerate(("z_even", "z_odd")):
        ahead = np.zeros((2, 4, 32, 2, 2, 32))
        back = np.zeros((2, 2, 2, 16, 2, 4, 2, 16))
        for k in range(4):
            for n in range(2):
                cc, ss = c[k, 2 * n + odd], s[k, 2 * n + odd]
                ahead[0, k, :, n, 0], ahead[1, k, :, n, 0] = cc * eye, ss * eye
                ahead[0, k, :, n, 1], ahead[1, k, :, n, 1] = -ss * eye, cc * eye
                for x in range(2):
                    back[x, n, 0, :, 0, k, x], back[x, n, 1, :, 0, k, x] = 2.0 * cc * half_eye, -2.0 * ss * half_eye
                    back[x, n, 0, :, 1, k, x], back[x, n, 1, :, 1, k, x] = 2.0 * ss * half_eye, 2.0 * cc * half_eye
        t[name], t[name + "_back"] = ahead.reshape(256, 128), back.reshape(128, 256)
    last = np.zeros((2, 2, 2, 16, 4, 2, 16))
    for k in range(4):
        for x in range(2):
            last[x, 0, 1, :, k, x] = (-1.0) ** k * half_eye
    t["z_last_back"] = last.reshape(128, 128)
    half, b, j = np.meshgrid(np.arange(2), np.arange(4), np.arange(8), indexing="ij")
    c, s = cos_sin(64, (16 * b + 8 * half + j).reshape(-1), np.arange(64))
    c, s = c.reshape(2, 4, 8, 64) / 8.0, s.reshape(2, 4, 8, 64) / 8.0
    ahead = np.zeros((2, 2, 2, 4, 8, 2, 4, 64))
    for f in range(2):
        ahead[:, f, 0, :, :, 0, f], ahead[:, f, 1, :, :, 0, f] = c, s
        ahead[:, f, 0, :, :, 1, f], ahead[:, f, 1, :, :, 1, f] = -s, c
    ahead[:, 0, 1, :, :, 0, 2], ahead[:, 0, 1, :, :, 1, 2] = c, -s
    t["y"] = ahead.reshape(256, 512)
    c, s = cos_sin(64, np.arange(64), np.arange(64))
    c, s = c.reshape(64, 4, 16) / 8.0, s.reshape(64, 4, 16) / 8.0
    back = np.zeros((2, 2, 64, 4, 2, 2, 16))
    for f in range(2):
        back[0, f, :, :, f, 0], back[1, f, :, :, f, 0] = c, -s
        back[0, f, :, :, f, 1], back[1, f, :, :, f, 1] = s, c
    t["y_back"] = back.reshape(256, 256)
    short = np.arange(64)
    some = np.concatenate([2 * short[:32], 2 * short[:32] + 1])
    for odd, name in enumerate(("x_even", "x_odd")):
        c, s = cos_sin(128, 2 * short + odd, short)
        t[name] = np.block([[c, s], [-s, c]]) / np.sqrt(128.0)
        c, s = cos_sin(128, 2 * short + odd, some)
        t[name + "_back"] = np.block([[c, -s], [s, c]]) / np.sqrt(128.0)
    d1x, d1y, d1z = first_symbol(NX), first_symbol(NY), first_symbol(NZ)
    d2x, d2y, d2z = second_symbol(NX), second_symbol(NY), second_symbol(NZ)
    column = np.zeros((128, 128))
    by_row = np.concatenate([2 * short, 2 * short + 1])
    column[:, 0], column[:, 1] = -INVERSE[0, 0] * d2x[by_row] / JACOBI_SCALE, d1x[by_row]
    by_ky = np.zeros((8, 256))
    by_ky[0] = np.tile(-INVERSE[1, 1] * d2y / JACOBI_SCALE, 4)
    by_ky[1] = np.tile(2.0 * INVERSE[1, 2] * d1y / JACOBI_SCALE, 4)
    by_ky[2] = np.tile(2.0 * INVERSE[0, 1] * d1y / JACOBI_SCALE, 4)
    by_kz = np.zeros((256, 128))
    low = np.arange(256)
    for f, kz in enumerate((low, low + 256, 0 * low + 512)):
        by_kz[:, 2 * f], by_kz[:, 2 * f + 1] = -INVERSE[2, 2] * d2z[kz] / JACOBI_SCALE, d1z[kz]
    t["column"], t["by_ky"], t["by_kz"] = column, by_ky, by_kz
    angle = (np.arange(NODES) + 0.5) * np.pi / NODES
    nodes = np.zeros((136, 128))
    nodes[:NODES, :NODES] = 2.0 / NODES * np.cos(np.outer(np.arange(NODES), angle))
    nodes[0, :NODES] = 1.0 / NODES
    nodes[128, :NODES] = 0.5 * LARGEST * (1.0 + np.cos(angle))
    t["nodes"] = nodes
    for name in ON_THE_RIGHT:
        high, low = halves_of(t[name])
        t[name] = np.concatenate([high, low], 0)
    for name in ON_THE_LEFT:
        high, low = halves_of(t[name])
        t[name] = np.concatenate([high, low], 1)
    return {n: v if v.dtype == ml_dtypes.bfloat16 else v.astype(np.float32) for n, v in t.items()}


def dot(a, b, contract=((1,), (0,))):
    return lax.dot_general(a, b, (contract, ((), ())), precision=HI, preferred_element_type=jnp.float32)


def index_of(shape, dim):
    return lax.broadcasted_iota(jnp.int32, shape, dim)


def solve(gram):
    ff, fc, cc, fs, cs = gram
    ridge = RIDGE_SHARE * 0.5 * (ff + cc)
    ff, cc = ff + ridge, cc + ridge
    determinant = ff * cc - fc * fc
    return (cc * fs - fc * cs) / determinant, (ff * cs - fc * fs) / determinant


def stack_rows(rows, count):
    at = index_of((count, 128), 0)
    stacked = jnp.zeros((count, 128), jnp.float32)
    for n, row in enumerate(rows):
        stacked = jnp.where(at == n, row, stacked)
    return stacked


def sums_on_lanes(arrays):
    rows = []
    for array in arrays:
        row = jnp.sum(array, axis=0, keepdims=True)
        rows.append(row[:, :128] + row[:, 128:])
    count = -(-len(rows) // 8) * 8
    totals = jnp.sum(stack_rows(rows, count), axis=1, keepdims=True)
    mine = index_of((count, 128), 0) == index_of((count, 128), 1)
    return jnp.sum(jnp.where(mine, totals, 0.0), axis=0, keepdims=True)


def in_three(array):
    high = array.astype(jnp.bfloat16)
    rest = array - high.astype(jnp.float32)
    middle = rest.astype(jnp.bfloat16)
    return high, middle, (rest - middle.astype(jnp.float32)).astype(jnp.bfloat16)


def exact_dot(a, b, contract=((1,), (0,))):
    return lax.dot_general(a, b, (contract, ((), ())), preferred_element_type=jnp.float32)


def in_two(array, axis):
    high = array.astype(jnp.bfloat16)
    low = (array - high.astype(jnp.float32)).astype(jnp.bfloat16)
    return jnp.concatenate([high, high, low], axis)


def times(data, table):
    return exact_dot(in_two(data, 1), jnp.concatenate([table[...], table[0 : table.shape[0] // 2, :]], 0))


def applied(table, data):
    return exact_dot(jnp.concatenate([table[...], table[:, 0 : table.shape[1] // 2]], 1), in_two(data, 0))


def blank_kernel(out):
    out[...] = jnp.zeros((8, 128), jnp.float32)


def slots_kernel(blank, site, charge, atom, tile, shift, out):
    values = [jnp.zeros((2, 32), jnp.float32) for _ in range(4)]
    for n in range(16):
        hit = atom[...] == n
        for p in range(3):
            values[p] = jnp.where(hit, site[p, :, n : n + 1], values[p])
        values[3] = jnp.where(hit, charge[:, n : n + 1], values[3])
    for p in range(3):
        values[p] = values[p] + 4.0 * shift[p].astype(jnp.float32)
    code = tile[...]
    values.append(((code & 15) + 16 * (index_of((2, 32), 1) & 7)).astype(jnp.float32))
    values.append((code >> 4).astype(jnp.float32))
    ux, uy, uz, peak, at, side = values
    nothing = jnp.zeros((2, 32), jnp.float32)
    ordered = [ux, uz, at, nothing, uy, peak, side, nothing]
    lane = index_of((8, 128), 1)
    packed = blank[...]
    for e in range(2):
        rows = [jnp.concatenate([v[e : e + 1], jnp.zeros((1, 96), jnp.float32)], 1) for v in ordered]
        rows = stack_rows(rows, 8)
        for b in range(4):
            moved = pltpu.roll(rows, 8 * b + 8 * e, 1)
            packed = jnp.where((lane >> 3) == 2 * b + e, moved, packed)
    packed = jnp.where(lane < 64, packed, pltpu.roll(pltpu.roll(packed, 4, 0), 64, 1))
    out[...] = jnp.where(index_of((8, 128), 0) < 4, packed, pltpu.roll(packed, 4, 0))


def send_kernel(density, packed, out):
    above = index_of((8, 128), 0) < 4
    slots = packed[...]
    for n in range(16):
        half, x = n // 8, 2 * n % 16
        even, odd = [density[x + m, 8 * half : 8 * half + 8, :] for m in range(2)]
        odd = pltpu.roll(odd, 4, 0)
        out[24 * n : 24 * n + 8, :] = even
        out[24 * n + 8 : 24 * n + 16, :] = jnp.where(above, slots, odd)
        out[24 * n + 16 : 24 * n + 24, :] = jnp.where(above, odd, slots)


def line_kernel(got, z_tile, twiddle, z_even, z_odd, out, cells):
    rank = lax.axis_index("gy") * 8 + lax.axis_index("gz")
    x, half = rank & 15, rank >> 4
    own = ((x >> 3) * 2 + half).astype(jnp.float32)
    along = (x & 7).astype(jnp.float32)
    lane = index_of((8, 128), 1)
    at_j = index_of((8, 512), 0).astype(jnp.float32) - 3.5
    tile_at = index_of((128, 512), 0).astype(jnp.float32)
    scale = -LOG2E / WIDTH_SQUARED
    above = index_of((8, 128), 0) < 4
    bricks, pairs = [], []
    for n in range(16):
        middle, last = got[24 * n + 8 : 24 * n + 16, :], got[24 * n + 16 : 24 * n + 24, :]
        bricks += [got[24 * n : 24 * n + 8, :], pltpu.roll(jnp.where(above, last, middle), 4, 0)]
        pairs.append(jnp.where(above, middle, last))
    charge = []
    for b in range(4):
        sides = []
        for side in range(2):
            parts = []
            for g in range(2):
                part = jnp.zeros((8, 128), jnp.float32)
                for r in range(8):
                    shift = 16 * (r - b - 4 * side) % 128
                    moved = pairs[8 * g + r]
                    if shift:
                        moved = pltpu.roll(moved, shift, 1)
                    part = jnp.where((lane >> 4) == r, moved, part)
                parts.append(part)
            parts += [pltpu.roll(part, 4, 0) for part in parts]
            sides.append(jnp.concatenate(parts, 1))
        one, two = sides
        slots = [one[0:1], two[0:1], one[1:2], two[1:2], one[2:3], two[2:3]]
        ex = along - slots[0]
        vy, vz = slots[1] - 3.5, slots[2] - 3.5
        m = METRIC
        fixed = m[0, 0] * ex * ex + m[1, 1] * vy * vy + m[2, 2] * vz * vz
        fixed = fixed - 2.0 * m[0, 1] * ex * vy - 2.0 * m[0, 2] * ex * vz + 2.0 * m[1, 2] * vy * vz
        by_j = -2.0 * m[1, 1] * vy + 2.0 * m[0, 1] * ex - 2.0 * m[1, 2] * vz
        by_k = -2.0 * m[2, 2] * vz + 2.0 * m[0, 2] * ex - 2.0 * m[1, 2] * vy
        exponents = []
        for k in range(8):
            at_k = k - 3.5
            row = scale * (fixed + at_k * by_k + m[2, 2] * at_k * at_k)
            exponents.append(row + at_j * (scale * by_j + 2.0 * scale * m[1, 2] * at_k + scale * m[1, 1] * at_j))
        blocks = jnp.exp2(jnp.concatenate(exponents, 0))
        peak = jnp.where(slots[5] == own, slots[3], 0.0)
        placed = jnp.where(slots[4] == tile_at, 1.0, 0.0).astype(jnp.bfloat16)
        parts = jnp.concatenate(in_three(blocks * peak), 0)
        sums = exact_dot(parts, placed, ((1,), (1,)))
        charge.append(sums[0:64] + sums[64:128] + sums[128:192])
    charge = [charge[b][8 * k : 8 * k + 8] for k in range(8) for b in range(4)]
    charge = [jnp.transpose(jnp.concatenate(charge[16 * n : 16 * n + 16], 0)) for n in range(2)]
    charge = jnp.concatenate(charge, 1)
    for c in range(8):
        piece = jnp.concatenate([bricks[8 * b + c] for b in range(4)], 0)
        cells[128 * c : 128 * c + 128, :] = jnp.transpose(jnp.concatenate([piece] * 4, 0))
    group = index_of((128, 128), 1) >> 5
    sides = []
    for side in range(2):
        total = jnp.zeros((128, 128), jnp.float32)
        for n in range(4):
            total = jnp.where(group == n, cells[pl.ds(4 * side + n, 128, stride=8), :], total)
        sides.append(total)
    field = jnp.concatenate(sides, 1) + charge
    spectrum = applied(z_tile, field)
    re, im = spectrum[:128], spectrum[128:]
    re, im = re * twiddle[0] + im * twiddle[1], im * twiddle[0] - re * twiddle[1]
    even = jnp.concatenate([re[:, :128] + re[:, 128:], im[:, :128] + im[:, 128:]], 1)
    odd = jnp.concatenate([re[:, :128] - re[:, 128:], im[:, :128] - im[:, 128:]], 1)
    out[0:128, :] = times(even, z_even)
    out[128:256, :] = times(odd, z_odd)
    last = jnp.where((lane >> 5) & 1 == 0, even[0:8, 0:128], -even[0:8, 0:128])
    last = last + pltpu.roll(last, 64, 1)
    last = last + pltpu.roll(last, 32, 1)
    here = (index_of((8, 128), 0) == 0) & ((lane >> 5) == 1)
    out[0:8, :] = jnp.where(here, last, out[0:8, :])


def own_rank():
    return (lax.axis_index("gx") * 4 + lax.axis_index("gy")) * 8 + lax.axis_index("gz")


def eigenvalues(column, by_ky, by_kz):
    rank = own_rank()
    mine = by_kz[pl.ds(rank, 1), :]
    field = index_of((1, 256), 1) >> 6
    second, first = [
        jnp.where(field == 0, mine[:, n : n + 1], jnp.where(field == 1, mine[:, n + 2 : n + 3], mine[:, n + 4 : n + 5]))
        for n in range(2)
    ]
    row = by_ky[0:1, :] + second + by_ky[1:2, :] * first
    other = by_ky[2:3, :] + (2.0 * INVERSE[0, 2] / JACOBI_SCALE) * first
    return column[:, 0:1] + row + column[:, 1:2] * other, rank


def weights_of(rank):
    field = index_of((1, 256), 1) >> 6
    first = jnp.where(field == 1, 2.0, jnp.where(field == 3, 0.0, 1.0))
    other = jnp.where(field < 2, 2.0, 0.0)
    return jnp.where(rank == 0, first, other)


def plane_kernel(got, y, x_even, x_odd, column, by_ky, by_kz, out_re, out_im, out_a, out):
    lam, rank = eigenvalues(column, by_ky, by_kz)
    first = jnp.where(rank == 0, 1.0, 0.0).astype(jnp.float32)
    halves = [jnp.concatenate([got[32 * a + 16 * h : 32 * a + 16 * h + 16, :] for a in range(8)], 0) for h in range(2)]
    lines = times(jnp.concatenate(halves, 1), y)
    even = applied(x_even, jnp.concatenate([lines[:64, n : n + 256] + lines[64:, n : n + 256] for n in (0, 256)], 0))
    odd = applied(x_odd, jnp.concatenate([lines[:64, n : n + 256] - lines[64:, n : n + 256] for n in (0, 256)], 0))
    re, im = [jnp.concatenate([even[n : n + 64], odd[n : n + 64]], 0) for n in (0, 64)]
    re, im = (
        jnp.concatenate([re[:, :128] + first * im[:, 128:], re[:, 128:]], 1),
        jnp.concatenate([im[:, :128] - first * re[:, 128:], im[:, 128:]], 1),
    )
    out_re[...] = re
    out_im[...] = im
    a = STEP * lam
    out_a[...] = a
    power = (re * re + im * im) * weights_of(rank) * a
    double = a * (4.0 / LARGEST) - 2.0
    moments = [power, 0.5 * double * power]
    while len(moments) < NODES:
        moments.append(double * moments[-1] - moments[-2])
    out[...] = jnp.broadcast_to(sums_on_lanes(moments), (256, 128))


def cycle_kernel(got, re_in, im_in, a_in, nodes, x_even_back, x_odd_back, y_back, out):
    moments = jnp.sum(got[...], axis=0, keepdims=True)
    weight = dot(jnp.broadcast_to(moments, (8, 128)), nodes[0:128, :])[0:1]
    node = nodes[128:129, :]
    fine = a_in[...]
    first = jnp.where(own_rank() == 0, 1.0, 0.0).astype(jnp.float32)
    sides = [(node, 1.0 - node), (fine, 1.0 - fine)]
    scaled, potential = [1.0, 1.0], 0.0
    for cycle in range(3):
        a, mu = sides[0]
        low = weight * scaled[0] * scaled[0]
        products = [low * a, low * a * mu, low * a * mu * mu, -low * mu * mu, -low * mu * mu * mu]
        g0, g1 = solve([jnp.sum(p, axis=1, keepdims=True) for p in products])
        a, mu = sides[1]
        potential = potential + STEP * scaled[1] * (1.0 + mu * ((1.0 - g0) + (1.0 - g1) * mu))
        if cycle < 2:
            scaled = [s * mu * (mu * mu + a * (g0 + mu * g1)) for s, (a, mu) in zip(scaled, sides)]
    residual = JACOBI_SCALE * scaled[1] * mu * mu
    re, im = re_in[...], im_in[...]
    columns = []
    for multiplier in (potential, residual):
        fr, fi = multiplier * re, multiplier * im
        columns.append(
            jnp.concatenate([fr[:, :128] - first * fi[:, 128:], fi[:, :128] + first * fr[:, 128:]], 0)
        )
    columns = jnp.concatenate(columns, 1)
    low = jnp.concatenate([columns[n : n + 32] for n in range(0, 256, 64)], 0)
    high = jnp.concatenate([columns[n + 32 : n + 64] for n in range(0, 256, 64)], 0)
    planes = jnp.concatenate([applied(x_even_back, low + high), applied(x_odd_back, low - high)], 0)
    lines = []
    for f in range(2):
        for odd in range(2):
            at = 128 * odd
            pair = [planes[at + n : at + n + 64, 128 * f : 128 * f + 128] for n in (0, 64)]
            lines.append(jnp.concatenate(pair, 1))
    lines = times(jnp.concatenate(lines, 0), y_back)
    left = index_of((64, 128), 1) < 64
    for f in range(2):
        for b in range(4):
            side = slice(128 * (b // 2), 128 * (b // 2) + 128)
            even, odd = lines[128 * f : 128 * f + 64, side], lines[128 * f + 64 : 128 * f + 128, side]
            if b % 2 == 0:
                odd = pltpu.roll(odd, 64, 1)
            else:
                even = pltpu.roll(even, 64, 1)
            message = jnp.where(left, even, odd)
            for n in range(8):
                out[pl.ds((32 * n + 8 * b) * 2 + f, 8, stride=2), :] = message[8 * n : 8 * n + 8]


def back_kernel(got, z_tile_back, twiddle, z_even_back, z_odd_back, z_last_back, out, cells):
    spectra = [got[pl.ds(f, 256, stride=2), :] for f in range(2)]
    low = jnp.concatenate([v[:128] for v in spectra], 0)
    high = jnp.concatenate([v[128:] for v in spectra], 0)
    top = index_of((256, 128), 0) & 127 == 0
    part = (index_of((256, 128), 1) & 63) >> 4
    last = jnp.where(top & (part == 1), low, 0.0)
    low = jnp.where(top & (part < 2), jnp.where(part == 0, 0.5 * low, 0.0), low)
    last = times(jnp.concatenate([last[0:8], last[128:136]], 0), z_last_back)
    even, odd = times(low, z_even_back), times(high, z_odd_back)
    turned = []
    for f in range(2):
        e, o = even[128 * f : 128 * f + 128], odd[128 * f : 128 * f + 128]
        real = jnp.concatenate([e[0:8, :128] + last[8 * f : 8 * f + 8], e[8:, :128]], 0)
        re = jnp.concatenate([real + o[:, :128], real - o[:, :128]], 1)
        im = jnp.concatenate([e[:, 128:] + o[:, 128:], e[:, 128:] - o[:, 128:]], 1)
        turned.append(
            jnp.concatenate([re * twiddle[0] - im * twiddle[1], im * twiddle[0] + re * twiddle[1]], 0)
        )
    fields = applied(z_tile_back, jnp.concatenate(turned, 1))
    group = index_of((128, 128), 1) >> 5
    for side in range(2):
        one = fields[:, 128 * side : 128 * side + 128]
        two = fields[:, 256 + 128 * side : 384 + 128 * side]
        for n in range(4):
            lower = one if n == 0 else pltpu.roll(one, 128 - 32 * n, 1)
            upper = two if n == 1 else pltpu.roll(two, (160 - 32 * n) % 128, 1)
            cells[pl.ds(4 * side + n, 128, stride=8), :] = jnp.where(group == 0, lower, upper)
    for c in range(8):
        out[c] = jnp.transpose(cells[128 * c : 128 * c + 128, :])[0:64]


def place_kernel(got, potential, residual, done):
    copies = [
        pltpu.make_async_copy(got.at[:, f], out, done.at[f]) for f, out in enumerate((potential, residual))
    ]
    for copy in copies:
        copy.start()
    for copy in copies:
        copy.wait()


VMEM = pl.BlockSpec(memory_space=pltpu.VMEM)
HBM = pl.BlockSpec(memory_space=pltpu.HBM)
SMEM = pl.BlockSpec(memory_space=pltpu.SMEM)


def call(kernel, out_shapes, specs, scratch=(), name=None, result=VMEM, limit=16, cost=None):
    shapes = [jax.ShapeDtypeStruct(s, jnp.float32) for s in out_shapes]
    single = len(shapes) == 1
    return pl.pallas_call(
        kernel,
        out_shape=shapes[0] if single else shapes,
        in_specs=specs,
        out_specs=result if single else [result] * len(shapes),
        scratch_shapes=list(scratch),
        compiler_params=pltpu.CompilerParams(vmem_limit_bytes=limit * 1024 * 1024),
        name=name,
        cost_estimate=cost and pl.CostEstimate(flops=cost, bytes_accessed=cost, transcendentals=0),
    )


def exchanged(array, axes):
    return lax.all_to_all(array, axes, 0, 0, tiled=True)


def per_device(density, atom_site, atom_charge, slot_atom, slot_tile, slot_shift):
    t = {name: jnp.asarray(value) for name, value in tables().items()}
    packed = call(slots_kernel, [(8, 128)], [VMEM] * 6, name="slots")(
        call(blank_kernel, [(8, 128)], [], name="blank", cost=10**8)(),
        atom_site.reshape(3, 1, 16),
        atom_charge.reshape(1, 16),
        slot_atom.reshape(32, 2).T,
        slot_tile.reshape(32, 2).T,
        jnp.swapaxes(slot_shift.reshape(3, 32, 2), 1, 2),
    )
    message = call(send_kernel, [(384, 128)], [VMEM] * 2, name="send")(density, packed)
    got = exchanged(message.reshape(32, 1, 1536), ("gy", "gz")).reshape(384, 128)
    cells = [pltpu.VMEM((1024, 128), jnp.float32)]
    message = call(line_kernel, [(256, 128)], [VMEM] * 5, cells, "line")(
        got, t["z_tile"], t["twiddle"], t["z_even"], t["z_odd"]
    )
    got = exchanged(message, AXES)
    re, im, a, message = call(plane_kernel, [(128, 256)] * 3 + [(256, 128)], [VMEM] * 7, name="plane")(
        got, t["y"], t["x_even"], t["x_odd"], t["column"], t["by_ky"], t["by_kz"]
    )
    got = exchanged(message, AXES)
    message = call(cycle_kernel, [(512, 128)], [VMEM] * 8, name="cycle")(
        got, re, im, a, t["nodes"], t["x_even_back"], t["x_odd_back"], t["y_back"]
    )
    got = exchanged(message.reshape(256, 2, 128), AXES).reshape(512, 128)
    message = call(back_kernel, [(8, 64, 128)], [VMEM] * 6, cells, "back")(
        got, t["z_tile_back"], t["twiddle"], t["z_even_back"], t["z_odd_back"], t["z_last_back"]
    )
    got = exchanged(message, "gz").reshape(8, 2, 2, 16, 128)
    place = call(place_kernel, [(8, 2, 16, 128)] * 2, [VMEM], [pltpu.SemaphoreType.DMA((2,))], "place", HBM)
    return tuple(out.reshape(16, 16, 128) for out in place(got))


def solution(mesh):
    return jax.shard_map(
        per_device,
        mesh=mesh,
        in_specs=(
            P("gx", "gy", "gz"),
            P(None, "gx", "gy", "gz", None),
            P("gx", "gy", "gz", None),
            P("gx", "gy", "gz", None, None),
            P("gx", "gy", "gz", None, None),
            P(None, "gx", "gy", "gz", None, None),
        ),
        out_specs=(P("gx", "gy", "gz"), P("gx", "gy", "gz")),
        check_vma=False,
    )
```

```python
import functools

import jax
import jax.numpy as jnp
import ml_dtypes
import numpy as np
from jax import lax
from jax.experimental import pallas as pl
from jax.experimental.pallas import tpu as pltpu
from jax.sharding import PartitionSpec as P


METRIC = np.array([[3.24, 0.972, 0.648], [0.972, 3.2157, 0.9639], [0.648, 0.9639, 2.9565]])
INVERSE = np.array(
    [
        [0.3450043297, -0.0904572938, -0.0461258313],
        [-0.0904572938, 0.3683733435, -0.1002735462],
        [-0.0461258313, -0.1002735462, 0.3810394757],
    ]
)
FIRST_WEIGHTS = np.array([6.0 / 7.0, -15.0 / 56.0, 5.0 / 63.0, -1.0 / 56.0, 2.0 / 385.0, -1.0 / 5544.0])
SECOND_WEIGHTS = 2.0 * FIRST_WEIGHTS / np.arange(1, 7)
CENTER_WEIGHT = -2.0 * SECOND_WEIGHTS.sum()
JACOBI_SCALE = float(-CENTER_WEIGHT * np.trace(INVERSE))
STEP = 0.3
WIDTH_SQUARED = 9.0
RIDGE_SHARE = 0.01
NX, NY, NZ = 128, 64, 1024
AXES = ("gx", "gy", "gz")
LOG2E = float(np.log2(np.e))
NODES = 16
LARGEST = STEP * 2.3721


def cos_sin(n, rows, columns):
    angle = 2.0 * np.pi * (np.outer(rows, columns) % n) / n
    return np.cos(angle), np.sin(angle)


def first_symbol(n):
    angle = 2.0 * np.pi * np.arange(n) / n
    return 2.0 * sum(w * np.sin((o + 1) * angle) for o, w in enumerate(FIRST_WEIGHTS))


def second_symbol(n):
    angle = 2.0 * np.pi * np.arange(n) / n
    return CENTER_WEIGHT + 2.0 * sum(w * np.cos((o + 1) * angle) for o, w in enumerate(SECOND_WEIGHTS))


def halves_of(table):
    high = table.astype(ml_dtypes.bfloat16)
    return high, (table - high.astype(np.float64)).astype(ml_dtypes.bfloat16)


ON_THE_RIGHT = ("z_even", "z_odd", "y", "y_back", "z_even_back", "z_odd_back", "z_last_back")
ON_THE_LEFT = ("z_tile", "x_even", "x_odd", "x_even_back", "x_odd_back", "z_tile_back")


@functools.lru_cache(maxsize=None)
def tables():
    eye = np.eye(32)
    freq = np.arange(128)
    c, s = cos_sin(128, freq, freq)
    t = {}
    t["z_tile"] = np.concatenate([c, -s], 0) / 32.0 / JACOBI_SCALE
    t["z_tile_back"] = np.concatenate([c, -s], 1) / 32.0
    t["twiddle"] = np.stack(cos_sin(1024, freq, np.arange(256) // 32))
    c, s = cos_sin(8, np.arange(4), np.arange(4))
    half_eye = np.eye(16)
    for odd, name in enumerate(("z_even", "z_odd")):
        ahead = np.zeros((2, 4, 32, 2, 2, 32))
        back = np.zeros((2, 2, 2, 16, 2, 4, 2, 16))
        for k in range(4):
            for n in range(2):
                cc, ss = c[k, 2 * n + odd], s[k, 2 * n + odd]
                ahead[0, k, :, n, 0], ahead[1, k, :, n, 0] = cc * eye, ss * eye
                ahead[0, k, :, n, 1], ahead[1, k, :, n, 1] = -ss * eye, cc * eye
                for x in range(2):
                    back[x, n, 0, :, 0, k, x], back[x, n, 1, :, 0, k, x] = 2.0 * cc * half_eye, -2.0 * ss * half_eye
                    back[x, n, 0, :, 1, k, x], back[x, n, 1, :, 1, k, x] = 2.0 * ss * half_eye, 2.0 * cc * half_eye
        t[name], t[name + "_back"] = ahead.reshape(256, 128), back.reshape(128, 256)
    last = np.zeros((2, 2, 2, 16, 4, 2, 16))
    for k in range(4):
        for x in range(2):
            last[x, 0, 1, :, k, x] = (-1.0) ** k * half_eye
    t["z_last_back"] = last.reshape(128, 128)
    half, b, j = np.meshgrid(np.arange(2), np.arange(4), np.arange(8), indexing="ij")
    c, s = cos_sin(64, (16 * b + 8 * half + j).reshape(-1), np.arange(64))
    c, s = c.reshape(2, 4, 8, 64) / 8.0, s.reshape(2, 4, 8, 64) / 8.0
    ahead = np.zeros((2, 2, 2, 4, 8, 2, 4, 64))
    for f in range(2):
        ahead[:, f, 0, :, :, 0, f], ahead[:, f, 1, :, :, 0, f] = c, s
        ahead[:, f, 0, :, :, 1, f], ahead[:, f, 1, :, :, 1, f] = -s, c
    ahead[:, 0, 1, :, :, 0, 2], ahead[:, 0, 1, :, :, 1, 2] = c, -s
    t["y"] = ahead.reshape(256, 512)
    c, s = cos_sin(64, np.arange(64), np.arange(64))
    c, s = c.reshape(64, 4, 16) / 8.0, s.reshape(64, 4, 16) / 8.0
    back = np.zeros((2, 2, 64, 4, 2, 2, 16))
    for f in range(2):
        back[0, f, :, :, f, 0], back[1, f, :, :, f, 0] = c, -s
        back[0, f, :, :, f, 1], back[1, f, :, :, f, 1] = s, c
    t["y_back"] = back.reshape(256, 256)
    short = np.arange(64)
    some = np.concatenate([2 * short[:32], 2 * short[:32] + 1])
    for odd, name in enumerate(("x_even", "x_odd")):
        c, s = cos_sin(128, 2 * short + odd, short)
        t[name] = np.block([[c, s], [-s, c]]) / np.sqrt(128.0)
        c, s = cos_sin(128, 2 * short + odd, some)
        t[name + "_back"] = np.block([[c, -s], [s, c]]) / np.sqrt(128.0)
    d1x, d1y, d1z = first_symbol(NX), first_symbol(NY), first_symbol(NZ)
    d2x, d2y, d2z = second_symbol(NX), second_symbol(NY), second_symbol(NZ)
    column = np.zeros((128, 128))
    by_row = np.concatenate([2 * short, 2 * short + 1])
    column[:, 0], column[:, 1] = -INVERSE[0, 0] * d2x[by_row] / JACOBI_SCALE, d1x[by_row]
    by_ky = np.zeros((8, 256))
    by_ky[0] = np.tile(-INVERSE[1, 1] * d2y / JACOBI_SCALE, 4)
    by_ky[1] = np.tile(2.0 * INVERSE[1, 2] * d1y / JACOBI_SCALE, 4)
    by_ky[2] = np.tile(2.0 * INVERSE[0, 1] * d1y / JACOBI_SCALE, 4)
    by_kz = np.zeros((256, 128))
    low = np.arange(256)
    for f, kz in enumerate((low, low + 256, 0 * low + 512)):
        by_kz[:, 2 * f], by_kz[:, 2 * f + 1] = -INVERSE[2, 2] * d2z[kz] / JACOBI_SCALE, d1z[kz]
    t["column"], t["by_ky"], t["by_kz"] = column, by_ky, by_kz
    angle = (np.arange(NODES) + 0.5) * np.pi / NODES
    nodes = np.zeros((24, 128))
    nodes[:NODES, :NODES] = 2.0 / NODES * np.cos(np.outer(np.arange(NODES), angle))
    nodes[0, :NODES] = 1.0 / NODES
    nodes[NODES, :NODES] = 0.5 * LARGEST * (1.0 + np.cos(angle))
    t["nodes"] = nodes
    for name in ON_THE_RIGHT:
        high, low = halves_of(t[name])
        t[name] = np.concatenate([high, low], 0)
    for name in ON_THE_LEFT:
        high, low = halves_of(t[name])
        t[name] = np.concatenate([high, low], 1)
    return {n: v if v.dtype == ml_dtypes.bfloat16 else v.astype(np.float32) for n, v in t.items()}


def index_of(shape, dim):
    return lax.broadcasted_iota(jnp.int32, shape, dim)


def solve(gram):
    ff, fc, cc, fs, cs = gram
    ridge = RIDGE_SHARE * 0.5 * (ff + cc)
    ff, cc = ff + ridge, cc + ridge
    determinant = ff * cc - fc * fc
    return (cc * fs - fc * cs) / determinant, (ff * cs - fc * fs) / determinant


def stack_rows(rows, count):
    at = index_of((count, 128), 0)
    stacked = jnp.zeros((count, 128), jnp.float32)
    for n, row in enumerate(rows):
        stacked = jnp.where(at == n, row, stacked)
    return stacked


def sums_of(arrays):
    rows = []
    for array in arrays:
        row = jnp.sum(array, axis=0, keepdims=True)
        rows.append(row[:, :128] + row[:, 128:])
    count = -(-len(rows) // 8) * 8
    return jnp.sum(stack_rows(rows, count), axis=1, keepdims=True)


def parts_of(array):
    high = array.astype(jnp.bfloat16)
    return high, (array - high.astype(jnp.float32)).astype(jnp.bfloat16)


def bf16_dot(a, b, contract=((1,), (0,))):
    return lax.dot_general(a, b, (contract, ((), ())), preferred_element_type=jnp.float32)


def in_two(array, axis):
    high, low = parts_of(array)
    return jnp.concatenate([high, high, low], axis)


def times(data, table):
    return bf16_dot(in_two(data, 1), jnp.concatenate([table[...], table[0 : table.shape[0] // 2, :]], 0))


def applied(table, data):
    return bf16_dot(jnp.concatenate([table[...], table[:, 0 : table.shape[1] // 2]], 1), in_two(data, 0))


def blank_kernel(out):
    out[...] = jnp.zeros((8, 128), jnp.float32)


def slots_kernel(blank, site, charge, atom, tile, shift, out):
    wide = jnp.concatenate([atom[...], jnp.zeros((2, 96), jnp.int32)], 1)
    wide = jnp.concatenate([wide, jnp.zeros((6, 128), jnp.int32)], 0)
    values = []
    for row in [site[0], site[1], site[2], charge[...]]:
        row = jnp.broadcast_to(jnp.concatenate([row, jnp.zeros((1, 112), jnp.float32)], 1), (8, 128))
        chosen = jnp.take_along_axis(row, wide, axis=1, mode="promise_in_bounds")
        values.append(chosen[0:2, 0:32])
    for p in range(3):
        values[p] = values[p] + 4.0 * shift[p].astype(jnp.float32)
    code = tile[...]
    values.append(((code & 15) + 16 * (index_of((2, 32), 1) & 7)).astype(jnp.float32))
    values.append((code >> 4).astype(jnp.float32))
    ux, uy, uz, peak, at, side = values
    nothing = jnp.zeros((2, 32), jnp.float32)
    ordered = [ux, uz, at, nothing, uy, peak, side, nothing]
    lane = index_of((8, 128), 1)
    packed = blank[...]
    for e in range(2):
        rows = [jnp.concatenate([v[e : e + 1], jnp.zeros((1, 96), jnp.float32)], 1) for v in ordered]
        rows = stack_rows(rows, 8)
        for b in range(4):
            moved = pltpu.roll(rows, 8 * b + 8 * e, 1)
            packed = jnp.where((lane >> 3) == 2 * b + e, moved, packed)
    packed = jnp.where(lane < 64, packed, pltpu.roll(pltpu.roll(packed, 4, 0), 64, 1))
    out[...] = jnp.where(index_of((8, 128), 0) < 4, packed, pltpu.roll(packed, 4, 0))


def send_kernel(density, packed, out):
    above = index_of((8, 128), 0) < 4
    slots = packed[...]
    for n in range(16):
        half, x = n // 8, 2 * n % 16
        even, odd = [density[x + m, 8 * half : 8 * half + 8, :] for m in range(2)]
        odd = pltpu.roll(odd, 4, 0)
        out[24 * n : 24 * n + 8, :] = even
        out[24 * n + 8 : 24 * n + 16, :] = jnp.where(above, slots, odd)
        out[24 * n + 16 : 24 * n + 24, :] = jnp.where(above, odd, slots)


def line_kernel(got, z_tile, twiddle, z_even, z_odd, out, cells):
    rank = lax.axis_index("gy") * 8 + lax.axis_index("gz")
    x, half = rank & 15, rank >> 4
    own = ((x >> 3) * 2 + half).astype(jnp.float32)
    along = (x & 7).astype(jnp.float32)
    lane = index_of((8, 128), 1)
    at_j = index_of((8, 512), 0).astype(jnp.float32) - 3.5
    tile_at = index_of((128, 512), 0).astype(jnp.float32)
    scale = -LOG2E / WIDTH_SQUARED
    above = index_of((8, 128), 0) < 4
    bricks, pairs = [], []
    for n in range(16):
        middle, last = got[24 * n + 8 : 24 * n + 16, :], got[24 * n + 16 : 24 * n + 24, :]
        bricks += [got[24 * n : 24 * n + 8, :], pltpu.roll(jnp.where(above, last, middle), 4, 0)]
        pairs.append(jnp.where(above, middle, last))
    charge = []
    for b in range(4):
        sides = []
        for side in range(2):
            parts = []
            for g in range(2):
                part = jnp.zeros((8, 128), jnp.float32)
                for r in range(8):
                    shift = 16 * (r - b - 4 * side) % 128
                    moved = pairs[8 * g + r]
                    if shift:
                        moved = pltpu.roll(moved, shift, 1)
                    part = jnp.where((lane >> 4) == r, moved, part)
                parts.append(part)
            parts += [pltpu.roll(part, 4, 0) for part in parts]
            sides.append(jnp.concatenate(parts, 1))
        one, two = sides
        slots = [one[0:1], two[0:1], one[1:2], two[1:2], one[2:3], two[2:3]]
        ex = along - slots[0]
        vy, vz = slots[1] - 3.5, slots[2] - 3.5
        m = METRIC
        fixed = m[0, 0] * ex * ex + m[1, 1] * vy * vy + m[2, 2] * vz * vz
        fixed = fixed - 2.0 * m[0, 1] * ex * vy - 2.0 * m[0, 2] * ex * vz + 2.0 * m[1, 2] * vy * vz
        by_j = -2.0 * m[1, 1] * vy + 2.0 * m[0, 1] * ex - 2.0 * m[1, 2] * vz
        by_k = -2.0 * m[2, 2] * vz + 2.0 * m[0, 2] * ex - 2.0 * m[1, 2] * vy
        exponents = []
        for k in range(8):
            at_k = k - 3.5
            row = scale * (fixed + at_k * by_k + m[2, 2] * at_k * at_k)
            exponents.append(row + at_j * (scale * by_j + 2.0 * scale * m[1, 2] * at_k + scale * m[1, 1] * at_j))
        blocks = jnp.exp2(jnp.concatenate(exponents, 0))
        peak = jnp.where(slots[5] == own, slots[3], 0.0)
        placed = jnp.where(slots[4] == tile_at, 1.0, 0.0).astype(jnp.bfloat16)
        parts = jnp.concatenate(parts_of(blocks * peak), 0)
        sums = bf16_dot(parts, placed, ((1,), (1,)))
        charge.append(sums[0:64] + sums[64:128])
    charge = [charge[b][8 * k : 8 * k + 8] for k in range(8) for b in range(4)]
    charge = [jnp.transpose(jnp.concatenate(charge[16 * n : 16 * n + 16], 0)) for n in range(2)]
    charge = jnp.concatenate(charge, 1)
    for c in range(8):
        piece = jnp.concatenate([bricks[8 * b + c] for b in range(4)], 0)
        cells[128 * c : 128 * c + 128, :] = jnp.transpose(jnp.concatenate([piece] * 4, 0))
    group = index_of((128, 128), 1) >> 5
    sides = []
    for side in range(2):
        total = jnp.zeros((128, 128), jnp.float32)
        for n in range(4):
            total = jnp.where(group == n, cells[pl.ds(4 * side + n, 128, stride=8), :], total)
        sides.append(total)
    field = jnp.concatenate(sides, 1) + charge
    spectrum = applied(z_tile, field)
    re, im = spectrum[:128], spectrum[128:]
    re, im = re * twiddle[0] + im * twiddle[1], im * twiddle[0] - re * twiddle[1]
    even = jnp.concatenate([re[:, :128] + re[:, 128:], im[:, :128] + im[:, 128:]], 1)
    odd = jnp.concatenate([re[:, :128] - re[:, 128:], im[:, :128] - im[:, 128:]], 1)
    out[0:128, :] = times(even, z_even)
    out[128:256, :] = times(odd, z_odd)
    last = jnp.where((lane >> 5) & 1 == 0, even[0:8, 0:128], -even[0:8, 0:128])
    last = last + pltpu.roll(last, 64, 1)
    last = last + pltpu.roll(last, 32, 1)
    here = (index_of((8, 128), 0) == 0) & ((lane >> 5) == 1)
    out[0:8, :] = jnp.where(here, last, out[0:8, :])


def own_rank():
    return (lax.axis_index("gx") * 4 + lax.axis_index("gy")) * 8 + lax.axis_index("gz")


def eigenvalues(column, by_ky, by_kz):
    rank = own_rank()
    mine = by_kz[pl.ds(rank, 1), :]
    field = index_of((1, 256), 1) >> 6
    second, first = [
        jnp.where(field == 0, mine[:, n : n + 1], jnp.where(field == 1, mine[:, n + 2 : n + 3], mine[:, n + 4 : n + 5]))
        for n in range(2)
    ]
    row = by_ky[0:1, :] + second + by_ky[1:2, :] * first
    other = by_ky[2:3, :] + (2.0 * INVERSE[0, 2] / JACOBI_SCALE) * first
    return column[:, 0:1] + row + column[:, 1:2] * other, rank


def weights_of(rank):
    field = index_of((1, 256), 1) >> 6
    first = jnp.where(field == 1, 2.0, jnp.where(field == 3, 0.0, 1.0))
    other = jnp.where(field < 2, 2.0, 0.0)
    return jnp.where(rank == 0, first, other)


def plane_kernel(got, y, x_even, x_odd, column, by_ky, by_kz, nodes, out_re, out_im, out_a, out):
    lam, rank = eigenvalues(column, by_ky, by_kz)
    first = jnp.where(rank == 0, 1.0, 0.0).astype(jnp.float32)
    halves = [jnp.concatenate([got[32 * a + 16 * h : 32 * a + 16 * h + 16, :] for a in range(8)], 0) for h in range(2)]
    lines = times(jnp.concatenate(halves, 1), y)
    even = applied(x_even, jnp.concatenate([lines[:64, n : n + 256] + lines[64:, n : n + 256] for n in (0, 256)], 0))
    odd = applied(x_odd, jnp.concatenate([lines[:64, n : n + 256] - lines[64:, n : n + 256] for n in (0, 256)], 0))
    re, im = [jnp.concatenate([even[n : n + 64], odd[n : n + 64]], 0) for n in (0, 64)]
    re, im = (
        jnp.concatenate([re[:, :128] + first * im[:, 128:], re[:, 128:]], 1),
        jnp.concatenate([im[:, :128] - first * re[:, 128:], im[:, 128:]], 1),
    )
    out_re[...] = re
    out_im[...] = im
    a = STEP * lam
    out_a[...] = a
    power = (re * re + im * im) * weights_of(rank) * a
    double = a * (4.0 / LARGEST) - 2.0
    moments = [power, 0.5 * double * power]
    while len(moments) < NODES:
        moments.append(double * moments[-1] - moments[-2])
    weight = jnp.sum(sums_of(moments) * nodes[0:NODES, :], axis=0, keepdims=True)
    out[...] = jnp.broadcast_to(weight, (256, 128))


def cycle_kernel(got, re_in, im_in, a_in, nodes, x_even_back, x_odd_back, y_back, out):
    weight = jnp.sum(got[...], axis=0, keepdims=True)
    node = nodes[NODES : NODES + 1, :]
    fine = a_in[...]
    first = jnp.where(own_rank() == 0, 1.0, 0.0).astype(jnp.float32)
    sides = [(node, 1.0 - node), (fine, 1.0 - fine)]
    scaled, potential = [1.0, 1.0], 0.0
    for cycle in range(3):
        a, mu = sides[0]
        low = weight * scaled[0] * scaled[0]
        products = [low * a, low * a * mu, low * a * mu * mu, -low * mu * mu, -low * mu * mu * mu]
        g0, g1 = solve([jnp.sum(p, axis=1, keepdims=True) for p in products])
        a, mu = sides[1]
        potential = potential + STEP * scaled[1] * (1.0 + mu * ((1.0 - g0) + (1.0 - g1) * mu))
        if cycle < 2:
            scaled = [s * mu * (mu * mu + a * (g0 + mu * g1)) for s, (a, mu) in zip(scaled, sides)]
    residual = JACOBI_SCALE * scaled[1] * mu * mu
    re, im = re_in[...], im_in[...]
    columns = []
    for multiplier in (potential, residual):
        fr, fi = multiplier * re, multiplier * im
        columns.append(
            jnp.concatenate([fr[:, :128] - first * fi[:, 128:], fi[:, :128] + first * fr[:, 128:]], 0)
        )
    columns = jnp.concatenate(columns, 1)
    low = jnp.concatenate([columns[n : n + 32] for n in range(0, 256, 64)], 0)
    high = jnp.concatenate([columns[n + 32 : n + 64] for n in range(0, 256, 64)], 0)
    planes = jnp.concatenate([applied(x_even_back, low + high), applied(x_odd_back, low - high)], 0)
    lines = []
    for f in range(2):
        for odd in range(2):
            at = 128 * odd
            pair = [planes[at + n : at + n + 64, 128 * f : 128 * f + 128] for n in (0, 64)]
            lines.append(jnp.concatenate(pair, 1))
    lines = times(jnp.concatenate(lines, 0), y_back)
    left = index_of((64, 128), 1) < 64
    for f in range(2):
        for b in range(4):
            side = slice(128 * (b // 2), 128 * (b // 2) + 128)
            even, odd = lines[128 * f : 128 * f + 64, side], lines[128 * f + 64 : 128 * f + 128, side]
            if b % 2 == 0:
                odd = pltpu.roll(odd, 64, 1)
            else:
                even = pltpu.roll(even, 64, 1)
            message = jnp.where(left, even, odd)
            for n in range(8):
                out[pl.ds((32 * n + 8 * b) * 2 + f, 8, stride=2), :] = message[8 * n : 8 * n + 8]


def back_kernel(got, z_tile_back, twiddle, z_even_back, z_odd_back, z_last_back, out, cells):
    spectra = [got[pl.ds(f, 256, stride=2), :] for f in range(2)]
    low = jnp.concatenate([v[:128] for v in spectra], 0)
    high = jnp.concatenate([v[128:] for v in spectra], 0)
    top = index_of((256, 128), 0) & 127 == 0
    part = (index_of((256, 128), 1) & 63) >> 4
    last = jnp.where(top & (part == 1), low, 0.0)
    low = jnp.where(top & (part < 2), jnp.where(part == 0, 0.5 * low, 0.0), low)
    last = times(jnp.concatenate([last[0:8], last[128:136]], 0), z_last_back)
    even, odd = times(low, z_even_back), times(high, z_odd_back)
    turned = []
    for f in range(2):
        e, o = even[128 * f : 128 * f + 128], odd[128 * f : 128 * f + 128]
        real = jnp.concatenate([e[0:8, :128] + last[8 * f : 8 * f + 8], e[8:, :128]], 0)
        re = jnp.concatenate([real + o[:, :128], real - o[:, :128]], 1)
        im = jnp.concatenate([e[:, 128:] + o[:, 128:], e[:, 128:] - o[:, 128:]], 1)
        turned.append(
            jnp.concatenate([re * twiddle[0] - im * twiddle[1], im * twiddle[0] + re * twiddle[1]], 0)
        )
    fields = applied(z_tile_back, jnp.concatenate(turned, 1))
    group = index_of((128, 128), 1) >> 5
    for side in range(2):
        one = fields[:, 128 * side : 128 * side + 128]
        two = fields[:, 256 + 128 * side : 384 + 128 * side]
        for n in range(4):
            lower = one if n == 0 else pltpu.roll(one, 128 - 32 * n, 1)
            upper = two if n == 1 else pltpu.roll(two, (160 - 32 * n) % 128, 1)
            cells[pl.ds(4 * side + n, 128, stride=8), :] = jnp.where(group == 0, lower, upper)
    for c in range(8):
        out[c] = jnp.transpose(cells[128 * c : 128 * c + 128, :])[0:64]


def place_kernel(got, potential, residual, done):
    copies = [
        pltpu.make_async_copy(got.at[:, f], out, done.at[f]) for f, out in enumerate((potential, residual))
    ]
    for copy in copies:
        copy.start()
    for copy in copies:
        copy.wait()


VMEM = pl.BlockSpec(memory_space=pltpu.VMEM)
HBM = pl.BlockSpec(memory_space=pltpu.HBM)
SMEM = pl.BlockSpec(memory_space=pltpu.SMEM)


def call(kernel, out_shapes, specs, scratch=(), name=None, result=VMEM, limit=16, cost=None):
    shapes = [jax.ShapeDtypeStruct(s, jnp.float32) for s in out_shapes]
    single = len(shapes) == 1
    return pl.pallas_call(
        kernel,
        out_shape=shapes[0] if single else shapes,
        in_specs=specs,
        out_specs=result if single else [result] * len(shapes),
        scratch_shapes=list(scratch),
        compiler_params=pltpu.CompilerParams(vmem_limit_bytes=limit * 1024 * 1024),
        name=name,
        cost_estimate=cost and pl.CostEstimate(flops=cost, bytes_accessed=cost, transcendentals=0),
    )


def exchanged(array, axes):
    return lax.all_to_all(array, axes, 0, 0, tiled=True)


def per_device(density, atom_site, atom_charge, slot_atom, slot_tile, slot_shift):
    t = {name: jnp.asarray(value) for name, value in tables().items()}
    packed = call(slots_kernel, [(8, 128)], [VMEM] * 6, name="slots")(
        call(blank_kernel, [(8, 128)], [], name="blank", cost=10**8)(),
        atom_site.reshape(3, 1, 16),
        atom_charge.reshape(1, 16),
        slot_atom.reshape(32, 2).T,
        slot_tile.reshape(32, 2).T,
        jnp.swapaxes(slot_shift.reshape(3, 32, 2), 1, 2),
    )
    message = call(send_kernel, [(384, 128)], [VMEM] * 2, name="send")(density, packed)
    got = exchanged(message.reshape(32, 1, 1536), ("gy", "gz")).reshape(384, 128)
    cells = [pltpu.VMEM((1024, 128), jnp.float32)]
    message = call(line_kernel, [(256, 128)], [VMEM] * 5, cells, "line")(
        got, t["z_tile"], t["twiddle"], t["z_even"], t["z_odd"]
    )
    got = exchanged(message, AXES)
    re, im, a, message = call(plane_kernel, [(128, 256)] * 3 + [(256, 128)], [VMEM] * 8, name="plane")(
        got, t["y"], t["x_even"], t["x_odd"], t["column"], t["by_ky"], t["by_kz"], t["nodes"]
    )
    got = exchanged(message, AXES)
    message = call(cycle_kernel, [(512, 128)], [VMEM] * 8, name="cycle")(
        got, re, im, a, t["nodes"], t["x_even_back"], t["x_odd_back"], t["y_back"]
    )
    got = exchanged(message.reshape(256, 2, 128), AXES).reshape(512, 128)
    message = call(back_kernel, [(8, 64, 128)], [VMEM] * 6, cells, "back")(
        got, t["z_tile_back"], t["twiddle"], t["z_even_back"], t["z_odd_back"], t["z_last_back"]
    )
    got = exchanged(message, "gz").reshape(8, 2, 2, 16, 128)
    place = call(place_kernel, [(8, 2, 16, 128)] * 2, [VMEM], [pltpu.SemaphoreType.DMA((2,))], "place", HBM)
    return tuple(out.reshape(16, 16, 128) for out in place(got))


def solution(mesh):
    return jax.shard_map(
        per_device,
        mesh=mesh,
        in_specs=(
            P("gx", "gy", "gz"),
            P(None, "gx", "gy", "gz", None),
            P("gx", "gy", "gz", None),
            P("gx", "gy", "gz", None, None),
            P("gx", "gy", "gz", None, None),
            P(None, "gx", "gy", "gz", None, None),
        ),
        out_specs=(P("gx", "gy", "gz"), P("gx", "gy", "gz")),
        check_vma=False,
    )
```

```python
import functools

import jax
import jax.numpy as jnp
import ml_dtypes
import numpy as np
from jax import lax
from jax.experimental import pallas as pl
from jax.experimental.pallas import tpu as pltpu
from jax.sharding import PartitionSpec as P


METRIC = np.array([[3.24, 0.972, 0.648], [0.972, 3.2157, 0.9639], [0.648, 0.9639, 2.9565]])
INVERSE = np.array(
    [
        [0.3450043297, -0.0904572938, -0.0461258313],
        [-0.0904572938, 0.3683733435, -0.1002735462],
        [-0.0461258313, -0.1002735462, 0.3810394757],
    ]
)
FIRST_WEIGHTS = np.array([6.0 / 7.0, -15.0 / 56.0, 5.0 / 63.0, -1.0 / 56.0, 2.0 / 385.0, -1.0 / 5544.0])
SECOND_WEIGHTS = 2.0 * FIRST_WEIGHTS / np.arange(1, 7)
CENTER_WEIGHT = -2.0 * SECOND_WEIGHTS.sum()
JACOBI_SCALE = float(-CENTER_WEIGHT * np.trace(INVERSE))
STEP = 0.3
WIDTH_SQUARED = 9.0
RIDGE_SHARE = 0.01
NX, NY, NZ = 128, 64, 1024
AXES = ("gx", "gy", "gz")
LOG2E = float(np.log2(np.e))
NODES = 16
LARGEST = STEP * 2.3721


def cos_sin(n, rows, columns):
    angle = 2.0 * np.pi * (np.outer(rows, columns) % n) / n
    return np.cos(angle), np.sin(angle)


def first_symbol(n):
    angle = 2.0 * np.pi * np.arange(n) / n
    return 2.0 * sum(w * np.sin((o + 1) * angle) for o, w in enumerate(FIRST_WEIGHTS))


def second_symbol(n):
    angle = 2.0 * np.pi * np.arange(n) / n
    return CENTER_WEIGHT + 2.0 * sum(w * np.cos((o + 1) * angle) for o, w in enumerate(SECOND_WEIGHTS))


def halves_of(table):
    high = table.astype(ml_dtypes.bfloat16)
    return high, (table - high.astype(np.float64)).astype(ml_dtypes.bfloat16)


ON_THE_RIGHT = ("z_even", "z_odd", "y", "y_back", "z_even_back", "z_odd_back", "z_last_back")
ON_THE_LEFT = ("z_tile", "x_even", "x_odd", "x_even_back", "x_odd_back", "z_tile_back")


@functools.lru_cache(maxsize=None)
def tables():
    eye = np.eye(32)
    freq = np.arange(128)
    c, s = cos_sin(128, freq, freq)
    t = {}
    t["z_tile"] = np.concatenate([c, -s], 0) / 32.0 / JACOBI_SCALE
    t["z_tile_back"] = np.concatenate([c, -s], 1) / 32.0
    t["twiddle"] = np.stack(cos_sin(1024, freq, np.arange(256) // 32))
    c, s = cos_sin(8, np.arange(4), np.arange(4))
    half_eye = np.eye(16)
    for odd, name in enumerate(("z_even", "z_odd")):
        ahead = np.zeros((2, 4, 32, 2, 2, 32))
        back = np.zeros((2, 2, 2, 16, 2, 4, 2, 16))
        for k in range(4):
            for n in range(2):
                cc, ss = c[k, 2 * n + odd], s[k, 2 * n + odd]
                ahead[0, k, :, n, 0], ahead[1, k, :, n, 0] = cc * eye, ss * eye
                ahead[0, k, :, n, 1], ahead[1, k, :, n, 1] = -ss * eye, cc * eye
                for x in range(2):
                    back[x, n, 0, :, 0, k, x], back[x, n, 1, :, 0, k, x] = 2.0 * cc * half_eye, -2.0 * ss * half_eye
                    back[x, n, 0, :, 1, k, x], back[x, n, 1, :, 1, k, x] = 2.0 * ss * half_eye, 2.0 * cc * half_eye
        t[name], t[name + "_back"] = ahead.reshape(256, 128), back.reshape(128, 256)
    last = np.zeros((2, 2, 2, 16, 4, 2, 16))
    for k in range(4):
        for x in range(2):
            last[x, 0, 1, :, k, x] = (-1.0) ** k * half_eye
    t["z_last_back"] = last.reshape(128, 128)
    half, b, j = np.meshgrid(np.arange(2), np.arange(4), np.arange(8), indexing="ij")
    c, s = cos_sin(64, (16 * b + 8 * half + j).reshape(-1), np.arange(64))
    c, s = c.reshape(2, 4, 8, 64) / 8.0, s.reshape(2, 4, 8, 64) / 8.0
    ahead = np.zeros((2, 2, 2, 4, 8, 2, 4, 64))
    for f in range(2):
        ahead[:, f, 0, :, :, 0, f], ahead[:, f, 1, :, :, 0, f] = c, s
        ahead[:, f, 0, :, :, 1, f], ahead[:, f, 1, :, :, 1, f] = -s, c
    ahead[:, 0, 1, :, :, 0, 2], ahead[:, 0, 1, :, :, 1, 2] = c, -s
    t["y"] = ahead.reshape(256, 512)
    c, s = cos_sin(64, np.arange(64), np.arange(64))
    c, s = c.reshape(64, 4, 16) / 8.0, s.reshape(64, 4, 16) / 8.0
    back = np.zeros((2, 2, 64, 4, 2, 2, 16))
    for f in range(2):
        back[0, f, :, :, f, 0], back[1, f, :, :, f, 0] = c, -s
        back[0, f, :, :, f, 1], back[1, f, :, :, f, 1] = s, c
    t["y_back"] = back.reshape(256, 256)
    short = np.arange(64)
    some = np.concatenate([2 * short[:32], 2 * short[:32] + 1])
    for odd, name in enumerate(("x_even", "x_odd")):
        c, s = cos_sin(128, 2 * short + odd, short)
        t[name] = np.block([[c, s], [-s, c]]) / np.sqrt(128.0)
        c, s = cos_sin(128, 2 * short + odd, some)
        t[name + "_back"] = np.block([[c, -s], [s, c]]) / np.sqrt(128.0)
    d1x, d1y, d1z = first_symbol(NX), first_symbol(NY), first_symbol(NZ)
    d2x, d2y, d2z = second_symbol(NX), second_symbol(NY), second_symbol(NZ)
    column = np.zeros((128, 128))
    by_row = np.concatenate([2 * short, 2 * short + 1])
    column[:, 0], column[:, 1] = -INVERSE[0, 0] * d2x[by_row] / JACOBI_SCALE, d1x[by_row]
    by_ky = np.zeros((8, 256))
    by_ky[0] = np.tile(-INVERSE[1, 1] * d2y / JACOBI_SCALE, 4)
    by_ky[1] = np.tile(2.0 * INVERSE[1, 2] * d1y / JACOBI_SCALE, 4)
    by_ky[2] = np.tile(2.0 * INVERSE[0, 1] * d1y / JACOBI_SCALE, 4)
    by_kz = np.zeros((256, 128))
    low = np.arange(256)
    for f, kz in enumerate((low, low + 256, 0 * low + 512)):
        by_kz[:, 2 * f], by_kz[:, 2 * f + 1] = -INVERSE[2, 2] * d2z[kz] / JACOBI_SCALE, d1z[kz]
    t["column"], t["by_ky"], t["by_kz"] = column, by_ky, by_kz
    angle = (np.arange(NODES) + 0.5) * np.pi / NODES
    nodes = np.zeros((24, 128))
    nodes[:NODES, :NODES] = 2.0 / NODES * np.cos(np.outer(np.arange(NODES), angle))
    nodes[0, :NODES] = 1.0 / NODES
    nodes[NODES, :NODES] = 0.5 * LARGEST * (1.0 + np.cos(angle))
    t["nodes"] = nodes
    for name in ON_THE_RIGHT:
        high, low = halves_of(t[name])
        t[name] = np.concatenate([high, low], 0)
    for name in ON_THE_LEFT:
        high, low = halves_of(t[name])
        t[name] = np.concatenate([high, low], 1)
    return {n: v if v.dtype == ml_dtypes.bfloat16 else v.astype(np.float32) for n, v in t.items()}


def index_of(shape, dim):
    return lax.broadcasted_iota(jnp.int32, shape, dim)


def solve(gram):
    ff, fc, cc, fs, cs = gram
    ridge = RIDGE_SHARE * 0.5 * (ff + cc)
    ff, cc = ff + ridge, cc + ridge
    determinant = ff * cc - fc * fc
    return (cc * fs - fc * cs) / determinant, (ff * cs - fc * fs) / determinant


def stack_rows(rows, count):
    at = index_of((count, 128), 0)
    stacked = jnp.zeros((count, 128), jnp.float32)
    for n, row in enumerate(rows):
        stacked = jnp.where(at == n, row, stacked)
    return stacked


def sums_of(arrays):
    rows = []
    for array in arrays:
        row = jnp.sum(array, axis=0, keepdims=True)
        rows.append(row[:, :128] + row[:, 128:])
    count = -(-len(rows) // 8) * 8
    return jnp.sum(stack_rows(rows, count), axis=1, keepdims=True)


def parts_of(array):
    high = array.astype(jnp.bfloat16)
    return high, (array - high.astype(jnp.float32)).astype(jnp.bfloat16)


def bf16_dot(a, b, contract=((1,), (0,))):
    return lax.dot_general(a, b, (contract, ((), ())), preferred_element_type=jnp.float32)


def in_two(array, axis):
    high, low = parts_of(array)
    return jnp.concatenate([high, high, low], axis)


def times(data, table):
    return bf16_dot(in_two(data, 1), jnp.concatenate([table[...], table[0 : table.shape[0] // 2, :]], 0))


def applied(table, data):
    return bf16_dot(jnp.concatenate([table[...], table[:, 0 : table.shape[1] // 2]], 1), in_two(data, 0))


def blank_kernel(out):
    out[...] = jnp.zeros((8, 128), jnp.float32)


def slots_kernel(blank, site, charge, atom, tile, shift, out):
    wide = jnp.concatenate([atom[...], jnp.zeros((2, 96), jnp.int32)], 1)
    wide = jnp.concatenate([wide, jnp.zeros((6, 128), jnp.int32)], 0)
    values = []
    for row in [site[0], site[1], site[2], charge[...]]:
        row = jnp.broadcast_to(jnp.concatenate([row, jnp.zeros((1, 112), jnp.float32)], 1), (8, 128))
        chosen = jnp.take_along_axis(row, wide, axis=1, mode="promise_in_bounds")
        values.append(chosen[0:2, 0:32])
    for p in range(3):
        values[p] = values[p] + 4.0 * shift[p].astype(jnp.float32)
    code = tile[...]
    values.append(((code & 15) + 16 * (index_of((2, 32), 1) & 7)).astype(jnp.float32))
    values.append((code >> 4).astype(jnp.float32))
    ux, uy, uz, peak, at, side = values
    nothing = jnp.zeros((2, 32), jnp.float32)
    ordered = [ux, uz, at, nothing, uy, peak, side, nothing]
    lane = index_of((8, 128), 1)
    packed = blank[...]
    for e in range(2):
        rows = [jnp.concatenate([v[e : e + 1], jnp.zeros((1, 96), jnp.float32)], 1) for v in ordered]
        rows = stack_rows(rows, 8)
        for b in range(4):
            moved = pltpu.roll(rows, 8 * b + 8 * e, 1)
            packed = jnp.where((lane >> 3) == 2 * b + e, moved, packed)
    packed = jnp.where(lane < 64, packed, pltpu.roll(pltpu.roll(packed, 4, 0), 64, 1))
    packed = jnp.where(index_of((8, 128), 0) < 4, packed, pltpu.roll(packed, 4, 0))
    place = ((lax.axis_index("gy") * 8 + lax.axis_index("gz")) >> 1) & 7
    out[...] = pltpu.roll(packed, 16 * place, 1)


def send_kernel(density, packed, out):
    above = index_of((8, 128), 0) < 4
    slots = packed[...]
    for n in range(16):
        half, x = n // 8, 2 * n % 16
        even, odd = [density[x + m, 8 * half : 8 * half + 8, :] for m in range(2)]
        odd = pltpu.roll(odd, 4, 0)
        out[24 * n : 24 * n + 8, :] = even
        out[24 * n + 8 : 24 * n + 16, :] = jnp.where(above, slots, odd)
        out[24 * n + 16 : 24 * n + 24, :] = jnp.where(above, odd, slots)


def line_kernel(got, z_tile, twiddle, z_even, z_odd, out, cells):
    rank = lax.axis_index("gy") * 8 + lax.axis_index("gz")
    x, half = rank & 15, rank >> 4
    own = ((x >> 3) * 2 + half).astype(jnp.float32)
    along = (x & 7).astype(jnp.float32)
    lane = index_of((8, 128), 1)
    at_j = index_of((8, 512), 0).astype(jnp.float32) - 3.5
    tile_at = index_of((128, 512), 0).astype(jnp.float32)
    scale = -LOG2E / WIDTH_SQUARED
    above = index_of((8, 128), 0) < 4
    bricks, pairs = [], []
    for n in range(16):
        middle, last = got[24 * n + 8 : 24 * n + 16, :], got[24 * n + 16 : 24 * n + 24, :]
        bricks += [got[24 * n : 24 * n + 8, :], pltpu.roll(jnp.where(above, last, middle), 4, 0)]
        pairs.append(jnp.where(above, middle, last))
    charge = []
    for b in range(4):
        sides = []
        for side in range(2):
            parts = []
            for g in range(2):
                part = jnp.zeros((8, 128), jnp.float32)
                for r in range(8):
                    part = jnp.where((lane >> 4) == (r + b + 4 * side) % 8, pairs[8 * g + r], part)
                parts.append(pltpu.roll(part, 64, 1) if side else part)
            parts += [pltpu.roll(part, 4, 0) for part in parts]
            sides.append(jnp.concatenate(parts, 1))
        one, two = sides
        slots = [one[0:1], two[0:1], one[1:2], two[1:2], one[2:3], two[2:3]]
        ex = along - slots[0]
        vy, vz = slots[1] - 3.5, slots[2] - 3.5
        m = METRIC
        fixed = m[0, 0] * ex * ex + m[1, 1] * vy * vy + m[2, 2] * vz * vz
        fixed = fixed - 2.0 * m[0, 1] * ex * vy - 2.0 * m[0, 2] * ex * vz + 2.0 * m[1, 2] * vy * vz
        by_j = -2.0 * m[1, 1] * vy + 2.0 * m[0, 1] * ex - 2.0 * m[1, 2] * vz
        by_k = -2.0 * m[2, 2] * vz + 2.0 * m[0, 2] * ex - 2.0 * m[1, 2] * vy
        exponents = []
        for k in range(8):
            at_k = k - 3.5
            row = scale * (fixed + at_k * by_k + m[2, 2] * at_k * at_k)
            exponents.append(row + at_j * (scale * by_j + 2.0 * scale * m[1, 2] * at_k + scale * m[1, 1] * at_j))
        blocks = jnp.exp2(jnp.concatenate(exponents, 0))
        peak = jnp.where(slots[5] == own, slots[3], 0.0)
        placed = jnp.where(slots[4] == tile_at, 1.0, 0.0).astype(jnp.bfloat16)
        parts = jnp.concatenate(parts_of(blocks * peak), 0)
        sums = bf16_dot(parts, placed, ((1,), (1,)))
        charge.append(sums[0:64] + sums[64:128])
    charge = [charge[b][8 * k : 8 * k + 8] for k in range(8) for b in range(4)]
    charge = [jnp.transpose(jnp.concatenate(charge[16 * n : 16 * n + 16], 0)) for n in range(2)]
    charge = jnp.concatenate(charge, 1)
    for c in range(8):
        piece = jnp.concatenate([bricks[8 * b + c] for b in range(4)], 0)
        cells[128 * c : 128 * c + 128, :] = jnp.transpose(jnp.concatenate([piece] * 4, 0))
    group = index_of((128, 128), 1) >> 5
    sides = []
    for side in range(2):
        total = jnp.zeros((128, 128), jnp.float32)
        for n in range(4):
            total = jnp.where(group == n, cells[pl.ds(4 * side + n, 128, stride=8), :], total)
        sides.append(total)
    field = jnp.concatenate(sides, 1) + charge
    spectrum = applied(z_tile, field)
    re, im = spectrum[:128], spectrum[128:]
    re, im = re * twiddle[0] + im * twiddle[1], im * twiddle[0] - re * twiddle[1]
    even = jnp.concatenate([re[:, :128] + re[:, 128:], im[:, :128] + im[:, 128:]], 1)
    odd = jnp.concatenate([re[:, :128] - re[:, 128:], im[:, :128] - im[:, 128:]], 1)
    out[0:128, :] = times(even, z_even)
    out[128:256, :] = times(odd, z_odd)
    last = jnp.where((lane >> 5) & 1 == 0, even[0:8, 0:128], -even[0:8, 0:128])
    last = last + pltpu.roll(last, 64, 1)
    last = last + pltpu.roll(last, 32, 1)
    here = (index_of((8, 128), 0) == 0) & ((lane >> 5) == 1)
    out[0:8, :] = jnp.where(here, last, out[0:8, :])


def own_rank():
    return (lax.axis_index("gx") * 4 + lax.axis_index("gy")) * 8 + lax.axis_index("gz")


def eigenvalues(column, by_ky, by_kz):
    rank = own_rank()
    mine = by_kz[pl.ds(rank, 1), :]
    field = index_of((1, 256), 1) >> 6
    second, first = [
        jnp.where(field == 0, mine[:, n : n + 1], jnp.where(field == 1, mine[:, n + 2 : n + 3], mine[:, n + 4 : n + 5]))
        for n in range(2)
    ]
    row = by_ky[0:1, :] + second + by_ky[1:2, :] * first
    other = by_ky[2:3, :] + (2.0 * INVERSE[0, 2] / JACOBI_SCALE) * first
    return column[:, 0:1] + row + column[:, 1:2] * other, rank


def weights_of(rank):
    field = index_of((1, 256), 1) >> 6
    first = jnp.where(field == 1, 2.0, jnp.where(field == 3, 0.0, 1.0))
    other = jnp.where(field < 2, 2.0, 0.0)
    return jnp.where(rank == 0, first, other)


def plane_kernel(got, y, x_even, x_odd, column, by_ky, by_kz, nodes, out_re, out_im, out_a, out):
    lam, rank = eigenvalues(column, by_ky, by_kz)
    first = jnp.where(rank == 0, 1.0, 0.0).astype(jnp.float32)
    halves = [jnp.concatenate([got[32 * a + 16 * h : 32 * a + 16 * h + 16, :] for a in range(8)], 0) for h in range(2)]
    lines = times(jnp.concatenate(halves, 1), y)
    even = applied(x_even, jnp.concatenate([lines[:64, n : n + 256] + lines[64:, n : n + 256] for n in (0, 256)], 0))
    odd = applied(x_odd, jnp.concatenate([lines[:64, n : n + 256] - lines[64:, n : n + 256] for n in (0, 256)], 0))
    re, im = [jnp.concatenate([even[n : n + 64], odd[n : n + 64]], 0) for n in (0, 64)]
    re, im = (
        jnp.concatenate([re[:, :128] + first * im[:, 128:], re[:, 128:]], 1),
        jnp.concatenate([im[:, :128] - first * re[:, 128:], im[:, 128:]], 1),
    )
    out_re[...] = re
    out_im[...] = im
    a = STEP * lam
    out_a[...] = a
    power = (re * re + im * im) * weights_of(rank) * a
    double = a * (4.0 / LARGEST) - 2.0
    moments = [power, 0.5 * double * power]
    while len(moments) < NODES:
        moments.append(double * moments[-1] - moments[-2])
    weight = jnp.sum(sums_of(moments) * nodes[0:NODES, :], axis=0, keepdims=True)
    out[...] = jnp.broadcast_to(weight, (256, 128))


def cycle_kernel(got, re_in, im_in, a_in, nodes, x_even_back, x_odd_back, y_back, out):
    weight = jnp.sum(got[...], axis=0, keepdims=True)
    node = nodes[NODES : NODES + 1, :]
    fine = a_in[...]
    first = jnp.where(own_rank() == 0, 1.0, 0.0).astype(jnp.float32)
    sides = [(node, 1.0 - node), (fine, 1.0 - fine)]
    scaled, potential = [1.0, 1.0], 0.0
    for cycle in range(3):
        a, mu = sides[0]
        low = weight * scaled[0] * scaled[0]
        products = [low * a, low * a * mu, low * a * mu * mu, -low * mu * mu, -low * mu * mu * mu]
        g0, g1 = solve([jnp.sum(p, axis=1, keepdims=True) for p in products])
        a, mu = sides[1]
        potential = potential + STEP * scaled[1] * (1.0 + mu * ((1.0 - g0) + (1.0 - g1) * mu))
        if cycle < 2:
            scaled = [s * mu * (mu * mu + a * (g0 + mu * g1)) for s, (a, mu) in zip(scaled, sides)]
    residual = JACOBI_SCALE * scaled[1] * mu * mu
    re, im = re_in[...], im_in[...]
    columns = []
    for multiplier in (potential, residual):
        fr, fi = multiplier * re, multiplier * im
        columns.append(
            jnp.concatenate([fr[:, :128] - first * fi[:, 128:], fi[:, :128] + first * fr[:, 128:]], 0)
        )
    columns = jnp.concatenate(columns, 1)
    low = jnp.concatenate([columns[n : n + 32] for n in range(0, 256, 64)], 0)
    high = jnp.concatenate([columns[n + 32 : n + 64] for n in range(0, 256, 64)], 0)
    planes = jnp.concatenate([applied(x_even_back, low + high), applied(x_odd_back, low - high)], 0)
    lines = []
    for f in range(2):
        for odd in range(2):
            at = 128 * odd
            pair = [planes[at + n : at + n + 64, 128 * f : 128 * f + 128] for n in (0, 64)]
            lines.append(jnp.concatenate(pair, 1))
    lines = times(jnp.concatenate(lines, 0), y_back)
    left = index_of((64, 128), 1) < 64
    for f in range(2):
        for b in range(4):
            side = slice(128 * (b // 2), 128 * (b // 2) + 128)
            even, odd = lines[128 * f : 128 * f + 64, side], lines[128 * f + 64 : 128 * f + 128, side]
            if b % 2 == 0:
                odd = pltpu.roll(odd, 64, 1)
            else:
                even = pltpu.roll(even, 64, 1)
            message = jnp.where(left, even, odd)
            for n in range(8):
                out[pl.ds((32 * n + 8 * b) * 2 + f, 8, stride=2), :] = message[8 * n : 8 * n + 8]


def back_kernel(got, z_tile_back, twiddle, z_even_back, z_odd_back, z_last_back, out, cells):
    spectra = [got[pl.ds(f, 256, stride=2), :] for f in range(2)]
    low = jnp.concatenate([v[:128] for v in spectra], 0)
    high = jnp.concatenate([v[128:] for v in spectra], 0)
    top = index_of((256, 128), 0) & 127 == 0
    part = (index_of((256, 128), 1) & 63) >> 4
    last = jnp.where(top & (part == 1), low, 0.0)
    low = jnp.where(top & (part < 2), jnp.where(part == 0, 0.5 * low, 0.0), low)
    last = times(jnp.concatenate([last[0:8], last[128:136]], 0), z_last_back)
    even, odd = times(low, z_even_back), times(high, z_odd_back)
    turned = []
    for f in range(2):
        e, o = even[128 * f : 128 * f + 128], odd[128 * f : 128 * f + 128]
        real = jnp.concatenate([e[0:8, :128] + last[8 * f : 8 * f + 8], e[8:, :128]], 0)
        re = jnp.concatenate([real + o[:, :128], real - o[:, :128]], 1)
        im = jnp.concatenate([e[:, 128:] + o[:, 128:], e[:, 128:] - o[:, 128:]], 1)
        turned.append(
            jnp.concatenate([re * twiddle[0] - im * twiddle[1], im * twiddle[0] + re * twiddle[1]], 0)
        )
    fields = applied(z_tile_back, jnp.concatenate(turned, 1))
    group = index_of((128, 128), 1) >> 5
    for side in range(2):
        one = fields[:, 128 * side : 128 * side + 128]
        two = pltpu.roll(fields[:, 256 + 128 * side : 384 + 128 * side], 64, 1)
        for n in range(4):
            cells[pl.ds(4 * side + n, 128, stride=8), :] = jnp.where(group == n, one, two)
    turn = index_of((32, 128), 1) & 3
    for c in range(8):
        piece = jnp.transpose(cells[128 * c : 128 * c + 128, :])
        rows = [piece[32 * n : 32 * n + 32] for n in range(4)]
        for f in range(2):
            low = jnp.where(turn == 0, rows[2 * f], rows[(2 * f + 1) % 4])
            high = jnp.where(turn == 2, rows[(2 * f + 2) % 4], rows[(2 * f + 3) % 4])
            out[c, 32 * f : 32 * f + 32, :] = jnp.where(turn < 2, low, high)


def place_kernel(got, potential, residual, done):
    copies = [
        pltpu.make_async_copy(got.at[:, f], out, done.at[f]) for f, out in enumerate((potential, residual))
    ]
    for copy in copies:
        copy.start()
    for copy in copies:
        copy.wait()


VMEM = pl.BlockSpec(memory_space=pltpu.VMEM)
HBM = pl.BlockSpec(memory_space=pltpu.HBM)
SMEM = pl.BlockSpec(memory_space=pltpu.SMEM)


def call(kernel, out_shapes, specs, scratch=(), name=None, result=VMEM, limit=16, cost=None):
    shapes = [jax.ShapeDtypeStruct(s, jnp.float32) for s in out_shapes]
    single = len(shapes) == 1
    return pl.pallas_call(
        kernel,
        out_shape=shapes[0] if single else shapes,
        in_specs=specs,
        out_specs=result if single else [result] * len(shapes),
        scratch_shapes=list(scratch),
        compiler_params=pltpu.CompilerParams(vmem_limit_bytes=limit * 1024 * 1024),
        name=name,
        cost_estimate=cost and pl.CostEstimate(flops=cost, bytes_accessed=cost, transcendentals=0),
    )


def exchanged(array, axes):
    return lax.all_to_all(array, axes, 0, 0, tiled=True)


def per_device(density, atom_site, atom_charge, slot_atom, slot_tile, slot_shift):
    t = {name: jnp.asarray(value) for name, value in tables().items()}
    packed = call(slots_kernel, [(8, 128)], [VMEM] * 6, name="slots")(
        call(blank_kernel, [(8, 128)], [], name="blank", cost=10**8)(),
        atom_site.reshape(3, 1, 16),
        atom_charge.reshape(1, 16),
        slot_atom.reshape(32, 2).T,
        slot_tile.reshape(32, 2).T,
        jnp.swapaxes(slot_shift.reshape(3, 32, 2), 1, 2),
    )
    message = call(send_kernel, [(384, 128)], [VMEM] * 2, name="send")(density, packed)
    got = exchanged(message.reshape(32, 1, 1536), ("gy", "gz")).reshape(384, 128)
    cells = [pltpu.VMEM((1024, 128), jnp.float32)]
    message = call(line_kernel, [(256, 128)], [VMEM] * 5, cells, "line")(
        got, t["z_tile"], t["twiddle"], t["z_even"], t["z_odd"]
    )
    got = exchanged(message, AXES)
    re, im, a, message = call(plane_kernel, [(128, 256)] * 3 + [(256, 128)], [VMEM] * 8, name="plane")(
        got, t["y"], t["x_even"], t["x_odd"], t["column"], t["by_ky"], t["by_kz"], t["nodes"]
    )
    got = exchanged(message, AXES)
    message = call(cycle_kernel, [(512, 128)], [VMEM] * 8, name="cycle")(
        got, re, im, a, t["nodes"], t["x_even_back"], t["x_odd_back"], t["y_back"]
    )
    got = exchanged(message.reshape(256, 2, 128), AXES).reshape(512, 128)
    message = call(back_kernel, [(8, 64, 128)], [VMEM] * 6, cells, "back")(
        got, t["z_tile_back"], t["twiddle"], t["z_even_back"], t["z_odd_back"], t["z_last_back"]
    )
    got = exchanged(message, "gz").reshape(8, 2, 2, 16, 128)
    place = call(place_kernel, [(8, 2, 16, 128)] * 2, [VMEM], [pltpu.SemaphoreType.DMA((2,))], "place", HBM)
    return tuple(out.reshape(16, 16, 128) for out in place(got))


def solution(mesh):
    return jax.shard_map(
        per_device,
        mesh=mesh,
        in_specs=(
            P("gx", "gy", "gz"),
            P(None, "gx", "gy", "gz", None),
            P("gx", "gy", "gz", None),
            P("gx", "gy", "gz", None, None),
            P("gx", "gy", "gz", None, None),
            P(None, "gx", "gy", "gz", None, None),
        ),
        out_specs=(P("gx", "gy", "gz"), P("gx", "gy", "gz")),
        check_vma=False,
    )
```

```python
import functools

import jax
import jax.numpy as jnp
import ml_dtypes
import numpy as np
from jax import lax
from jax.experimental import pallas as pl
from jax.experimental.pallas import tpu as pltpu
from jax.sharding import PartitionSpec as P


METRIC = np.array([[3.24, 0.972, 0.648], [0.972, 3.2157, 0.9639], [0.648, 0.9639, 2.9565]])
INVERSE = np.array(
    [
        [0.3450043297, -0.0904572938, -0.0461258313],
        [-0.0904572938, 0.3683733435, -0.1002735462],
        [-0.0461258313, -0.1002735462, 0.3810394757],
    ]
)
FIRST_WEIGHTS = np.array([6.0 / 7.0, -15.0 / 56.0, 5.0 / 63.0, -1.0 / 56.0, 2.0 / 385.0, -1.0 / 5544.0])
SECOND_WEIGHTS = 2.0 * FIRST_WEIGHTS / np.arange(1, 7)
CENTER_WEIGHT = -2.0 * SECOND_WEIGHTS.sum()
JACOBI_SCALE = float(-CENTER_WEIGHT * np.trace(INVERSE))
STEP = 0.3
WIDTH_SQUARED = 9.0
RIDGE_SHARE = 0.01
NX, NY, NZ = 128, 64, 1024
AXES = ("gx", "gy", "gz")
LOG2E = float(np.log2(np.e))
NODES = 16
LARGEST = STEP * 2.3721


def cos_sin(n, rows, columns):
    angle = 2.0 * np.pi * (np.outer(rows, columns) % n) / n
    return np.cos(angle), np.sin(angle)


def first_symbol(n):
    angle = 2.0 * np.pi * np.arange(n) / n
    return 2.0 * sum(w * np.sin((o + 1) * angle) for o, w in enumerate(FIRST_WEIGHTS))


def second_symbol(n):
    angle = 2.0 * np.pi * np.arange(n) / n
    return CENTER_WEIGHT + 2.0 * sum(w * np.cos((o + 1) * angle) for o, w in enumerate(SECOND_WEIGHTS))


def halves_of(table):
    high = table.astype(ml_dtypes.bfloat16)
    return high, (table - high.astype(np.float64)).astype(ml_dtypes.bfloat16)


ON_THE_RIGHT = ("z_even", "z_odd", "y", "y_back", "z_even_back", "z_odd_back", "z_last_back")
ON_THE_LEFT = ("z_tile", "x_even", "x_odd", "x_even_back", "x_odd_back", "z_tile_back")


@functools.lru_cache(maxsize=None)
def tables():
    eye = np.eye(32)
    freq = np.arange(128)
    c, s = cos_sin(128, freq, freq)
    t = {}
    t["z_tile"] = np.concatenate([c, -s], 0) / 32.0 / JACOBI_SCALE
    t["z_tile_back"] = np.concatenate([c, -s], 1) / 32.0
    t["twiddle"] = np.stack(cos_sin(1024, freq, np.arange(256) // 32))
    c, s = cos_sin(8, np.arange(4), np.arange(4))
    half_eye = np.eye(16)
    for odd, name in enumerate(("z_even", "z_odd")):
        ahead = np.zeros((2, 4, 32, 2, 2, 32))
        back = np.zeros((2, 2, 2, 16, 2, 4, 2, 16))
        for k in range(4):
            for n in range(2):
                cc, ss = c[k, 2 * n + odd], s[k, 2 * n + odd]
                ahead[0, k, :, n, 0], ahead[1, k, :, n, 0] = cc * eye, ss * eye
                ahead[0, k, :, n, 1], ahead[1, k, :, n, 1] = -ss * eye, cc * eye
                for x in range(2):
                    back[x, n, 0, :, 0, k, x], back[x, n, 1, :, 0, k, x] = 2.0 * cc * half_eye, -2.0 * ss * half_eye
                    back[x, n, 0, :, 1, k, x], back[x, n, 1, :, 1, k, x] = 2.0 * ss * half_eye, 2.0 * cc * half_eye
        t[name], t[name + "_back"] = ahead.reshape(256, 128), back.reshape(128, 256)
    last = np.zeros((2, 2, 2, 16, 4, 2, 16))
    for k in range(4):
        for x in range(2):
            last[x, 0, 1, :, k, x] = (-1.0) ** k * half_eye
    t["z_last_back"] = last.reshape(128, 128)
    half, b, j = np.meshgrid(np.arange(2), np.arange(4), np.arange(8), indexing="ij")
    c, s = cos_sin(64, (16 * b + 8 * half + j).reshape(-1), np.arange(64))
    c, s = c.reshape(2, 4, 8, 64) / 8.0, s.reshape(2, 4, 8, 64) / 8.0
    ahead = np.zeros((2, 2, 2, 4, 8, 2, 4, 64))
    for f in range(2):
        ahead[:, f, 0, :, :, 0, f], ahead[:, f, 1, :, :, 0, f] = c, s
        ahead[:, f, 0, :, :, 1, f], ahead[:, f, 1, :, :, 1, f] = -s, c
    ahead[:, 0, 1, :, :, 0, 2], ahead[:, 0, 1, :, :, 1, 2] = c, -s
    t["y"] = ahead.reshape(256, 512)
    c, s = cos_sin(64, np.arange(64), np.arange(64))
    c, s = c.reshape(64, 4, 16) / 8.0, s.reshape(64, 4, 16) / 8.0
    back = np.zeros((2, 2, 64, 4, 2, 2, 16))
    for f in range(2):
        back[0, f, :, :, f, 0], back[1, f, :, :, f, 0] = c, -s
        back[0, f, :, :, f, 1], back[1, f, :, :, f, 1] = s, c
    t["y_back"] = back.reshape(256, 256)
    short = np.arange(64)
    some = np.concatenate([2 * short[:32], 2 * short[:32] + 1])
    for odd, name in enumerate(("x_even", "x_odd")):
        c, s = cos_sin(128, 2 * short + odd, short)
        t[name] = np.block([[c, s], [-s, c]]) / np.sqrt(128.0)
        c, s = cos_sin(128, 2 * short + odd, some)
        t[name + "_back"] = np.block([[c, -s], [s, c]]) / np.sqrt(128.0)
    d1x, d1y, d1z = first_symbol(NX), first_symbol(NY), first_symbol(NZ)
    d2x, d2y, d2z = second_symbol(NX), second_symbol(NY), second_symbol(NZ)
    column = np.zeros((128, 128))
    by_row = np.concatenate([2 * short, 2 * short + 1])
    column[:, 0], column[:, 1] = -INVERSE[0, 0] * d2x[by_row] / JACOBI_SCALE, d1x[by_row]
    by_ky = np.zeros((8, 256))
    by_ky[0] = np.tile(-INVERSE[1, 1] * d2y / JACOBI_SCALE, 4)
    by_ky[1] = np.tile(2.0 * INVERSE[1, 2] * d1y / JACOBI_SCALE, 4)
    by_ky[2] = np.tile(2.0 * INVERSE[0, 1] * d1y / JACOBI_SCALE, 4)
    by_kz = np.zeros((256, 128))
    low = np.arange(256)
    for f, kz in enumerate((low, low + 256, 0 * low + 512)):
        by_kz[:, 2 * f], by_kz[:, 2 * f + 1] = -INVERSE[2, 2] * d2z[kz] / JACOBI_SCALE, d1z[kz]
    t["column"], t["by_ky"], t["by_kz"] = column, by_ky, by_kz
    angle = (np.arange(NODES) + 0.5) * np.pi / NODES
    nodes = np.zeros((24, 128))
    nodes[:NODES, :NODES] = 2.0 / NODES * np.cos(np.outer(np.arange(NODES), angle))
    nodes[0, :NODES] = 1.0 / NODES
    nodes[NODES, :NODES] = 0.5 * LARGEST * (1.0 + np.cos(angle))
    t["nodes"] = nodes
    for name in ON_THE_RIGHT:
        high, low = halves_of(t[name])
        t[name] = np.concatenate([high, low], 0)
    for name in ON_THE_LEFT:
        high, low = halves_of(t[name])
        t[name] = np.concatenate([high, low], 1)
    return {n: v if v.dtype == ml_dtypes.bfloat16 else v.astype(np.float32) for n, v in t.items()}


def index_of(shape, dim):
    return lax.broadcasted_iota(jnp.int32, shape, dim)


def solve(gram):
    ff, fc, cc, fs, cs = gram
    ridge = RIDGE_SHARE * 0.5 * (ff + cc)
    ff, cc = ff + ridge, cc + ridge
    determinant = ff * cc - fc * fc
    return (cc * fs - fc * cs) / determinant, (ff * cs - fc * fs) / determinant


def stack_rows(rows, count):
    at = index_of((count, 128), 0)
    stacked = jnp.zeros((count, 128), jnp.float32)
    for n, row in enumerate(rows):
        stacked = jnp.where(at == n, row, stacked)
    return stacked


def sums_of(arrays):
    rows = []
    for array in arrays:
        row = jnp.sum(array, axis=0, keepdims=True)
        rows.append(row[:, :128] + row[:, 128:])
    count = -(-len(rows) // 8) * 8
    return jnp.sum(stack_rows(rows, count), axis=1, keepdims=True)


def parts_of(array):
    high = array.astype(jnp.bfloat16)
    return high, (array - high.astype(jnp.float32)).astype(jnp.bfloat16)


def bf16_dot(a, b, contract=((1,), (0,))):
    return lax.dot_general(a, b, (contract, ((), ())), preferred_element_type=jnp.float32)


def in_two(array, axis):
    high, low = parts_of(array)
    return jnp.concatenate([high, high, low], axis)


def times(data, table):
    return bf16_dot(in_two(data, 1), jnp.concatenate([table[...], table[0 : table.shape[0] // 2, :]], 0))


def applied(table, data):
    return bf16_dot(jnp.concatenate([table[...], table[:, 0 : table.shape[1] // 2]], 1), in_two(data, 0))


def blank_kernel(out):
    out[...] = jnp.zeros((8, 128), jnp.float32)


def slots_kernel(blank, site, charge, atom, tile, shift, out):
    wide = jnp.concatenate([atom[...], jnp.zeros((2, 96), jnp.int32)], 1)
    wide = jnp.concatenate([wide, jnp.zeros((6, 128), jnp.int32)], 0)
    values = []
    for row in [site[0], site[1], site[2], charge[...]]:
        row = jnp.broadcast_to(jnp.concatenate([row, jnp.zeros((1, 112), jnp.float32)], 1), (8, 128))
        chosen = jnp.take_along_axis(row, wide, axis=1, mode="promise_in_bounds")
        values.append(chosen[0:2, 0:32])
    for p in range(3):
        values[p] = values[p] + 4.0 * shift[p].astype(jnp.float32)
    code = tile[...]
    values.append(((code & 15) + 16 * (index_of((2, 32), 1) & 7)).astype(jnp.float32))
    values.append((code >> 4).astype(jnp.float32))
    ux, uy, uz, peak, at, side = values
    nothing = jnp.zeros((2, 32), jnp.float32)
    ordered = [ux, uz, at, nothing, uy, peak, side, nothing]
    lane = index_of((8, 128), 1)
    packed = blank[...]
    for e in range(2):
        rows = [jnp.concatenate([v[e : e + 1], jnp.zeros((1, 96), jnp.float32)], 1) for v in ordered]
        rows = stack_rows(rows, 8)
        for b in range(4):
            moved = pltpu.roll(rows, 8 * b + 8 * e, 1)
            packed = jnp.where((lane >> 3) == 2 * b + e, moved, packed)
    packed = jnp.where(lane < 64, packed, pltpu.roll(pltpu.roll(packed, 4, 0), 64, 1))
    packed = jnp.where(index_of((8, 128), 0) < 4, packed, pltpu.roll(packed, 4, 0))
    place = ((lax.axis_index("gy") * 8 + lax.axis_index("gz")) >> 1) & 7
    out[...] = pltpu.roll(packed, 16 * place, 1)


def send_kernel(density, packed, out):
    above = index_of((8, 128), 0) < 4
    slots = packed[...]
    for n in range(16):
        half, x = n // 8, 2 * n % 16
        even, odd = [density[x + m, 8 * half : 8 * half + 8, :] for m in range(2)]
        odd = pltpu.roll(odd, 4, 0)
        out[24 * n : 24 * n + 8, :] = even
        out[24 * n + 8 : 24 * n + 16, :] = jnp.where(above, slots, odd)
        out[24 * n + 16 : 24 * n + 24, :] = jnp.where(above, odd, slots)


def line_kernel(got, z_tile, twiddle, z_even, z_odd, out, cells):
    rank = lax.axis_index("gy") * 8 + lax.axis_index("gz")
    x, half = rank & 15, rank >> 4
    own = ((x >> 3) * 2 + half).astype(jnp.float32)
    along = (x & 7).astype(jnp.float32)
    lane = index_of((8, 128), 1)
    at_j = index_of((8, 512), 0).astype(jnp.float32) - 3.5
    tile_at = index_of((128, 512), 0).astype(jnp.float32)
    scale = -LOG2E / WIDTH_SQUARED
    crossed = [jnp.exp2(2.0 * scale * METRIC[1, 2] * (k - 3.5) * at_j) for k in range(8)]
    above = index_of((8, 128), 0) < 4
    bricks, pairs = [], []
    for n in range(16):
        middle, last = got[24 * n + 8 : 24 * n + 16, :], got[24 * n + 16 : 24 * n + 24, :]
        bricks += [got[24 * n : 24 * n + 8, :], pltpu.roll(jnp.where(above, last, middle), 4, 0)]
        pairs.append(jnp.where(above, middle, last))
    charge = []
    for b in range(4):
        sides = []
        for side in range(2):
            parts = []
            for g in range(2):
                part = jnp.zeros((8, 128), jnp.float32)
                for r in range(8):
                    part = jnp.where((lane >> 4) == (r + b + 4 * side) % 8, pairs[8 * g + r], part)
                parts.append(pltpu.roll(part, 64, 1) if side else part)
            parts += [pltpu.roll(part, 4, 0) for part in parts]
            sides.append(jnp.concatenate(parts, 1))
        one, two = sides
        slots = [one[0:1], two[0:1], one[1:2], two[1:2], one[2:3], two[2:3]]
        ex = along - slots[0]
        vy, vz = slots[1] - 3.5, slots[2] - 3.5
        m = METRIC
        fixed = m[0, 0] * ex * ex + m[1, 1] * vy * vy + m[2, 2] * vz * vz
        fixed = fixed - 2.0 * m[0, 1] * ex * vy - 2.0 * m[0, 2] * ex * vz + 2.0 * m[1, 2] * vy * vz
        by_j = -2.0 * m[1, 1] * vy + 2.0 * m[0, 1] * ex - 2.0 * m[1, 2] * vz
        by_k = -2.0 * m[2, 2] * vz + 2.0 * m[0, 2] * ex - 2.0 * m[1, 2] * vy
        peak = jnp.where(slots[5] == own, slots[3], 0.0)
        by_row = peak * jnp.exp2(scale * (fixed + at_j * by_k + m[2, 2] * at_j * at_j))
        by_cell = jnp.exp2(scale * at_j * (by_j + m[1, 1] * at_j))
        blocks = jnp.concatenate([by_row[k : k + 1] * (by_cell * crossed[k]) for k in range(8)], 0)
        placed = jnp.where(slots[4] == tile_at, 1.0, 0.0).astype(jnp.bfloat16)
        parts = jnp.concatenate(parts_of(blocks), 0)
        sums = bf16_dot(parts, placed, ((1,), (1,)))
        charge.append(sums[0:64] + sums[64:128])
    charge = [charge[b][8 * k : 8 * k + 8] for k in range(8) for b in range(4)]
    charge = [jnp.transpose(jnp.concatenate(charge[16 * n : 16 * n + 16], 0)) for n in range(2)]
    charge = jnp.concatenate(charge, 1)
    for c in range(8):
        piece = jnp.concatenate([bricks[8 * b + c] for b in range(4)], 0)
        cells[128 * c : 128 * c + 128, :] = jnp.transpose(jnp.concatenate([piece] * 4, 0))
    group = index_of((128, 128), 1) >> 5
    sides = []
    for side in range(2):
        total = jnp.zeros((128, 128), jnp.float32)
        for n in range(4):
            total = jnp.where(group == n, cells[pl.ds(4 * side + n, 128, stride=8), :], total)
        sides.append(total)
    field = jnp.concatenate(sides, 1) + charge
    spectrum = applied(z_tile, field)
    re, im = spectrum[:128], spectrum[128:]
    re, im = re * twiddle[0] + im * twiddle[1], im * twiddle[0] - re * twiddle[1]
    even = jnp.concatenate([re[:, :128] + re[:, 128:], im[:, :128] + im[:, 128:]], 1)
    odd = jnp.concatenate([re[:, :128] - re[:, 128:], im[:, :128] - im[:, 128:]], 1)
    out[0:128, :] = times(even, z_even)
    out[128:256, :] = times(odd, z_odd)
    last = jnp.where((lane >> 5) & 1 == 0, even[0:8, 0:128], -even[0:8, 0:128])
    last = last + pltpu.roll(last, 64, 1)
    last = last + pltpu.roll(last, 32, 1)
    here = (index_of((8, 128), 0) == 0) & ((lane >> 5) == 1)
    out[0:8, :] = jnp.where(here, last, out[0:8, :])


def own_rank():
    return (lax.axis_index("gx") * 4 + lax.axis_index("gy")) * 8 + lax.axis_index("gz")


def eigenvalues(column, by_ky, by_kz):
    rank = own_rank()
    mine = by_kz[pl.ds(rank, 1), :]
    field = index_of((1, 256), 1) >> 6
    second, first = [
        jnp.where(field == 0, mine[:, n : n + 1], jnp.where(field == 1, mine[:, n + 2 : n + 3], mine[:, n + 4 : n + 5]))
        for n in range(2)
    ]
    row = by_ky[0:1, :] + second + by_ky[1:2, :] * first
    other = by_ky[2:3, :] + (2.0 * INVERSE[0, 2] / JACOBI_SCALE) * first
    return column[:, 0:1] + row + column[:, 1:2] * other, rank


def weights_of(rank):
    field = index_of((1, 256), 1) >> 6
    first = jnp.where(field == 1, 2.0, jnp.where(field == 3, 0.0, 1.0))
    other = jnp.where(field < 2, 2.0, 0.0)
    return jnp.where(rank == 0, first, other)


def plane_kernel(got, y, x_even, x_odd, column, by_ky, by_kz, nodes, out_re, out_im, out_a, out):
    lam, rank = eigenvalues(column, by_ky, by_kz)
    first = jnp.where(rank == 0, 1.0, 0.0).astype(jnp.float32)
    halves = [jnp.concatenate([got[32 * a + 16 * h : 32 * a + 16 * h + 16, :] for a in range(8)], 0) for h in range(2)]
    lines = times(jnp.concatenate(halves, 1), y)
    even = applied(x_even, jnp.concatenate([lines[:64, n : n + 256] + lines[64:, n : n + 256] for n in (0, 256)], 0))
    odd = applied(x_odd, jnp.concatenate([lines[:64, n : n + 256] - lines[64:, n : n + 256] for n in (0, 256)], 0))
    re, im = [jnp.concatenate([even[n : n + 64], odd[n : n + 64]], 0) for n in (0, 64)]
    re, im = (
        jnp.concatenate([re[:, :128] + first * im[:, 128:], re[:, 128:]], 1),
        jnp.concatenate([im[:, :128] - first * re[:, 128:], im[:, 128:]], 1),
    )
    out_re[...] = re
    out_im[...] = im
    a = STEP * lam
    out_a[...] = a
    power = (re * re + im * im) * weights_of(rank) * a
    double = a * (4.0 / LARGEST) - 2.0
    moments = [power, 0.5 * double * power]
    while len(moments) < NODES:
        moments.append(double * moments[-1] - moments[-2])
    weight = jnp.sum(sums_of(moments) * nodes[0:NODES, :], axis=0, keepdims=True)
    out[...] = jnp.broadcast_to(weight, (256, 128))


def cycle_kernel(got, re_in, im_in, a_in, nodes, x_even_back, x_odd_back, y_back, out):
    weight = jnp.sum(got[...], axis=0, keepdims=True)
    node = nodes[NODES : NODES + 1, :]
    fine = a_in[...]
    first = jnp.where(own_rank() == 0, 1.0, 0.0).astype(jnp.float32)
    sides = [(node, 1.0 - node), (fine, 1.0 - fine)]
    scaled, potential = [1.0, 1.0], 0.0
    for cycle in range(3):
        a, mu = sides[0]
        low = weight * scaled[0] * scaled[0]
        products = [low * a, low * a * mu, low * a * mu * mu, -low * mu * mu, -low * mu * mu * mu]
        g0, g1 = solve([jnp.sum(p, axis=1, keepdims=True) for p in products])
        a, mu = sides[1]
        potential = potential + STEP * scaled[1] * (1.0 + mu * ((1.0 - g0) + (1.0 - g1) * mu))
        if cycle < 2:
            scaled = [s * mu * (mu * mu + a * (g0 + mu * g1)) for s, (a, mu) in zip(scaled, sides)]
    residual = JACOBI_SCALE * scaled[1] * mu * mu
    re, im = re_in[...], im_in[...]
    columns = []
    for multiplier in (potential, residual):
        fr, fi = multiplier * re, multiplier * im
        columns.append(
            jnp.concatenate([fr[:, :128] - first * fi[:, 128:], fi[:, :128] + first * fr[:, 128:]], 0)
        )
    columns = jnp.concatenate(columns, 1)
    low = jnp.concatenate([columns[n : n + 32] for n in range(0, 256, 64)], 0)
    high = jnp.concatenate([columns[n + 32 : n + 64] for n in range(0, 256, 64)], 0)
    planes = jnp.concatenate([applied(x_even_back, low + high), applied(x_odd_back, low - high)], 0)
    lines = []
    for f in range(2):
        for odd in range(2):
            at = 128 * odd
            pair = [planes[at + n : at + n + 64, 128 * f : 128 * f + 128] for n in (0, 64)]
            lines.append(jnp.concatenate(pair, 1))
    lines = times(jnp.concatenate(lines, 0), y_back)
    left = index_of((64, 128), 1) < 64
    for f in range(2):
        for b in range(4):
            side = slice(128 * (b // 2), 128 * (b // 2) + 128)
            even, odd = lines[128 * f : 128 * f + 64, side], lines[128 * f + 64 : 128 * f + 128, side]
            if b % 2 == 0:
                odd = pltpu.roll(odd, 64, 1)
            else:
                even = pltpu.roll(even, 64, 1)
            message = jnp.where(left, even, odd)
            for n in range(8):
                out[pl.ds((32 * n + 8 * b) * 2 + f, 8, stride=2), :] = message[8 * n : 8 * n + 8]


def back_kernel(got, z_tile_back, twiddle, z_even_back, z_odd_back, z_last_back, out, cells):
    spectra = [got[pl.ds(f, 256, stride=2), :] for f in range(2)]
    low = jnp.concatenate([v[:128] for v in spectra], 0)
    high = jnp.concatenate([v[128:] for v in spectra], 0)
    top = index_of((256, 128), 0) & 127 == 0
    part = (index_of((256, 128), 1) & 63) >> 4
    last = jnp.where(top & (part == 1), low, 0.0)
    low = jnp.where(top & (part < 2), jnp.where(part == 0, 0.5 * low, 0.0), low)
    last = times(jnp.concatenate([last[0:8], last[128:136]], 0), z_last_back)
    even, odd = times(low, z_even_back), times(high, z_odd_back)
    turned = []
    for f in range(2):
        e, o = even[128 * f : 128 * f + 128], odd[128 * f : 128 * f + 128]
        real = jnp.concatenate([e[0:8, :128] + last[8 * f : 8 * f + 8], e[8:, :128]], 0)
        re = jnp.concatenate([real + o[:, :128], real - o[:, :128]], 1)
        im = jnp.concatenate([e[:, 128:] + o[:, 128:], e[:, 128:] - o[:, 128:]], 1)
        turned.append(
            jnp.concatenate([re * twiddle[0] - im * twiddle[1], im * twiddle[0] + re * twiddle[1]], 0)
        )
    fields = applied(z_tile_back, jnp.concatenate(turned, 1))
    group = index_of((128, 128), 1) >> 5
    for side in range(2):
        one = fields[:, 128 * side : 128 * side + 128]
        two = pltpu.roll(fields[:, 256 + 128 * side : 384 + 128 * side], 64, 1)
        for n in range(4):
            cells[pl.ds(4 * side + n, 128, stride=8), :] = jnp.where(group == n, one, two)
    turn = index_of((32, 128), 1) & 3
    for c in range(8):
        piece = jnp.transpose(cells[128 * c : 128 * c + 128, :])
        rows = [piece[32 * n : 32 * n + 32] for n in range(4)]
        for f in range(2):
            low = jnp.where(turn == 0, rows[2 * f], rows[(2 * f + 1) % 4])
            high = jnp.where(turn == 2, rows[(2 * f + 2) % 4], rows[(2 * f + 3) % 4])
            out[c, 32 * f : 32 * f + 32, :] = jnp.where(turn < 2, low, high)


def place_kernel(got, potential, residual, done):
    copies = [
        pltpu.make_async_copy(got.at[:, f], out, done.at[f]) for f, out in enumerate((potential, residual))
    ]
    for copy in copies:
        copy.start()
    for copy in copies:
        copy.wait()


VMEM = pl.BlockSpec(memory_space=pltpu.VMEM)
HBM = pl.BlockSpec(memory_space=pltpu.HBM)
SMEM = pl.BlockSpec(memory_space=pltpu.SMEM)


def call(kernel, out_shapes, specs, scratch=(), name=None, result=VMEM, limit=16, cost=None):
    shapes = [jax.ShapeDtypeStruct(s, jnp.float32) for s in out_shapes]
    single = len(shapes) == 1
    return pl.pallas_call(
        kernel,
        out_shape=shapes[0] if single else shapes,
        in_specs=specs,
        out_specs=result if single else [result] * len(shapes),
        scratch_shapes=list(scratch),
        compiler_params=pltpu.CompilerParams(vmem_limit_bytes=limit * 1024 * 1024),
        name=name,
        cost_estimate=cost and pl.CostEstimate(flops=cost, bytes_accessed=cost, transcendentals=0),
    )


def exchanged(array, axes):
    return lax.all_to_all(array, axes, 0, 0, tiled=True)


def per_device(density, atom_site, atom_charge, slot_atom, slot_tile, slot_shift):
    t = {name: jnp.asarray(value) for name, value in tables().items()}
    packed = call(slots_kernel, [(8, 128)], [VMEM] * 6, name="slots")(
        call(blank_kernel, [(8, 128)], [], name="blank", cost=10**8)(),
        atom_site.reshape(3, 1, 16),
        atom_charge.reshape(1, 16),
        slot_atom.reshape(32, 2).T,
        slot_tile.reshape(32, 2).T,
        jnp.swapaxes(slot_shift.reshape(3, 32, 2), 1, 2),
    )
    message = call(send_kernel, [(384, 128)], [VMEM] * 2, name="send")(density, packed)
    got = exchanged(message.reshape(32, 1, 1536), ("gy", "gz")).reshape(384, 128)
    cells = [pltpu.VMEM((1024, 128), jnp.float32)]
    message = call(line_kernel, [(256, 128)], [VMEM] * 5, cells, "line")(
        got, t["z_tile"], t["twiddle"], t["z_even"], t["z_odd"]
    )
    got = exchanged(message, AXES)
    re, im, a, message = call(plane_kernel, [(128, 256)] * 3 + [(256, 128)], [VMEM] * 8, name="plane")(
        got, t["y"], t["x_even"], t["x_odd"], t["column"], t["by_ky"], t["by_kz"], t["nodes"]
    )
    got = exchanged(message, AXES)
    message = call(cycle_kernel, [(512, 128)], [VMEM] * 8, name="cycle")(
        got, re, im, a, t["nodes"], t["x_even_back"], t["x_odd_back"], t["y_back"]
    )
    got = exchanged(message.reshape(256, 2, 128), AXES).reshape(512, 128)
    message = call(back_kernel, [(8, 64, 128)], [VMEM] * 6, cells, "back")(
        got, t["z_tile_back"], t["twiddle"], t["z_even_back"], t["z_odd_back"], t["z_last_back"]
    )
    got = exchanged(message, "gz").reshape(8, 2, 2, 16, 128)
    place = call(place_kernel, [(8, 2, 16, 128)] * 2, [VMEM], [pltpu.SemaphoreType.DMA((2,))], "place", HBM)
    return tuple(out.reshape(16, 16, 128) for out in place(got))


def solution(mesh):
    return jax.shard_map(
        per_device,
        mesh=mesh,
        in_specs=(
            P("gx", "gy", "gz"),
            P(None, "gx", "gy", "gz", None),
            P("gx", "gy", "gz", None),
            P("gx", "gy", "gz", None, None),
            P("gx", "gy", "gz", None, None),
            P(None, "gx", "gy", "gz", None, None),
        ),
        out_specs=(P("gx", "gy", "gz"), P("gx", "gy", "gz")),
        check_vma=False,
    )
```

```python
import functools

import jax
import jax.numpy as jnp
import ml_dtypes
import numpy as np
from jax import lax
from jax.experimental import pallas as pl
from jax.experimental.pallas import tpu as pltpu
from jax.sharding import PartitionSpec as P


METRIC = np.array([[3.24, 0.972, 0.648], [0.972, 3.2157, 0.9639], [0.648, 0.9639, 2.9565]])
INVERSE = np.array(
    [
        [0.3450043297, -0.0904572938, -0.0461258313],
        [-0.0904572938, 0.3683733435, -0.1002735462],
        [-0.0461258313, -0.1002735462, 0.3810394757],
    ]
)
FIRST_WEIGHTS = np.array([6.0 / 7.0, -15.0 / 56.0, 5.0 / 63.0, -1.0 / 56.0, 2.0 / 385.0, -1.0 / 5544.0])
SECOND_WEIGHTS = 2.0 * FIRST_WEIGHTS / np.arange(1, 7)
CENTER_WEIGHT = -2.0 * SECOND_WEIGHTS.sum()
JACOBI_SCALE = float(-CENTER_WEIGHT * np.trace(INVERSE))
STEP = 0.3
WIDTH_SQUARED = 9.0
RIDGE_SHARE = 0.01
NX, NY, NZ = 128, 64, 1024
AXES = ("gx", "gy", "gz")
LOG2E = float(np.log2(np.e))
NODES = 16
LARGEST = STEP * 2.3721


def cos_sin(n, rows, columns):
    angle = 2.0 * np.pi * (np.outer(rows, columns) % n) / n
    return np.cos(angle), np.sin(angle)


def first_symbol(n):
    angle = 2.0 * np.pi * np.arange(n) / n
    return 2.0 * sum(w * np.sin((o + 1) * angle) for o, w in enumerate(FIRST_WEIGHTS))


def second_symbol(n):
    angle = 2.0 * np.pi * np.arange(n) / n
    return CENTER_WEIGHT + 2.0 * sum(w * np.cos((o + 1) * angle) for o, w in enumerate(SECOND_WEIGHTS))


def halves_of(table):
    high = table.astype(ml_dtypes.bfloat16)
    return high, (table - high.astype(np.float64)).astype(ml_dtypes.bfloat16)


ON_THE_RIGHT = ("z_even", "z_odd", "y", "y_back", "z_even_back", "z_odd_back", "z_last_back")
ON_THE_LEFT = ("x_even", "x_odd", "x_even_back", "x_odd_back")
ON_THE_LEFT += ("z_tile_even", "z_tile_odd", "z_tile_back")


@functools.lru_cache(maxsize=None)
def tables():
    eye = np.eye(32)
    freq = np.arange(128)
    short = np.arange(64)
    by_row = np.concatenate([2 * short, 2 * short + 1])
    some = np.concatenate([2 * short[:32], 2 * short[:32] + 1])
    t = {}
    for odd, name in enumerate(("z_tile_even", "z_tile_odd")):
        c, s = cos_sin(128, 2 * short + odd, short)
        t[name] = np.concatenate([c, -s], 0) / 32.0 / JACOBI_SCALE
    c, s = cos_sin(128, freq, by_row)
    t["z_tile_back"] = np.concatenate([c, -s], 1) / 32.0
    t["twiddle"] = np.stack(cos_sin(1024, by_row, np.arange(256) // 32))
    c, s = cos_sin(8, np.arange(4), np.arange(4))
    half_eye = np.eye(16)
    for odd, name in enumerate(("z_even", "z_odd")):
        ahead = np.zeros((2, 4, 32, 2, 2, 32))
        back = np.zeros((2, 2, 2, 16, 2, 4, 2, 16))
        for k in range(4):
            for n in range(2):
                cc, ss = c[k, 2 * n + odd], s[k, 2 * n + odd]
                ahead[0, k, :, n, 0], ahead[1, k, :, n, 0] = cc * eye, ss * eye
                ahead[0, k, :, n, 1], ahead[1, k, :, n, 1] = -ss * eye, cc * eye
                for x in range(2):
                    back[x, n, 0, :, 0, k, x], back[x, n, 1, :, 0, k, x] = 2.0 * cc * half_eye, -2.0 * ss * half_eye
                    back[x, n, 0, :, 1, k, x], back[x, n, 1, :, 1, k, x] = 2.0 * ss * half_eye, 2.0 * cc * half_eye
        t[name], t[name + "_back"] = ahead.reshape(256, 128), back.reshape(128, 256)
    last = np.zeros((2, 2, 2, 16, 4, 2, 16))
    for k in range(4):
        for x in range(2):
            last[x, 0, 1, :, k, x] = (-1.0) ** k * half_eye
    t["z_last_back"] = last.reshape(128, 128)
    half, b, j = np.meshgrid(np.arange(2), np.arange(4), np.arange(8), indexing="ij")
    c, s = cos_sin(64, (16 * b + 8 * half + j).reshape(-1), np.arange(64))
    c, s = c.reshape(2, 4, 8, 64) / 8.0, s.reshape(2, 4, 8, 64) / 8.0
    ahead = np.zeros((2, 2, 2, 4, 8, 2, 4, 64))
    for f in range(2):
        ahead[:, f, 0, :, :, 0, f], ahead[:, f, 1, :, :, 0, f] = c, s
        ahead[:, f, 0, :, :, 1, f], ahead[:, f, 1, :, :, 1, f] = -s, c
    ahead[:, 0, 1, :, :, 0, 2], ahead[:, 0, 1, :, :, 1, 2] = c, -s
    t["y"] = ahead.reshape(256, 512)
    c, s = cos_sin(64, np.arange(64), np.arange(64))
    c, s = c.reshape(64, 4, 16) / 8.0, s.reshape(64, 4, 16) / 8.0
    back = np.zeros((2, 2, 64, 4, 2, 2, 16))
    for f in range(2):
        back[0, f, :, :, f, 0], back[1, f, :, :, f, 0] = c, -s
        back[0, f, :, :, f, 1], back[1, f, :, :, f, 1] = s, c
    t["y_back"] = back.reshape(256, 256)
    for odd, name in enumerate(("x_even", "x_odd")):
        c, s = cos_sin(128, 2 * short + odd, short)
        t[name] = np.block([[c, s], [-s, c]]) / np.sqrt(128.0)
        c, s = cos_sin(128, 2 * short + odd, some)
        t[name + "_back"] = np.block([[c, -s], [s, c]]) / np.sqrt(128.0)
    d1x, d1y, d1z = first_symbol(NX), first_symbol(NY), first_symbol(NZ)
    d2x, d2y, d2z = second_symbol(NX), second_symbol(NY), second_symbol(NZ)
    column = np.zeros((128, 128))
    column[:, 0], column[:, 1] = -INVERSE[0, 0] * d2x[by_row] / JACOBI_SCALE, d1x[by_row]
    by_ky = np.zeros((8, 256))
    by_ky[0] = np.tile(-INVERSE[1, 1] * d2y / JACOBI_SCALE, 4)
    by_ky[1] = np.tile(2.0 * INVERSE[1, 2] * d1y / JACOBI_SCALE, 4)
    by_ky[2] = np.tile(2.0 * INVERSE[0, 1] * d1y / JACOBI_SCALE, 4)
    by_kz = np.zeros((256, 128))
    low = np.concatenate([by_row, by_row + 128])
    for f, kz in enumerate((low, low + 256, 0 * low + 512)):
        by_kz[:, 2 * f], by_kz[:, 2 * f + 1] = -INVERSE[2, 2] * d2z[kz] / JACOBI_SCALE, d1z[kz]
    t["column"], t["by_ky"], t["by_kz"] = column, by_ky, by_kz
    angle = (np.arange(NODES) + 0.5) * np.pi / NODES
    nodes = np.zeros((24, 128))
    nodes[:NODES, :NODES] = 2.0 / NODES * np.cos(np.outer(np.arange(NODES), angle))
    nodes[0, :NODES] = 1.0 / NODES
    nodes[NODES, :NODES] = 0.5 * LARGEST * (1.0 + np.cos(angle))
    t["nodes"] = nodes
    for name in ON_THE_RIGHT:
        high, low = halves_of(t[name])
        t[name] = np.concatenate([high, low], 0)
    for name in ON_THE_LEFT:
        high, low = halves_of(t[name])
        t[name] = np.concatenate([high, low], 1)
    return {n: v if v.dtype == ml_dtypes.bfloat16 else v.astype(np.float32) for n, v in t.items()}


def index_of(shape, dim):
    return lax.broadcasted_iota(jnp.int32, shape, dim)


def solve(gram):
    ff, fc, cc, fs, cs = gram
    ridge = RIDGE_SHARE * 0.5 * (ff + cc)
    ff, cc = ff + ridge, cc + ridge
    determinant = ff * cc - fc * fc
    return (cc * fs - fc * cs) / determinant, (ff * cs - fc * fs) / determinant


def stack_rows(rows, count):
    at = index_of((count, 128), 0)
    stacked = jnp.zeros((count, 128), jnp.float32)
    for n, row in enumerate(rows):
        stacked = jnp.where(at == n, row, stacked)
    return stacked


def sums_of(arrays):
    rows = []
    for array in arrays:
        row = jnp.sum(array, axis=0, keepdims=True)
        rows.append(row[:, :128] + row[:, 128:])
    count = -(-len(rows) // 8) * 8
    return jnp.sum(stack_rows(rows, count), axis=1, keepdims=True)


def parts_of(array):
    high = array.astype(jnp.bfloat16)
    return high, (array - high.astype(jnp.float32)).astype(jnp.bfloat16)


def bf16_dot(a, b, contract=((1,), (0,))):
    return lax.dot_general(a, b, (contract, ((), ())), preferred_element_type=jnp.float32)


def in_two(array, axis):
    high, low = parts_of(array)
    return jnp.concatenate([high, high, low], axis)


def times(data, table):
    return bf16_dot(in_two(data, 1), jnp.concatenate([table[...], table[0 : table.shape[0] // 2, :]], 0))


def applied(table, data):
    return bf16_dot(jnp.concatenate([table[...], table[:, 0 : table.shape[1] // 2]], 1), in_two(data, 0))


def blank_kernel(out):
    out[...] = jnp.zeros((8, 128), jnp.float32)


def slots_kernel(blank, site, charge, atom, tile, shift, out):
    wide = jnp.concatenate([atom[...], jnp.zeros((2, 96), jnp.int32)], 1)
    wide = jnp.concatenate([wide, jnp.zeros((6, 128), jnp.int32)], 0)
    values = []
    for row in [site[0], site[1], site[2], charge[...]]:
        row = jnp.broadcast_to(jnp.concatenate([row, jnp.zeros((1, 112), jnp.float32)], 1), (8, 128))
        chosen = jnp.take_along_axis(row, wide, axis=1, mode="promise_in_bounds")
        values.append(chosen[0:2, 0:32])
    for p in range(3):
        values[p] = values[p] + 4.0 * shift[p].astype(jnp.float32)
    code = tile[...]
    values.append(((code & 15) + 16 * (index_of((2, 32), 1) & 7)).astype(jnp.float32))
    values.append((code >> 4).astype(jnp.float32))
    ux, uy, uz, peak, at, side = values
    nothing = jnp.zeros((2, 32), jnp.float32)
    ordered = [ux, uz, at, nothing, uy, peak, side, nothing]
    lane = index_of((8, 128), 1)
    packed = blank[...]
    for e in range(2):
        rows = [jnp.concatenate([v[e : e + 1], jnp.zeros((1, 96), jnp.float32)], 1) for v in ordered]
        rows = stack_rows(rows, 8)
        for b in range(4):
            moved = pltpu.roll(rows, 8 * b + 8 * e, 1)
            packed = jnp.where((lane >> 3) == 2 * b + e, moved, packed)
    packed = jnp.where(lane < 64, packed, pltpu.roll(pltpu.roll(packed, 4, 0), 64, 1))
    packed = jnp.where(index_of((8, 128), 0) < 4, packed, pltpu.roll(packed, 4, 0))
    place = ((lax.axis_index("gy") * 8 + lax.axis_index("gz")) >> 1) & 7
    out[...] = pltpu.roll(packed, 16 * place, 1)


def send_kernel(density, packed, out):
    above = index_of((8, 128), 0) < 4
    slots = packed[...]
    for n in range(16):
        half, x = n // 8, 2 * n % 16
        even, odd = [density[x + m, 8 * half : 8 * half + 8, :] for m in range(2)]
        odd = pltpu.roll(odd, 4, 0)
        out[24 * n : 24 * n + 8, :] = even
        out[24 * n + 8 : 24 * n + 16, :] = jnp.where(above, slots, odd)
        out[24 * n + 16 : 24 * n + 24, :] = jnp.where(above, odd, slots)


def line_kernel(got, z_tile_even, z_tile_odd, twiddle, z_even, z_odd, out, cells):
    rank = lax.axis_index("gy") * 8 + lax.axis_index("gz")
    x, half = rank & 15, rank >> 4
    own = ((x >> 3) * 2 + half).astype(jnp.float32)
    along = (x & 7).astype(jnp.float32)
    lane = index_of((8, 128), 1)
    at_j = index_of((8, 512), 0).astype(jnp.float32) - 3.5
    tile_at = index_of((128, 512), 0).astype(jnp.float32)
    scale = -LOG2E / WIDTH_SQUARED
    crossed = [jnp.exp2(2.0 * scale * METRIC[1, 2] * (k - 3.5) * at_j) for k in range(8)]
    above = index_of((8, 128), 0) < 4
    bricks, pairs = [], []
    for n in range(16):
        middle, last = got[24 * n + 8 : 24 * n + 16, :], got[24 * n + 16 : 24 * n + 24, :]
        bricks += [got[24 * n : 24 * n + 8, :], pltpu.roll(jnp.where(above, last, middle), 4, 0)]
        pairs.append(jnp.where(above, middle, last))
    charge = []
    for b in range(4):
        sides = []
        for side in range(2):
            parts = []
            for g in range(2):
                part = jnp.zeros((8, 128), jnp.float32)
                for r in range(8):
                    part = jnp.where((lane >> 4) == (r + b + 4 * side) % 8, pairs[8 * g + r], part)
                parts.append(pltpu.roll(part, 64, 1) if side else part)
            parts += [pltpu.roll(part, 4, 0) for part in parts]
            sides.append(jnp.concatenate(parts, 1))
        one, two = sides
        slots = [one[0:1], two[0:1], one[1:2], two[1:2], one[2:3], two[2:3]]
        ex = along - slots[0]
        vy, vz = slots[1] - 3.5, slots[2] - 3.5
        m = METRIC
        fixed = m[0, 0] * ex * ex + m[1, 1] * vy * vy + m[2, 2] * vz * vz
        fixed = fixed - 2.0 * m[0, 1] * ex * vy - 2.0 * m[0, 2] * ex * vz + 2.0 * m[1, 2] * vy * vz
        by_j = -2.0 * m[1, 1] * vy + 2.0 * m[0, 1] * ex - 2.0 * m[1, 2] * vz
        by_k = -2.0 * m[2, 2] * vz + 2.0 * m[0, 2] * ex - 2.0 * m[1, 2] * vy
        peak = jnp.where(slots[5] == own, slots[3], 0.0)
        by_row = peak * jnp.exp2(scale * (fixed + at_j * by_k + m[2, 2] * at_j * at_j))
        by_cell = jnp.exp2(scale * at_j * (by_j + m[1, 1] * at_j))
        blocks = jnp.concatenate([by_row[k : k + 1] * (by_cell * crossed[k]) for k in range(8)], 0)
        placed = jnp.where(slots[4] == tile_at, 1.0, 0.0).astype(jnp.bfloat16)
        parts = jnp.concatenate(parts_of(blocks), 0)
        sums = bf16_dot(parts, placed, ((1,), (1,)))
        charge.append(sums[0:64] + sums[64:128])
    charge = [charge[b][8 * k : 8 * k + 8] for k in range(8) for b in range(4)]
    charge = [jnp.transpose(jnp.concatenate(charge[16 * n : 16 * n + 16], 0)) for n in range(2)]
    charge = jnp.concatenate(charge, 1)
    for c in range(8):
        piece = jnp.concatenate([bricks[8 * b + c] for b in range(4)], 0)
        cells[128 * c : 128 * c + 128, :] = jnp.transpose(jnp.concatenate([piece] * 4, 0))
    group = index_of((128, 128), 1) >> 5
    sides = []
    for side in range(2):
        total = jnp.zeros((128, 128), jnp.float32)
        for n in range(4):
            total = jnp.where(group == n, cells[pl.ds(4 * side + n, 128, stride=8), :], total)
        sides.append(total)
    field = jnp.concatenate(sides, 1) + charge
    even = applied(z_tile_even, field[:64] + field[64:])
    odd = applied(z_tile_odd, field[:64] - field[64:])
    re, im = [jnp.concatenate([even[n : n + 64], odd[n : n + 64]], 0) for n in (0, 64)]
    re, im = re * twiddle[0] + im * twiddle[1], im * twiddle[0] - re * twiddle[1]
    even = jnp.concatenate([re[:, :128] + re[:, 128:], im[:, :128] + im[:, 128:]], 1)
    odd = jnp.concatenate([re[:, :128] - re[:, 128:], im[:, :128] - im[:, 128:]], 1)
    out[0:128, :] = times(even, z_even)
    out[128:256, :] = times(odd, z_odd)
    last = jnp.where((lane >> 5) & 1 == 0, even[0:8, 0:128], -even[0:8, 0:128])
    last = last + pltpu.roll(last, 64, 1)
    last = last + pltpu.roll(last, 32, 1)
    here = (index_of((8, 128), 0) == 0) & ((lane >> 5) == 1)
    out[0:8, :] = jnp.where(here, last, out[0:8, :])


def own_rank():
    return (lax.axis_index("gx") * 4 + lax.axis_index("gy")) * 8 + lax.axis_index("gz")


def eigenvalues(column, by_ky, by_kz):
    rank = own_rank()
    mine = by_kz[pl.ds(rank, 1), :]
    field = index_of((1, 256), 1) >> 6
    second, first = [
        jnp.where(field == 0, mine[:, n : n + 1], jnp.where(field == 1, mine[:, n + 2 : n + 3], mine[:, n + 4 : n + 5]))
        for n in range(2)
    ]
    row = by_ky[0:1, :] + second + by_ky[1:2, :] * first
    other = by_ky[2:3, :] + (2.0 * INVERSE[0, 2] / JACOBI_SCALE) * first
    return column[:, 0:1] + row + column[:, 1:2] * other, rank


def weights_of(rank):
    field = index_of((1, 256), 1) >> 6
    first = jnp.where(field == 1, 2.0, jnp.where(field == 3, 0.0, 1.0))
    other = jnp.where(field < 2, 2.0, 0.0)
    return jnp.where(rank == 0, first, other)


def plane_kernel(got, y, x_even, x_odd, column, by_ky, by_kz, nodes, out_re, out_im, out_a, out):
    lam, rank = eigenvalues(column, by_ky, by_kz)
    first = jnp.where(rank == 0, 1.0, 0.0).astype(jnp.float32)
    halves = [jnp.concatenate([got[32 * a + 16 * h : 32 * a + 16 * h + 16, :] for a in range(8)], 0) for h in range(2)]
    lines = times(jnp.concatenate(halves, 1), y)
    even = applied(x_even, jnp.concatenate([lines[:64, n : n + 256] + lines[64:, n : n + 256] for n in (0, 256)], 0))
    odd = applied(x_odd, jnp.concatenate([lines[:64, n : n + 256] - lines[64:, n : n + 256] for n in (0, 256)], 0))
    re, im = [jnp.concatenate([even[n : n + 64], odd[n : n + 64]], 0) for n in (0, 64)]
    re, im = (
        jnp.concatenate([re[:, :128] + first * im[:, 128:], re[:, 128:]], 1),
        jnp.concatenate([im[:, :128] - first * re[:, 128:], im[:, 128:]], 1),
    )
    out_re[...] = re
    out_im[...] = im
    a = STEP * lam
    out_a[...] = a
    power = (re * re + im * im) * weights_of(rank) * a
    double = a * (4.0 / LARGEST) - 2.0
    moments = [power, 0.5 * double * power]
    while len(moments) < NODES:
        moments.append(double * moments[-1] - moments[-2])
    weight = jnp.sum(sums_of(moments) * nodes[0:NODES, :], axis=0, keepdims=True)
    out[...] = jnp.broadcast_to(weight, (256, 128))


def cycle_kernel(got, re_in, im_in, a_in, nodes, x_even_back, x_odd_back, y_back, out):
    weight = jnp.sum(got[...], axis=0, keepdims=True)
    node = nodes[NODES : NODES + 1, :]
    fine = a_in[...]
    first = jnp.where(own_rank() == 0, 1.0, 0.0).astype(jnp.float32)
    sides = [(node, 1.0 - node), (fine, 1.0 - fine)]
    scaled, potential = [1.0, 1.0], 0.0
    for cycle in range(3):
        a, mu = sides[0]
        low = weight * scaled[0] * scaled[0]
        products = [low * a, low * a * mu, low * a * mu * mu, -low * mu * mu, -low * mu * mu * mu]
        g0, g1 = solve([jnp.sum(p, axis=1, keepdims=True) for p in products])
        a, mu = sides[1]
        potential = potential + STEP * scaled[1] * (1.0 + mu * ((1.0 - g0) + (1.0 - g1) * mu))
        if cycle < 2:
            scaled = [s * mu * (mu * mu + a * (g0 + mu * g1)) for s, (a, mu) in zip(scaled, sides)]
    residual = JACOBI_SCALE * scaled[1] * mu * mu
    re, im = re_in[...], im_in[...]
    columns = []
    for multiplier in (potential, residual):
        fr, fi = multiplier * re, multiplier * im
        columns.append(
            jnp.concatenate([fr[:, :128] - first * fi[:, 128:], fi[:, :128] + first * fr[:, 128:]], 0)
        )
    columns = jnp.concatenate(columns, 1)
    low = jnp.concatenate([columns[n : n + 32] for n in range(0, 256, 64)], 0)
    high = jnp.concatenate([columns[n + 32 : n + 64] for n in range(0, 256, 64)], 0)
    planes = jnp.concatenate([applied(x_even_back, low + high), applied(x_odd_back, low - high)], 0)
    lines = []
    for f in range(2):
        for odd in range(2):
            at = 128 * odd
            pair = [planes[at + n : at + n + 64, 128 * f : 128 * f + 128] for n in (0, 64)]
            lines.append(jnp.concatenate(pair, 1))
    lines = times(jnp.concatenate(lines, 0), y_back)
    left = index_of((64, 128), 1) < 64
    for f in range(2):
        for b in range(4):
            side = slice(128 * (b // 2), 128 * (b // 2) + 128)
            even, odd = lines[128 * f : 128 * f + 64, side], lines[128 * f + 64 : 128 * f + 128, side]
            if b % 2 == 0:
                odd = pltpu.roll(odd, 64, 1)
            else:
                even = pltpu.roll(even, 64, 1)
            message = jnp.where(left, even, odd)
            for n in range(8):
                out[pl.ds((32 * n + 8 * b) * 2 + f, 8, stride=2), :] = message[8 * n : 8 * n + 8]


def back_kernel(got, z_tile_back, twiddle, z_even_back, z_odd_back, z_last_back, out, cells):
    spectra = [got[pl.ds(f, 256, stride=2), :] for f in range(2)]
    low = jnp.concatenate([v[:128] for v in spectra], 0)
    high = jnp.concatenate([v[128:] for v in spectra], 0)
    top = index_of((256, 128), 0) & 127 == 0
    part = (index_of((256, 128), 1) & 63) >> 4
    last = jnp.where(top & (part == 1), low, 0.0)
    low = jnp.where(top & (part < 2), jnp.where(part == 0, 0.5 * low, 0.0), low)
    last = times(jnp.concatenate([last[0:8], last[128:136]], 0), z_last_back)
    even, odd = times(low, z_even_back), times(high, z_odd_back)
    turned = []
    for f in range(2):
        e, o = even[128 * f : 128 * f + 128], odd[128 * f : 128 * f + 128]
        real = jnp.concatenate([e[0:8, :128] + last[8 * f : 8 * f + 8], e[8:, :128]], 0)
        re = jnp.concatenate([real + o[:, :128], real - o[:, :128]], 1)
        im = jnp.concatenate([e[:, 128:] + o[:, 128:], e[:, 128:] - o[:, 128:]], 1)
        turned.append(
            jnp.concatenate([re * twiddle[0] - im * twiddle[1], im * twiddle[0] + re * twiddle[1]], 0)
        )
    fields = applied(z_tile_back, jnp.concatenate(turned, 1))
    group = index_of((128, 128), 1) >> 5
    for side in range(2):
        one = fields[:, 128 * side : 128 * side + 128]
        two = pltpu.roll(fields[:, 256 + 128 * side : 384 + 128 * side], 64, 1)
        for n in range(4):
            cells[pl.ds(4 * side + n, 128, stride=8), :] = jnp.where(group == n, one, two)
    turn = index_of((32, 128), 1) & 3
    for c in range(8):
        piece = jnp.transpose(cells[128 * c : 128 * c + 128, :])
        rows = [piece[32 * n : 32 * n + 32] for n in range(4)]
        for f in range(2):
            low = jnp.where(turn == 0, rows[2 * f], rows[(2 * f + 1) % 4])
            high = jnp.where(turn == 2, rows[(2 * f + 2) % 4], rows[(2 * f + 3) % 4])
            out[c, 32 * f : 32 * f + 32, :] = jnp.where(turn < 2, low, high)


def place_kernel(got, potential, residual, done):
    copies = [
        pltpu.make_async_copy(got.at[:, f], out, done.at[f]) for f, out in enumerate((potential, residual))
    ]
    for copy in copies:
        copy.start()
    for copy in copies:
        copy.wait()


VMEM = pl.BlockSpec(memory_space=pltpu.VMEM)
HBM = pl.BlockSpec(memory_space=pltpu.HBM)
SMEM = pl.BlockSpec(memory_space=pltpu.SMEM)


def call(kernel, out_shapes, specs, scratch=(), name=None, result=VMEM, limit=16, cost=None):
    shapes = [jax.ShapeDtypeStruct(s, jnp.float32) for s in out_shapes]
    single = len(shapes) == 1
    return pl.pallas_call(
        kernel,
        out_shape=shapes[0] if single else shapes,
        in_specs=specs,
        out_specs=result if single else [result] * len(shapes),
        scratch_shapes=list(scratch),
        compiler_params=pltpu.CompilerParams(vmem_limit_bytes=limit * 1024 * 1024),
        name=name,
        cost_estimate=cost and pl.CostEstimate(flops=cost, bytes_accessed=cost, transcendentals=0),
    )


def exchanged(array, axes):
    return lax.all_to_all(array, axes, 0, 0, tiled=True)


def per_device(density, atom_site, atom_charge, slot_atom, slot_tile, slot_shift):
    t = {name: jnp.asarray(value) for name, value in tables().items()}
    packed = call(slots_kernel, [(8, 128)], [VMEM] * 6, name="slots")(
        call(blank_kernel, [(8, 128)], [], name="blank", cost=10**8)(),
        atom_site.reshape(3, 1, 16),
        atom_charge.reshape(1, 16),
        slot_atom.reshape(32, 2).T,
        slot_tile.reshape(32, 2).T,
        jnp.swapaxes(slot_shift.reshape(3, 32, 2), 1, 2),
    )
    message = call(send_kernel, [(384, 128)], [VMEM] * 2, name="send")(density, packed)
    got = exchanged(message.reshape(32, 1, 1536), ("gy", "gz")).reshape(384, 128)
    cells = [pltpu.VMEM((1024, 128), jnp.float32)]
    message = call(line_kernel, [(256, 128)], [VMEM] * 6, cells, "line")(
        got, t["z_tile_even"], t["z_tile_odd"], t["twiddle"], t["z_even"], t["z_odd"]
    )
    got = exchanged(message, AXES)
    re, im, a, message = call(plane_kernel, [(128, 256)] * 3 + [(256, 128)], [VMEM] * 8, name="plane")(
        got, t["y"], t["x_even"], t["x_odd"], t["column"], t["by_ky"], t["by_kz"], t["nodes"]
    )
    got = exchanged(message, AXES)
    message = call(cycle_kernel, [(512, 128)], [VMEM] * 8, name="cycle")(
        got, re, im, a, t["nodes"], t["x_even_back"], t["x_odd_back"], t["y_back"]
    )
    got = exchanged(message.reshape(256, 2, 128), AXES).reshape(512, 128)
    message = call(back_kernel, [(8, 64, 128)], [VMEM] * 6, cells, "back")(
        got, t["z_tile_back"], t["twiddle"], t["z_even_back"], t["z_odd_back"], t["z_last_back"]
    )
    got = exchanged(message, "gz").reshape(8, 2, 2, 16, 128)
    place = call(place_kernel, [(8, 2, 16, 128)] * 2, [VMEM], [pltpu.SemaphoreType.DMA((2,))], "place", HBM)
    return tuple(out.reshape(16, 16, 128) for out in place(got))


def solution(mesh):
    return jax.shard_map(
        per_device,
        mesh=mesh,
        in_specs=(
            P("gx", "gy", "gz"),
            P(None, "gx", "gy", "gz", None),
            P("gx", "gy", "gz", None),
            P("gx", "gy", "gz", None, None),
            P("gx", "gy", "gz", None, None),
            P(None, "gx", "gy", "gz", None, None),
        ),
        out_specs=(P("gx", "gy", "gz"), P("gx", "gy", "gz")),
        check_vma=False,
    )
```

```python
import functools

import jax
import jax.numpy as jnp
import ml_dtypes
import numpy as np
from jax import lax
from jax.experimental import pallas as pl
from jax.experimental.pallas import tpu as pltpu
from jax.sharding import PartitionSpec as P


METRIC = np.array([[3.24, 0.972, 0.648], [0.972, 3.2157, 0.9639], [0.648, 0.9639, 2.9565]])
INVERSE = np.array(
    [
        [0.3450043297, -0.0904572938, -0.0461258313],
        [-0.0904572938, 0.3683733435, -0.1002735462],
        [-0.0461258313, -0.1002735462, 0.3810394757],
    ]
)
FIRST_WEIGHTS = np.array([6.0 / 7.0, -15.0 / 56.0, 5.0 / 63.0, -1.0 / 56.0, 2.0 / 385.0, -1.0 / 5544.0])
SECOND_WEIGHTS = 2.0 * FIRST_WEIGHTS / np.arange(1, 7)
CENTER_WEIGHT = -2.0 * SECOND_WEIGHTS.sum()
JACOBI_SCALE = float(-CENTER_WEIGHT * np.trace(INVERSE))
STEP = 0.3
WIDTH_SQUARED = 9.0
RIDGE_SHARE = 0.01
NX, NY, NZ = 128, 64, 1024
AXES = ("gx", "gy", "gz")
LOG2E = float(np.log2(np.e))
NODES = 16
LARGEST = STEP * 2.3721


def cos_sin(n, rows, columns):
    angle = 2.0 * np.pi * (np.outer(rows, columns) % n) / n
    return np.cos(angle), np.sin(angle)


def first_symbol(n):
    angle = 2.0 * np.pi * np.arange(n) / n
    return 2.0 * sum(w * np.sin((o + 1) * angle) for o, w in enumerate(FIRST_WEIGHTS))


def second_symbol(n):
    angle = 2.0 * np.pi * np.arange(n) / n
    return CENTER_WEIGHT + 2.0 * sum(w * np.cos((o + 1) * angle) for o, w in enumerate(SECOND_WEIGHTS))


def halves_of(table):
    high = table.astype(ml_dtypes.bfloat16)
    return high, (table - high.astype(np.float64)).astype(ml_dtypes.bfloat16)


ON_THE_RIGHT = ("z_even", "z_odd", "y", "y_back", "z_even_back", "z_odd_back", "z_last_back")
ON_THE_LEFT = ("x_even", "x_odd", "x_even_back", "x_odd_back")
ON_THE_LEFT += ("z_tile_even", "z_tile_odd", "z_tile_back")


@functools.lru_cache(maxsize=None)
def tables():
    eye = np.eye(32)
    freq = np.arange(128)
    short = np.arange(64)
    by_row = np.concatenate([2 * short, 2 * short + 1])
    some = np.concatenate([2 * short[:32], 2 * short[:32] + 1])
    t = {}
    for odd, name in enumerate(("z_tile_even", "z_tile_odd")):
        c, s = cos_sin(128, 2 * short + odd, short)
        t[name] = np.concatenate([c, -s], 0) / 32.0 / JACOBI_SCALE
    c, s = cos_sin(128, freq, by_row)
    t["z_tile_back"] = np.concatenate([c, -s], 1) / 32.0
    t["twiddle"] = np.stack(cos_sin(1024, by_row, np.arange(256) // 32))
    c, s = cos_sin(8, np.arange(4), np.arange(4))
    half_eye = np.eye(16)
    for odd, name in enumerate(("z_even", "z_odd")):
        ahead = np.zeros((2, 4, 32, 2, 2, 32))
        back = np.zeros((2, 2, 2, 16, 2, 4, 2, 16))
        for k in range(4):
            for n in range(2):
                cc, ss = c[k, 2 * n + odd], s[k, 2 * n + odd]
                ahead[0, k, :, n, 0], ahead[1, k, :, n, 0] = cc * eye, ss * eye
                ahead[0, k, :, n, 1], ahead[1, k, :, n, 1] = -ss * eye, cc * eye
                for x in range(2):
                    back[x, n, 0, :, 0, k, x], back[x, n, 1, :, 0, k, x] = 2.0 * cc * half_eye, -2.0 * ss * half_eye
                    back[x, n, 0, :, 1, k, x], back[x, n, 1, :, 1, k, x] = 2.0 * ss * half_eye, 2.0 * cc * half_eye
        t[name], t[name + "_back"] = ahead.reshape(256, 128), back.reshape(128, 256)
    last = np.zeros((2, 2, 2, 16, 4, 2, 16))
    for k in range(4):
        for x in range(2):
            last[x, 0, 1, :, k, x] = (-1.0) ** k * half_eye
    t["z_last_back"] = last.reshape(128, 128)
    half, b, j = np.meshgrid(np.arange(2), np.arange(4), np.arange(8), indexing="ij")
    c, s = cos_sin(64, (16 * b + 8 * half + j).reshape(-1), np.arange(64))
    c, s = c.reshape(2, 4, 8, 64) / 8.0, s.reshape(2, 4, 8, 64) / 8.0
    ahead = np.zeros((2, 2, 2, 4, 8, 2, 4, 64))
    for f in range(2):
        ahead[:, f, 0, :, :, 0, f], ahead[:, f, 1, :, :, 0, f] = c, s
        ahead[:, f, 0, :, :, 1, f], ahead[:, f, 1, :, :, 1, f] = -s, c
    ahead[:, 0, 1, :, :, 0, 2], ahead[:, 0, 1, :, :, 1, 2] = c, -s
    t["y"] = ahead.reshape(256, 512)
    c, s = cos_sin(64, np.arange(64), np.arange(64))
    c, s = c.reshape(64, 4, 16) / 8.0, s.reshape(64, 4, 16) / 8.0
    back = np.zeros((2, 2, 64, 4, 2, 2, 16))
    for f in range(2):
        back[0, f, :, :, f, 0], back[1, f, :, :, f, 0] = c, -s
        back[0, f, :, :, f, 1], back[1, f, :, :, f, 1] = s, c
    t["y_back"] = back.reshape(256, 256)
    for odd, name in enumerate(("x_even", "x_odd")):
        c, s = cos_sin(128, 2 * short + odd, short)
        t[name] = np.block([[c, s], [-s, c]]) / np.sqrt(128.0)
        c, s = cos_sin(128, 2 * short + odd, some)
        t[name + "_back"] = np.block([[c, -s], [s, c]]) / np.sqrt(128.0)
    d1x, d1y, d1z = first_symbol(NX), first_symbol(NY), first_symbol(NZ)
    d2x, d2y, d2z = second_symbol(NX), second_symbol(NY), second_symbol(NZ)
    column = np.zeros((128, 128))
    column[:, 0], column[:, 1] = -INVERSE[0, 0] * d2x[by_row] / JACOBI_SCALE, d1x[by_row]
    by_ky = np.zeros((8, 256))
    by_ky[0] = np.tile(-INVERSE[1, 1] * d2y / JACOBI_SCALE, 4)
    by_ky[1] = np.tile(2.0 * INVERSE[1, 2] * d1y / JACOBI_SCALE, 4)
    by_ky[2] = np.tile(2.0 * INVERSE[0, 1] * d1y / JACOBI_SCALE, 4)
    by_kz = np.zeros((256, 128))
    low = np.concatenate([by_row, by_row + 128])
    for f, kz in enumerate((low, low + 256, 0 * low + 512)):
        by_kz[:, 2 * f], by_kz[:, 2 * f + 1] = -INVERSE[2, 2] * d2z[kz] / JACOBI_SCALE, d1z[kz]
    t["column"], t["by_ky"], t["by_kz"] = column, by_ky, by_kz
    angle = (np.arange(NODES) + 0.5) * np.pi / NODES
    nodes = np.zeros((24, 128))
    nodes[:NODES, :NODES] = 2.0 / NODES * np.cos(np.outer(np.arange(NODES), angle))
    nodes[0, :NODES] = 1.0 / NODES
    nodes[NODES, :NODES] = 0.5 * LARGEST * (1.0 + np.cos(angle))
    t["nodes"] = nodes
    for name in ON_THE_RIGHT:
        high, low = halves_of(t[name])
        t[name] = np.concatenate([high, low], 0)
    for name in ON_THE_LEFT:
        high, low = halves_of(t[name])
        t[name] = np.concatenate([high, low], 1)
    return {n: v if v.dtype == ml_dtypes.bfloat16 else v.astype(np.float32) for n, v in t.items()}


def index_of(shape, dim):
    return lax.broadcasted_iota(jnp.int32, shape, dim)


def solve(gram):
    ff, fc, cc, fs, cs = gram
    ridge = RIDGE_SHARE * 0.5 * (ff + cc)
    ff, cc = ff + ridge, cc + ridge
    determinant = ff * cc - fc * fc
    return (cc * fs - fc * cs) / determinant, (ff * cs - fc * fs) / determinant


def stack_rows(rows, count):
    at = index_of((count, 128), 0)
    stacked = jnp.zeros((count, 128), jnp.float32)
    for n, row in enumerate(rows):
        stacked = jnp.where(at == n, row, stacked)
    return stacked


def sums_of(arrays):
    rows = []
    for array in arrays:
        row = jnp.sum(array, axis=0, keepdims=True)
        rows.append(row[:, :128] + row[:, 128:])
    count = -(-len(rows) // 8) * 8
    return jnp.sum(stack_rows(rows, count), axis=1, keepdims=True)


def parts_of(array):
    high = array.astype(jnp.bfloat16)
    return high, (array - high.astype(jnp.float32)).astype(jnp.bfloat16)


def bf16_dot(a, b, contract=((1,), (0,))):
    return lax.dot_general(a, b, (contract, ((), ())), preferred_element_type=jnp.float32)


def in_two(array, axis):
    high, low = parts_of(array)
    return jnp.concatenate([high, high, low], axis)


def times(data, table):
    return bf16_dot(in_two(data, 1), jnp.concatenate([table[...], table[0 : table.shape[0] // 2, :]], 0))


def applied(table, data):
    return bf16_dot(jnp.concatenate([table[...], table[:, 0 : table.shape[1] // 2]], 1), in_two(data, 0))


def blank_kernel(out):
    out[...] = jnp.zeros((8, 128), jnp.float32)


def slots_kernel(blank, site, charge, atom, tile, shift, out):
    wide = jnp.concatenate([atom[...], jnp.zeros((2, 96), jnp.int32)], 1)
    wide = jnp.concatenate([wide, jnp.zeros((6, 128), jnp.int32)], 0)
    values = []
    for row in [site[0], site[1], site[2], charge[...]]:
        row = jnp.broadcast_to(jnp.concatenate([row, jnp.zeros((1, 112), jnp.float32)], 1), (8, 128))
        chosen = jnp.take_along_axis(row, wide, axis=1, mode="promise_in_bounds")
        values.append(chosen[0:2, 0:32])
    for p in range(3):
        values[p] = values[p] + 4.0 * shift[p].astype(jnp.float32)
    code = tile[...]
    values.append(((code & 15) + 16 * (index_of((2, 32), 1) & 7)).astype(jnp.float32))
    values.append((code >> 4).astype(jnp.float32))
    ux, uy, uz, peak, at, side = values
    nothing = jnp.zeros((2, 32), jnp.float32)
    ordered = [ux, uz, at, nothing, uy, peak, side, nothing]
    lane = index_of((8, 128), 1)
    packed = blank[...]
    for e in range(2):
        rows = [jnp.concatenate([v[e : e + 1], jnp.zeros((1, 96), jnp.float32)], 1) for v in ordered]
        rows = stack_rows(rows, 8)
        for b in range(4):
            moved = pltpu.roll(rows, 8 * b + 8 * e, 1)
            packed = jnp.where((lane >> 3) == 2 * b + e, moved, packed)
    packed = jnp.where(lane < 64, packed, pltpu.roll(pltpu.roll(packed, 4, 0), 64, 1))
    packed = jnp.where(index_of((8, 128), 0) < 4, packed, pltpu.roll(packed, 4, 0))
    place = ((lax.axis_index("gy") * 8 + lax.axis_index("gz")) >> 1) & 7
    out[...] = pltpu.roll(packed, 16 * place, 1)


def send_kernel(density, packed, out):
    above = index_of((8, 128), 0) < 4
    slots = packed[...]
    for n in range(16):
        half, x = n // 8, 2 * n % 16
        even, odd = [density[x + m, 8 * half : 8 * half + 8, :] for m in range(2)]
        odd = pltpu.roll(odd, 4, 0)
        out[24 * n : 24 * n + 8, :] = even
        out[24 * n + 8 : 24 * n + 16, :] = jnp.where(above, slots, odd)
        out[24 * n + 16 : 24 * n + 24, :] = jnp.where(above, odd, slots)


def line_kernel(got, z_tile_even, z_tile_odd, twiddle, z_even, z_odd, out, cells):
    rank = lax.axis_index("gy") * 8 + lax.axis_index("gz")
    x, half = rank & 15, rank >> 4
    own = ((x >> 3) * 2 + half).astype(jnp.float32)
    along = (x & 7).astype(jnp.float32)
    lane = index_of((8, 128), 1)
    at_j = index_of((8, 512), 0).astype(jnp.float32) - 3.5
    tile_at = index_of((128, 512), 0).astype(jnp.float32)
    scale = -LOG2E / WIDTH_SQUARED
    crossed = [jnp.exp2(2.0 * scale * METRIC[1, 2] * (k - 3.5) * at_j) for k in range(8)]
    above = index_of((8, 128), 0) < 4
    bricks, pairs = [], []
    for n in range(16):
        middle, last = got[24 * n + 8 : 24 * n + 16, :], got[24 * n + 16 : 24 * n + 24, :]
        bricks += [got[24 * n : 24 * n + 8, :], pltpu.roll(jnp.where(above, last, middle), 4, 0)]
        pairs.append(jnp.where(above, middle, last))
    charge = []
    for b in range(4):
        sides = []
        for side in range(2):
            parts = []
            for g in range(2):
                part = jnp.zeros((8, 128), jnp.float32)
                for r in range(8):
                    part = jnp.where((lane >> 4) == (r + b + 4 * side) % 8, pairs[8 * g + r], part)
                parts.append(pltpu.roll(part, 64, 1) if side else part)
            parts += [pltpu.roll(part, 4, 0) for part in parts]
            sides.append(jnp.concatenate(parts, 1))
        one, two = sides
        slots = [one[0:1], two[0:1], one[1:2], two[1:2], one[2:3], two[2:3]]
        ex = along - slots[0]
        vy, vz = slots[1] - 3.5, slots[2] - 3.5
        m = METRIC
        fixed = m[0, 0] * ex * ex + m[1, 1] * vy * vy + m[2, 2] * vz * vz
        fixed = fixed - 2.0 * m[0, 1] * ex * vy - 2.0 * m[0, 2] * ex * vz + 2.0 * m[1, 2] * vy * vz
        by_j = -2.0 * m[1, 1] * vy + 2.0 * m[0, 1] * ex - 2.0 * m[1, 2] * vz
        by_k = -2.0 * m[2, 2] * vz + 2.0 * m[0, 2] * ex - 2.0 * m[1, 2] * vy
        peak = jnp.where(slots[5] == own, slots[3], 0.0)
        by_row = peak * jnp.exp2(scale * (fixed + at_j * by_k + m[2, 2] * at_j * at_j))
        by_cell = jnp.exp2(scale * at_j * (by_j + m[1, 1] * at_j))
        blocks = jnp.concatenate([by_row[k : k + 1] * (by_cell * crossed[k]) for k in range(8)], 0)
        placed = jnp.where(slots[4] == tile_at, 1.0, 0.0).astype(jnp.bfloat16)
        parts = jnp.concatenate(parts_of(blocks), 0)
        sums = bf16_dot(parts, placed, ((1,), (1,)))
        charge.append(sums[0:64] + sums[64:128])
    charge = [charge[b][8 * k : 8 * k + 8] for k in range(8) for b in range(4)]
    charge = [jnp.transpose(jnp.concatenate(charge[16 * n : 16 * n + 16], 0)) for n in range(2)]
    charge = jnp.concatenate(charge, 1)
    for c in range(8):
        piece = jnp.concatenate([bricks[8 * b + c] for b in range(4)], 0)
        cells[128 * c : 128 * c + 128, :] = jnp.transpose(jnp.concatenate([piece] * 4, 0))
    group = index_of((128, 128), 1) >> 5
    sides = []
    for side in range(2):
        total = jnp.zeros((128, 128), jnp.float32)
        for n in range(4):
            total = jnp.where(group == n, cells[pl.ds(4 * side + n, 128, stride=8), :], total)
        sides.append(total)
    field = jnp.concatenate(sides, 1) + charge
    even = applied(z_tile_even, field[:64] + field[64:])
    odd = applied(z_tile_odd, field[:64] - field[64:])
    re, im = [jnp.concatenate([even[n : n + 64], odd[n : n + 64]], 0) for n in (0, 64)]
    re, im = re * twiddle[0] + im * twiddle[1], im * twiddle[0] - re * twiddle[1]
    even = jnp.concatenate([re[:, :128] + re[:, 128:], im[:, :128] + im[:, 128:]], 1)
    odd = jnp.concatenate([re[:, :128] - re[:, 128:], im[:, :128] - im[:, 128:]], 1)
    out[0:128, :] = times(even, z_even)
    out[128:256, :] = times(odd, z_odd)
    last = jnp.where((lane >> 5) & 1 == 0, even[0:8, 0:128], -even[0:8, 0:128])
    last = last + pltpu.roll(last, 64, 1)
    last = last + pltpu.roll(last, 32, 1)
    here = (index_of((8, 128), 0) == 0) & ((lane >> 5) == 1)
    out[0:8, :] = jnp.where(here, last, out[0:8, :])


def own_rank():
    return (lax.axis_index("gx") * 4 + lax.axis_index("gy")) * 8 + lax.axis_index("gz")


def eigenvalues(column, by_ky, by_kz):
    rank = own_rank()
    mine = by_kz[pl.ds(rank, 1), :]
    field = index_of((1, 256), 1) >> 6
    second, first = [
        jnp.where(field == 0, mine[:, n : n + 1], jnp.where(field == 1, mine[:, n + 2 : n + 3], mine[:, n + 4 : n + 5]))
        for n in range(2)
    ]
    row = by_ky[0:1, :] + second + by_ky[1:2, :] * first
    other = by_ky[2:3, :] + (2.0 * INVERSE[0, 2] / JACOBI_SCALE) * first
    return column[:, 0:1] + row + column[:, 1:2] * other, rank


def weights_of(rank):
    field = index_of((1, 256), 1) >> 6
    first = jnp.where(field == 1, 2.0, jnp.where(field == 3, 0.0, 1.0))
    other = jnp.where(field < 2, 2.0, 0.0)
    return jnp.where(rank == 0, first, other)


def plane_kernel(got, y, x_even, x_odd, column, by_ky, by_kz, nodes, out_re, out_im, out_a, out):
    lam, rank = eigenvalues(column, by_ky, by_kz)
    first = jnp.where(rank == 0, 1.0, 0.0).astype(jnp.float32)
    halves = [jnp.concatenate([got[32 * a + 16 * h : 32 * a + 16 * h + 16, :] for a in range(8)], 0) for h in range(2)]
    lines = times(jnp.concatenate(halves, 1), y)
    even = applied(x_even, jnp.concatenate([lines[:64, n : n + 256] + lines[64:, n : n + 256] for n in (0, 256)], 0))
    odd = applied(x_odd, jnp.concatenate([lines[:64, n : n + 256] - lines[64:, n : n + 256] for n in (0, 256)], 0))
    re, im = [jnp.concatenate([even[n : n + 64], odd[n : n + 64]], 0) for n in (0, 64)]
    re, im = (
        jnp.concatenate([re[:, :128] + first * im[:, 128:], re[:, 128:]], 1),
        jnp.concatenate([im[:, :128] - first * re[:, 128:], im[:, 128:]], 1),
    )
    out_re[...] = re
    out_im[...] = im
    a = STEP * lam
    out_a[...] = a
    power = (re * re + im * im) * weights_of(rank) * a
    double = a * (4.0 / LARGEST) - 2.0
    moments = [power, 0.5 * double * power]
    while len(moments) < NODES:
        moments.append(double * moments[-1] - moments[-2])
    weight = jnp.sum(sums_of(moments) * nodes[0:NODES, :], axis=0, keepdims=True)
    out[...] = jnp.broadcast_to(weight, (256, 128))


def cycle_kernel(got, re_in, im_in, a_in, nodes, x_even_back, x_odd_back, y_back, out):
    weight = jnp.sum(got[...], axis=0, keepdims=True)
    node = nodes[NODES : NODES + 1, :]
    fine = a_in[...]
    first = jnp.where(own_rank() == 0, 1.0, 0.0).astype(jnp.float32)
    sides = [(node, 1.0 - node), (fine, 1.0 - fine)]
    scaled, potential = [1.0, 1.0], 0.0
    for cycle in range(3):
        a, mu = sides[0]
        low = weight * scaled[0] * scaled[0]
        products = [low * a, low * a * mu, low * a * mu * mu, -low * mu * mu, -low * mu * mu * mu]
        g0, g1 = solve([jnp.sum(p, axis=1, keepdims=True) for p in products])
        a, mu = sides[1]
        potential = potential + STEP * scaled[1] * (1.0 + mu * ((1.0 - g0) + (1.0 - g1) * mu))
        if cycle < 2:
            scaled = [s * mu * (mu * mu + a * (g0 + mu * g1)) for s, (a, mu) in zip(scaled, sides)]
    residual = JACOBI_SCALE * scaled[1] * mu * mu
    re, im = re_in[...], im_in[...]
    columns = []
    for multiplier in (potential, residual):
        fr, fi = multiplier * re, multiplier * im
        columns.append(
            jnp.concatenate([fr[:, :128] - first * fi[:, 128:], fi[:, :128] + first * fr[:, 128:]], 0)
        )
    columns = jnp.concatenate(columns, 1)
    low = jnp.concatenate([columns[n : n + 32] for n in range(0, 256, 64)], 0)
    high = jnp.concatenate([columns[n + 32 : n + 64] for n in range(0, 256, 64)], 0)
    planes = jnp.concatenate([applied(x_even_back, low + high), applied(x_odd_back, low - high)], 0)
    lines = []
    for f in range(2):
        for odd in range(2):
            at = 128 * odd
            pair = [planes[at + n : at + n + 64, 128 * f : 128 * f + 128] for n in (0, 64)]
            lines.append(jnp.concatenate(pair, 1))
    lines = times(jnp.concatenate(lines, 0), y_back)
    left = index_of((64, 128), 1) < 64
    for f in range(2):
        for b in range(4):
            side = slice(128 * (b // 2), 128 * (b // 2) + 128)
            even, odd = lines[128 * f : 128 * f + 64, side], lines[128 * f + 64 : 128 * f + 128, side]
            if b % 2 == 0:
                odd = pltpu.roll(odd, 64, 1)
            else:
                even = pltpu.roll(even, 64, 1)
            message = jnp.where(left, even, odd)
            for n in range(8):
                out[pl.ds((32 * n + 8 * b) * 2 + f, 8, stride=2), :] = message[8 * n : 8 * n + 8]


def back_kernel(got, z_tile_back, twiddle, z_even_back, z_odd_back, z_last_back, out, cells):
    spectra = [got[pl.ds(f, 256, stride=2), :] for f in range(2)]
    low = jnp.concatenate([v[:128] for v in spectra], 0)
    high = jnp.concatenate([v[128:] for v in spectra], 0)
    top = index_of((256, 128), 0) & 127 == 0
    part = (index_of((256, 128), 1) & 63) >> 4
    last = jnp.where(top & (part == 1), low, 0.0)
    low = jnp.where(top & (part < 2), jnp.where(part == 0, 0.5 * low, 0.0), low)
    last = times(jnp.concatenate([last[0:8], last[128:136]], 0), z_last_back)
    even, odd = times(low, z_even_back), times(high, z_odd_back)
    turned = []
    for f in range(2):
        e, o = even[128 * f : 128 * f + 128], odd[128 * f : 128 * f + 128]
        real = jnp.concatenate([e[0:8, :128] + last[8 * f : 8 * f + 8], e[8:, :128]], 0)
        re = jnp.concatenate([real + o[:, :128], real - o[:, :128]], 1)
        im = jnp.concatenate([e[:, 128:] + o[:, 128:], e[:, 128:] - o[:, 128:]], 1)
        turned.append(
            jnp.concatenate([re * twiddle[0] - im * twiddle[1], im * twiddle[0] + re * twiddle[1]], 0)
        )
    fields = applied(z_tile_back, jnp.concatenate(turned, 1))
    group = index_of((128, 128), 1) >> 5
    for side in range(2):
        one = fields[:, 128 * side : 128 * side + 128]
        two = pltpu.roll(fields[:, 256 + 128 * side : 384 + 128 * side], 64, 1)
        for n in range(4):
            cells[pl.ds(4 * side + n, 128, stride=8), :] = jnp.where(group == n, one, two)
    turn = index_of((32, 128), 1) & 3
    for c in range(8):
        piece = jnp.transpose(cells[128 * c : 128 * c + 128, :])
        rows = [piece[32 * n : 32 * n + 32] for n in range(4)]
        for f in range(2):
            low = jnp.where(turn == 0, rows[2 * f], rows[(2 * f + 1) % 4])
            high = jnp.where(turn == 2, rows[(2 * f + 2) % 4], rows[(2 * f + 3) % 4])
            out[c, 32 * f : 32 * f + 32, :] = jnp.where(turn < 2, low, high)


def place_kernel(got, potential, residual, done):
    copies = [
        pltpu.make_async_copy(got.at[:, f], out, done.at[f]) for f, out in enumerate((potential, residual))
    ]
    for copy in copies:
        copy.start()
    for copy in copies:
        copy.wait()


VMEM = pl.BlockSpec(memory_space=pltpu.VMEM)
HBM = pl.BlockSpec(memory_space=pltpu.HBM)
SMEM = pl.BlockSpec(memory_space=pltpu.SMEM)


def call(kernel, out_shapes, specs, scratch=(), name=None, result=VMEM, limit=16, cost=None):
    shapes = [jax.ShapeDtypeStruct(s, jnp.float32) for s in out_shapes]
    single = len(shapes) == 1
    return pl.pallas_call(
        kernel,
        out_shape=shapes[0] if single else shapes,
        in_specs=specs,
        out_specs=result if single else [result] * len(shapes),
        scratch_shapes=list(scratch),
        compiler_params=pltpu.CompilerParams(vmem_limit_bytes=limit * 1024 * 1024),
        name=name,
        cost_estimate=cost and pl.CostEstimate(flops=cost, bytes_accessed=cost, transcendentals=0),
    )


def exchanged(array, axes):
    return lax.all_to_all(array, axes, 0, 0, tiled=True)


def per_device(density, atom_site, atom_charge, slot_atom, slot_tile, slot_shift):
    t = {name: jnp.asarray(value) for name, value in tables().items()}
    packed = call(slots_kernel, [(8, 128)], [VMEM] * 6, name="slots")(
        call(blank_kernel, [(8, 128)], [], name="blank", cost=10**8)(),
        atom_site.reshape(3, 1, 16),
        atom_charge.reshape(1, 16),
        slot_atom.reshape(32, 2).T,
        slot_tile.reshape(32, 2).T,
        jnp.swapaxes(slot_shift.reshape(3, 32, 2), 1, 2),
    )
    message = call(send_kernel, [(384, 128)], [VMEM] * 2, name="send")(density, packed)
    got = exchanged(message.reshape(32, 1, 1536), ("gy", "gz")).reshape(384, 128)
    cells = [pltpu.VMEM((1024, 128), jnp.float32)]
    message = call(line_kernel, [(256, 128)], [VMEM] * 6, cells, "line")(
        got, t["z_tile_even"], t["z_tile_odd"], t["twiddle"], t["z_even"], t["z_odd"]
    )
    got = exchanged(message, AXES)
    re, im, a, message = call(plane_kernel, [(128, 256)] * 3 + [(256, 128)], [VMEM] * 8, name="plane")(
        got, t["y"], t["x_even"], t["x_odd"], t["column"], t["by_ky"], t["by_kz"], t["nodes"]
    )
    got = exchanged(message, AXES)
    message = call(cycle_kernel, [(512, 128)], [VMEM] * 8, name="cycle")(
        got, re, im, a, t["nodes"], t["x_even_back"], t["x_odd_back"], t["y_back"]
    )
    got = exchanged(message.reshape(256, 1, 256), AXES).reshape(512, 128)
    message = call(back_kernel, [(8, 64, 128)], [VMEM] * 6, cells, "back")(
        got, t["z_tile_back"], t["twiddle"], t["z_even_back"], t["z_odd_back"], t["z_last_back"]
    )
    got = exchanged(message.reshape(8, 1, 8192), "gz").reshape(8, 2, 2, 16, 128)
    place = call(place_kernel, [(8, 2, 16, 128)] * 2, [VMEM], [pltpu.SemaphoreType.DMA((2,))], "place", HBM)
    return tuple(out.reshape(16, 16, 128) for out in place(got))


def solution(mesh):
    return jax.shard_map(
        per_device,
        mesh=mesh,
        in_specs=(
            P("gx", "gy", "gz"),
            P(None, "gx", "gy", "gz", None),
            P("gx", "gy", "gz", None),
            P("gx", "gy", "gz", None, None),
            P("gx", "gy", "gz", None, None),
            P(None, "gx", "gy", "gz", None, None),
        ),
        out_specs=(P("gx", "gy", "gz"), P("gx", "gy", "gz")),
        check_vma=False,
    )
```

```python
import functools

import jax
import jax.numpy as jnp
import ml_dtypes
import numpy as np
from jax import lax
from jax.experimental import pallas as pl
from jax.experimental.pallas import tpu as pltpu
from jax.sharding import PartitionSpec as P


METRIC = np.array([[3.24, 0.972, 0.648], [0.972, 3.2157, 0.9639], [0.648, 0.9639, 2.9565]])
INVERSE = np.array(
    [
        [0.3450043297, -0.0904572938, -0.0461258313],
        [-0.0904572938, 0.3683733435, -0.1002735462],
        [-0.0461258313, -0.1002735462, 0.3810394757],
    ]
)
FIRST_WEIGHTS = np.array([6.0 / 7.0, -15.0 / 56.0, 5.0 / 63.0, -1.0 / 56.0, 2.0 / 385.0, -1.0 / 5544.0])
SECOND_WEIGHTS = 2.0 * FIRST_WEIGHTS / np.arange(1, 7)
CENTER_WEIGHT = -2.0 * SECOND_WEIGHTS.sum()
JACOBI_SCALE = float(-CENTER_WEIGHT * np.trace(INVERSE))
STEP = 0.3
WIDTH_SQUARED = 9.0
RIDGE_SHARE = 0.01
NX, NY, NZ = 128, 64, 1024
AXES = ("gx", "gy", "gz")
LOG2E = float(np.log2(np.e))
NODES = 16
LARGEST = STEP * 2.3721


def cos_sin(n, rows, columns):
    angle = 2.0 * np.pi * (np.outer(rows, columns) % n) / n
    return np.cos(angle), np.sin(angle)


def first_symbol(n):
    angle = 2.0 * np.pi * np.arange(n) / n
    return 2.0 * sum(w * np.sin((o + 1) * angle) for o, w in enumerate(FIRST_WEIGHTS))


def second_symbol(n):
    angle = 2.0 * np.pi * np.arange(n) / n
    return CENTER_WEIGHT + 2.0 * sum(w * np.cos((o + 1) * angle) for o, w in enumerate(SECOND_WEIGHTS))


def halves_of(table):
    high = table.astype(ml_dtypes.bfloat16)
    return high, (table - high.astype(np.float64)).astype(ml_dtypes.bfloat16)


ON_THE_RIGHT = ("z_even", "z_odd", "y", "y_back", "z_even_back", "z_odd_back", "z_last_back")
ON_THE_LEFT = ("x_even", "x_odd", "x_even_back", "x_odd_back")
ON_THE_LEFT += ("z_tile_even", "z_tile_odd", "z_tile_back")


@functools.lru_cache(maxsize=None)
def tables():
    eye = np.eye(32)
    freq = np.arange(128)
    short = np.arange(64)
    by_row = np.concatenate([2 * short, 2 * short + 1])
    some = np.concatenate([2 * short[:32], 2 * short[:32] + 1])
    t = {}
    for odd, name in enumerate(("z_tile_even", "z_tile_odd")):
        c, s = cos_sin(128, 2 * short + odd, short)
        t[name] = np.concatenate([c, -s], 0) / 32.0 / JACOBI_SCALE
    c, s = cos_sin(128, freq, by_row)
    t["z_tile_back"] = np.concatenate([c, -s], 1) / 32.0
    t["twiddle"] = np.stack(cos_sin(1024, by_row, np.arange(256) // 32))
    c, s = cos_sin(8, np.arange(4), np.arange(4))
    half_eye = np.eye(16)
    for odd, name in enumerate(("z_even", "z_odd")):
        ahead = np.zeros((2, 4, 32, 2, 2, 32))
        back = np.zeros((2, 2, 2, 16, 2, 4, 2, 16))
        for k in range(4):
            for n in range(2):
                cc, ss = c[k, 2 * n + odd], s[k, 2 * n + odd]
                ahead[0, k, :, n, 0], ahead[1, k, :, n, 0] = cc * eye, ss * eye
                ahead[0, k, :, n, 1], ahead[1, k, :, n, 1] = -ss * eye, cc * eye
                for x in range(2):
                    back[x, n, 0, :, 0, k, x], back[x, n, 1, :, 0, k, x] = 2.0 * cc * half_eye, -2.0 * ss * half_eye
                    back[x, n, 0, :, 1, k, x], back[x, n, 1, :, 1, k, x] = 2.0 * ss * half_eye, 2.0 * cc * half_eye
        t[name], t[name + "_back"] = ahead.reshape(256, 128), back.reshape(128, 256)
    last = np.zeros((2, 2, 2, 16, 4, 2, 16))
    for k in range(4):
        for x in range(2):
            last[x, 0, 1, :, k, x] = (-1.0) ** k * half_eye
    t["z_last_back"] = last.reshape(128, 128)
    half, b, j = np.meshgrid(np.arange(2), np.arange(4), np.arange(8), indexing="ij")
    c, s = cos_sin(64, (16 * b + 8 * half + j).reshape(-1), np.arange(64))
    c, s = c.reshape(2, 4, 8, 64) / 8.0, s.reshape(2, 4, 8, 64) / 8.0
    ahead = np.zeros((2, 2, 2, 4, 8, 2, 4, 64))
    for f in range(2):
        ahead[:, f, 0, :, :, 0, f], ahead[:, f, 1, :, :, 0, f] = c, s
        ahead[:, f, 0, :, :, 1, f], ahead[:, f, 1, :, :, 1, f] = -s, c
    ahead[:, 0, 1, :, :, 0, 2], ahead[:, 0, 1, :, :, 1, 2] = c, -s
    t["y"] = ahead.reshape(256, 512)
    c, s = cos_sin(64, np.arange(64), np.arange(64))
    c, s = c.reshape(64, 4, 16) / 8.0, s.reshape(64, 4, 16) / 8.0
    back = np.zeros((2, 2, 64, 4, 2, 2, 16))
    for f in range(2):
        back[0, f, :, :, f, 0], back[1, f, :, :, f, 0] = c, -s
        back[0, f, :, :, f, 1], back[1, f, :, :, f, 1] = s, c
    t["y_back"] = back.reshape(256, 256)
    for odd, name in enumerate(("x_even", "x_odd")):
        c, s = cos_sin(128, 2 * short + odd, short)
        t[name] = np.block([[c, s], [-s, c]]) / np.sqrt(128.0)
        c, s = cos_sin(128, 2 * short + odd, some)
        t[name + "_back"] = np.block([[c, -s], [s, c]]) / np.sqrt(128.0)
    d1x, d1y, d1z = first_symbol(NX), first_symbol(NY), first_symbol(NZ)
    d2x, d2y, d2z = second_symbol(NX), second_symbol(NY), second_symbol(NZ)
    column = np.zeros((128, 128))
    column[:, 0], column[:, 1] = -INVERSE[0, 0] * d2x[by_row] / JACOBI_SCALE, d1x[by_row]
    by_ky = np.zeros((8, 256))
    by_ky[0] = np.tile(-INVERSE[1, 1] * d2y / JACOBI_SCALE, 4)
    by_ky[1] = np.tile(2.0 * INVERSE[1, 2] * d1y / JACOBI_SCALE, 4)
    by_ky[2] = np.tile(2.0 * INVERSE[0, 1] * d1y / JACOBI_SCALE, 4)
    by_kz = np.zeros((256, 128))
    low = np.concatenate([by_row, by_row + 128])
    for f, kz in enumerate((low, low + 256, 0 * low + 512)):
        by_kz[:, 2 * f], by_kz[:, 2 * f + 1] = -INVERSE[2, 2] * d2z[kz] / JACOBI_SCALE, d1z[kz]
    t["column"], t["by_ky"], t["by_kz"] = column, by_ky, by_kz
    angle = (np.arange(NODES) + 0.5) * np.pi / NODES
    nodes = np.zeros((24, 128))
    nodes[:NODES, :NODES] = 2.0 / NODES * np.cos(np.outer(np.arange(NODES), angle))
    nodes[0, :NODES] = 1.0 / NODES
    nodes[NODES, :NODES] = 0.5 * LARGEST * (1.0 + np.cos(angle))
    t["nodes"] = nodes
    for name in ON_THE_RIGHT:
        high, low = halves_of(t[name])
        t[name] = np.concatenate([high, low], 0)
    for name in ON_THE_LEFT:
        high, low = halves_of(t[name])
        t[name] = np.concatenate([high, low], 1)
    for name in ("z_tile", "x", "z", "x_back", "z_back"):
        end = "_back" if name.endswith("_back") else ""
        even, odd = [t.pop(name.removesuffix("_back") + side + end) for side in ("_even", "_odd")]
        t[name + "_pair"] = np.concatenate([even, odd], 0)
    t["by_row"] = np.concatenate([t.pop("column"), t.pop("by_kz")], 0)
    return {n: v if v.dtype == ml_dtypes.bfloat16 else v.astype(np.float32) for n, v in t.items()}


def index_of(shape, dim):
    return lax.broadcasted_iota(jnp.int32, shape, dim)


def solve(gram):
    ff, fc, cc, fs, cs = gram
    ridge = RIDGE_SHARE * 0.5 * (ff + cc)
    ff, cc = ff + ridge, cc + ridge
    determinant = ff * cc - fc * fc
    return (cc * fs - fc * cs) / determinant, (ff * cs - fc * fs) / determinant


def stack_rows(rows, count):
    at = index_of((count, 128), 0)
    stacked = jnp.zeros((count, 128), jnp.float32)
    for n, row in enumerate(rows):
        stacked = jnp.where(at == n, row, stacked)
    return stacked


def sums_of(arrays):
    rows = []
    for array in arrays:
        row = jnp.sum(array, axis=0, keepdims=True)
        rows.append(row[:, :128] + row[:, 128:])
    count = -(-len(rows) // 8) * 8
    return jnp.sum(stack_rows(rows, count), axis=1, keepdims=True)


def parts_of(array):
    high = array.astype(jnp.bfloat16)
    return high, (array - high.astype(jnp.float32)).astype(jnp.bfloat16)


def bf16_dot(a, b, contract=((1,), (0,))):
    return lax.dot_general(a, b, (contract, ((), ())), preferred_element_type=jnp.float32)


def in_two(array, axis):
    high, low = parts_of(array)
    return jnp.concatenate([high, high, low], axis)


def times(data, table):
    return bf16_dot(in_two(data, 1), jnp.concatenate([table[...], table[0 : table.shape[0] // 2, :]], 0))


def applied(table, data):
    return bf16_dot(jnp.concatenate([table[...], table[:, 0 : table.shape[1] // 2]], 1), in_two(data, 0))


def blank_kernel(out):
    out[...] = jnp.zeros((8, 128), jnp.float32)


def slots_kernel(blank, site, charge, atom, tile, shift, out):
    wide = jnp.concatenate([atom[...], jnp.zeros((2, 96), jnp.int32)], 1)
    wide = jnp.concatenate([wide, jnp.zeros((6, 128), jnp.int32)], 0)
    values = []
    for row in [site[0], site[1], site[2], charge[...]]:
        row = jnp.broadcast_to(jnp.concatenate([row, jnp.zeros((1, 112), jnp.float32)], 1), (8, 128))
        chosen = jnp.take_along_axis(row, wide, axis=1, mode="promise_in_bounds")
        values.append(chosen[0:2, 0:32])
    for p in range(3):
        values[p] = values[p] + 4.0 * shift[p].astype(jnp.float32)
    code = tile[...]
    values.append(((code & 15) + 16 * (index_of((2, 32), 1) & 7)).astype(jnp.float32))
    values.append((code >> 4).astype(jnp.float32))
    ux, uy, uz, peak, at, side = values
    nothing = jnp.zeros((2, 32), jnp.float32)
    ordered = [ux, uz, at, nothing, uy, peak, side, nothing]
    lane = index_of((8, 128), 1)
    packed = blank[...]
    for e in range(2):
        rows = [jnp.concatenate([v[e : e + 1], jnp.zeros((1, 96), jnp.float32)], 1) for v in ordered]
        rows = stack_rows(rows, 8)
        for b in range(4):
            moved = pltpu.roll(rows, 8 * b + 8 * e, 1)
            packed = jnp.where((lane >> 3) == 2 * b + e, moved, packed)
    packed = jnp.where(lane < 64, packed, pltpu.roll(pltpu.roll(packed, 4, 0), 64, 1))
    packed = jnp.where(index_of((8, 128), 0) < 4, packed, pltpu.roll(packed, 4, 0))
    place = ((lax.axis_index("gy") * 8 + lax.axis_index("gz")) >> 1) & 7
    out[...] = pltpu.roll(packed, 16 * place, 1)


def send_kernel(density, packed, out):
    above = index_of((8, 128), 0) < 4
    slots = packed[...]
    for n in range(16):
        half, x = n // 8, 2 * n % 16
        even, odd = [density[x + m, 8 * half : 8 * half + 8, :] for m in range(2)]
        odd = pltpu.roll(odd, 4, 0)
        out[24 * n : 24 * n + 8, :] = even
        out[24 * n + 8 : 24 * n + 16, :] = jnp.where(above, slots, odd)
        out[24 * n + 16 : 24 * n + 24, :] = jnp.where(above, odd, slots)


def even_odd(pair):
    rows = pair.shape[0] // 2
    return pair.at[0:rows], pair.at[rows : 2 * rows]


def line_kernel(got, z_tile_pair, twiddle, z_pair, out, cells):
    z_tile_even, z_tile_odd = even_odd(z_tile_pair)
    z_even, z_odd = even_odd(z_pair)
    rank = lax.axis_index("gy") * 8 + lax.axis_index("gz")
    x, half = rank & 15, rank >> 4
    own = ((x >> 3) * 2 + half).astype(jnp.float32)
    along = (x & 7).astype(jnp.float32)
    lane = index_of((8, 128), 1)
    at_j = index_of((8, 512), 0).astype(jnp.float32) - 3.5
    tile_at = index_of((128, 512), 0).astype(jnp.float32)
    scale = -LOG2E / WIDTH_SQUARED
    crossed = [jnp.exp2(2.0 * scale * METRIC[1, 2] * (k - 3.5) * at_j) for k in range(8)]
    above = index_of((8, 128), 0) < 4
    bricks, pairs = [], []
    for n in range(16):
        middle, last = got[24 * n + 8 : 24 * n + 16, :], got[24 * n + 16 : 24 * n + 24, :]
        bricks += [got[24 * n : 24 * n + 8, :], pltpu.roll(jnp.where(above, last, middle), 4, 0)]
        pairs.append(jnp.where(above, middle, last))
    charge = []
    for b in range(4):
        sides = []
        for side in range(2):
            parts = []
            for g in range(2):
                part = jnp.zeros((8, 128), jnp.float32)
                for r in range(8):
                    part = jnp.where((lane >> 4) == (r + b + 4 * side) % 8, pairs[8 * g + r], part)
                parts.append(pltpu.roll(part, 64, 1) if side else part)
            parts += [pltpu.roll(part, 4, 0) for part in parts]
            sides.append(jnp.concatenate(parts, 1))
        one, two = sides
        slots = [one[0:1], two[0:1], one[1:2], two[1:2], one[2:3], two[2:3]]
        ex = along - slots[0]
        vy, vz = slots[1] - 3.5, slots[2] - 3.5
        m = METRIC
        fixed = m[0, 0] * ex * ex + m[1, 1] * vy * vy + m[2, 2] * vz * vz
        fixed = fixed - 2.0 * m[0, 1] * ex * vy - 2.0 * m[0, 2] * ex * vz + 2.0 * m[1, 2] * vy * vz
        by_j = -2.0 * m[1, 1] * vy + 2.0 * m[0, 1] * ex - 2.0 * m[1, 2] * vz
        by_k = -2.0 * m[2, 2] * vz + 2.0 * m[0, 2] * ex - 2.0 * m[1, 2] * vy
        peak = jnp.where(slots[5] == own, slots[3], 0.0)
        by_row = peak * jnp.exp2(scale * (fixed + at_j * by_k + m[2, 2] * at_j * at_j))
        by_cell = jnp.exp2(scale * at_j * (by_j + m[1, 1] * at_j))
        blocks = jnp.concatenate([by_row[k : k + 1] * (by_cell * crossed[k]) for k in range(8)], 0)
        placed = jnp.where(slots[4] == tile_at, 1.0, 0.0).astype(jnp.bfloat16)
        parts = jnp.concatenate(parts_of(blocks), 0)
        sums = bf16_dot(parts, placed, ((1,), (1,)))
        charge.append(sums[0:64] + sums[64:128])
    charge = [charge[b][8 * k : 8 * k + 8] for k in range(8) for b in range(4)]
    charge = [jnp.transpose(jnp.concatenate(charge[16 * n : 16 * n + 16], 0)) for n in range(2)]
    charge = jnp.concatenate(charge, 1)
    for c in range(8):
        piece = jnp.concatenate([bricks[8 * b + c] for b in range(4)], 0)
        cells[128 * c : 128 * c + 128, :] = jnp.transpose(jnp.concatenate([piece] * 4, 0))
    group = index_of((128, 128), 1) >> 5
    sides = []
    for side in range(2):
        total = jnp.zeros((128, 128), jnp.float32)
        for n in range(4):
            total = jnp.where(group == n, cells[pl.ds(4 * side + n, 128, stride=8), :], total)
        sides.append(total)
    field = jnp.concatenate(sides, 1) + charge
    even = applied(z_tile_even, field[:64] + field[64:])
    odd = applied(z_tile_odd, field[:64] - field[64:])
    re, im = [jnp.concatenate([even[n : n + 64], odd[n : n + 64]], 0) for n in (0, 64)]
    re, im = re * twiddle[0] + im * twiddle[1], im * twiddle[0] - re * twiddle[1]
    even = jnp.concatenate([re[:, :128] + re[:, 128:], im[:, :128] + im[:, 128:]], 1)
    odd = jnp.concatenate([re[:, :128] - re[:, 128:], im[:, :128] - im[:, 128:]], 1)
    out[0:128, :] = times(even, z_even)
    out[128:256, :] = times(odd, z_odd)
    last = jnp.where((lane >> 5) & 1 == 0, even[0:8, 0:128], -even[0:8, 0:128])
    last = last + pltpu.roll(last, 64, 1)
    last = last + pltpu.roll(last, 32, 1)
    here = (index_of((8, 128), 0) == 0) & ((lane >> 5) == 1)
    out[0:8, :] = jnp.where(here, last, out[0:8, :])


def own_rank():
    return (lax.axis_index("gx") * 4 + lax.axis_index("gy")) * 8 + lax.axis_index("gz")


def eigenvalues(column, by_ky, by_kz):
    rank = own_rank()
    mine = by_kz[pl.ds(rank, 1), :]
    field = index_of((1, 256), 1) >> 6
    second, first = [
        jnp.where(field == 0, mine[:, n : n + 1], jnp.where(field == 1, mine[:, n + 2 : n + 3], mine[:, n + 4 : n + 5]))
        for n in range(2)
    ]
    row = by_ky[0:1, :] + second + by_ky[1:2, :] * first
    other = by_ky[2:3, :] + (2.0 * INVERSE[0, 2] / JACOBI_SCALE) * first
    return column[:, 0:1] + row + column[:, 1:2] * other, rank


def weights_of(rank):
    field = index_of((1, 256), 1) >> 6
    first = jnp.where(field == 1, 2.0, jnp.where(field == 3, 0.0, 1.0))
    other = jnp.where(field < 2, 2.0, 0.0)
    return jnp.where(rank == 0, first, other)


def plane_kernel(got, y, x_pair, by_row, by_ky, nodes, out_re, out_im, out_a, out):
    x_even, x_odd = even_odd(x_pair)
    column, by_kz = by_row.at[0:128], by_row.at[128:384]
    lam, rank = eigenvalues(column, by_ky, by_kz)
    first = jnp.where(rank == 0, 1.0, 0.0).astype(jnp.float32)
    halves = [jnp.concatenate([got[32 * a + 16 * h : 32 * a + 16 * h + 16, :] for a in range(8)], 0) for h in range(2)]
    lines = times(jnp.concatenate(halves, 1), y)
    even = applied(x_even, jnp.concatenate([lines[:64, n : n + 256] + lines[64:, n : n + 256] for n in (0, 256)], 0))
    odd = applied(x_odd, jnp.concatenate([lines[:64, n : n + 256] - lines[64:, n : n + 256] for n in (0, 256)], 0))
    re, im = [jnp.concatenate([even[n : n + 64], odd[n : n + 64]], 0) for n in (0, 64)]
    re, im = (
        jnp.concatenate([re[:, :128] + first * im[:, 128:], re[:, 128:]], 1),
        jnp.concatenate([im[:, :128] - first * re[:, 128:], im[:, 128:]], 1),
    )
    out_re[...] = re
    out_im[...] = im
    a = STEP * lam
    out_a[...] = a
    power = (re * re + im * im) * weights_of(rank) * a
    double = a * (4.0 / LARGEST) - 2.0
    moments = [power, 0.5 * double * power]
    while len(moments) < NODES:
        moments.append(double * moments[-1] - moments[-2])
    weight = jnp.sum(sums_of(moments) * nodes[0:NODES, :], axis=0, keepdims=True)
    out[...] = jnp.broadcast_to(weight, (256, 128))


def cycle_kernel(got, re_in, im_in, a_in, nodes, x_back_pair, y_back, out):
    x_even_back, x_odd_back = even_odd(x_back_pair)
    weight = jnp.sum(got[...], axis=0, keepdims=True)
    node = nodes[NODES : NODES + 1, :]
    fine = a_in[...]
    first = jnp.where(own_rank() == 0, 1.0, 0.0).astype(jnp.float32)
    sides = [(node, 1.0 - node), (fine, 1.0 - fine)]
    scaled, potential = [1.0, 1.0], 0.0
    for cycle in range(3):
        a, mu = sides[0]
        low = weight * scaled[0] * scaled[0]
        products = [low * a, low * a * mu, low * a * mu * mu, -low * mu * mu, -low * mu * mu * mu]
        g0, g1 = solve([jnp.sum(p, axis=1, keepdims=True) for p in products])
        a, mu = sides[1]
        potential = potential + STEP * scaled[1] * (1.0 + mu * ((1.0 - g0) + (1.0 - g1) * mu))
        if cycle < 2:
            scaled = [s * mu * (mu * mu + a * (g0 + mu * g1)) for s, (a, mu) in zip(scaled, sides)]
    residual = JACOBI_SCALE * scaled[1] * mu * mu
    re, im = re_in[...], im_in[...]
    columns = []
    for multiplier in (potential, residual):
        fr, fi = multiplier * re, multiplier * im
        columns.append(
            jnp.concatenate([fr[:, :128] - first * fi[:, 128:], fi[:, :128] + first * fr[:, 128:]], 0)
        )
    columns = jnp.concatenate(columns, 1)
    low = jnp.concatenate([columns[n : n + 32] for n in range(0, 256, 64)], 0)
    high = jnp.concatenate([columns[n + 32 : n + 64] for n in range(0, 256, 64)], 0)
    planes = jnp.concatenate([applied(x_even_back, low + high), applied(x_odd_back, low - high)], 0)
    lines = []
    for f in range(2):
        for odd in range(2):
            at = 128 * odd
            pair = [planes[at + n : at + n + 64, 128 * f : 128 * f + 128] for n in (0, 64)]
            lines.append(jnp.concatenate(pair, 1))
    lines = times(jnp.concatenate(lines, 0), y_back)
    left = index_of((64, 128), 1) < 64
    for f in range(2):
        for b in range(4):
            side = slice(128 * (b // 2), 128 * (b // 2) + 128)
            even, odd = lines[128 * f : 128 * f + 64, side], lines[128 * f + 64 : 128 * f + 128, side]
            if b % 2 == 0:
                odd = pltpu.roll(odd, 64, 1)
            else:
                even = pltpu.roll(even, 64, 1)
            message = jnp.where(left, even, odd)
            for n in range(8):
                out[pl.ds((32 * n + 8 * b) * 2 + f, 8, stride=2), :] = message[8 * n : 8 * n + 8]


def back_kernel(got, z_tile_back, twiddle, z_back_pair, z_last_back, out, cells):
    z_even_back, z_odd_back = even_odd(z_back_pair)
    spectra = [got[pl.ds(f, 256, stride=2), :] for f in range(2)]
    low = jnp.concatenate([v[:128] for v in spectra], 0)
    high = jnp.concatenate([v[128:] for v in spectra], 0)
    top = index_of((256, 128), 0) & 127 == 0
    part = (index_of((256, 128), 1) & 63) >> 4
    last = jnp.where(top & (part == 1), low, 0.0)
    low = jnp.where(top & (part < 2), jnp.where(part == 0, 0.5 * low, 0.0), low)
    last = times(jnp.concatenate([last[0:8], last[128:136]], 0), z_last_back)
    even, odd = times(low, z_even_back), times(high, z_odd_back)
    turned = []
    for f in range(2):
        e, o = even[128 * f : 128 * f + 128], odd[128 * f : 128 * f + 128]
        real = jnp.concatenate([e[0:8, :128] + last[8 * f : 8 * f + 8], e[8:, :128]], 0)
        re = jnp.concatenate([real + o[:, :128], real - o[:, :128]], 1)
        im = jnp.concatenate([e[:, 128:] + o[:, 128:], e[:, 128:] - o[:, 128:]], 1)
        turned.append(
            jnp.concatenate([re * twiddle[0] - im * twiddle[1], im * twiddle[0] + re * twiddle[1]], 0)
        )
    fields = applied(z_tile_back, jnp.concatenate(turned, 1))
    group = index_of((128, 128), 1) >> 5
    for side in range(2):
        one = fields[:, 128 * side : 128 * side + 128]
        two = pltpu.roll(fields[:, 256 + 128 * side : 384 + 128 * side], 64, 1)
        for n in range(4):
            cells[pl.ds(4 * side + n, 128, stride=8), :] = jnp.where(group == n, one, two)
    turn = index_of((32, 128), 1) & 3
    for c in range(8):
        piece = jnp.transpose(cells[128 * c : 128 * c + 128, :])
        rows = [piece[32 * n : 32 * n + 32] for n in range(4)]
        for f in range(2):
            low = jnp.where(turn == 0, rows[2 * f], rows[(2 * f + 1) % 4])
            high = jnp.where(turn == 2, rows[(2 * f + 2) % 4], rows[(2 * f + 3) % 4])
            out[c, 32 * f : 32 * f + 32, :] = jnp.where(turn < 2, low, high)


def place_kernel(got, potential, residual, done):
    copies = [
        pltpu.make_async_copy(got.at[:, f], out, done.at[f]) for f, out in enumerate((potential, residual))
    ]
    for copy in copies:
        copy.start()
    for copy in copies:
        copy.wait()


VMEM = pl.BlockSpec(memory_space=pltpu.VMEM)
HBM = pl.BlockSpec(memory_space=pltpu.HBM)
SMEM = pl.BlockSpec(memory_space=pltpu.SMEM)


def call(kernel, out_shapes, specs, scratch=(), name=None, result=VMEM, limit=16, cost=None):
    shapes = [jax.ShapeDtypeStruct(s, jnp.float32) for s in out_shapes]
    single = len(shapes) == 1
    return pl.pallas_call(
        kernel,
        out_shape=shapes[0] if single else shapes,
        in_specs=specs,
        out_specs=result if single else [result] * len(shapes),
        scratch_shapes=list(scratch),
        compiler_params=pltpu.CompilerParams(vmem_limit_bytes=limit * 1024 * 1024),
        name=name,
        cost_estimate=cost and pl.CostEstimate(flops=cost, bytes_accessed=cost, transcendentals=0),
    )


def exchanged(array, axes):
    return lax.all_to_all(array, axes, 0, 0, tiled=True)


def per_device(density, atom_site, atom_charge, slot_atom, slot_tile, slot_shift):
    t = {name: jnp.asarray(value) for name, value in tables().items()}
    packed = call(slots_kernel, [(8, 128)], [VMEM] * 6, name="slots")(
        call(blank_kernel, [(8, 128)], [], name="blank", cost=10**8)(),
        atom_site.reshape(3, 1, 16),
        atom_charge.reshape(1, 16),
        slot_atom.reshape(32, 2).T,
        slot_tile.reshape(32, 2).T,
        jnp.swapaxes(slot_shift.reshape(3, 32, 2), 1, 2),
    )
    message = call(send_kernel, [(384, 128)], [VMEM] * 2, name="send")(density, packed)
    got = exchanged(message.reshape(32, 1, 1536), ("gy", "gz")).reshape(384, 128)
    cells = [pltpu.VMEM((1024, 128), jnp.float32)]
    message = call(line_kernel, [(256, 128)], [VMEM] * 4, cells, "line")(
        got, t["z_tile_pair"], t["twiddle"], t["z_pair"]
    )
    got = exchanged(message, AXES)
    re, im, a, message = call(plane_kernel, [(128, 256)] * 3 + [(256, 128)], [VMEM] * 6, name="plane")(
        got, t["y"], t["x_pair"], t["by_row"], t["by_ky"], t["nodes"]
    )
    got = exchanged(message, AXES)
    message = call(cycle_kernel, [(512, 128)], [VMEM] * 7, name="cycle")(
        got, re, im, a, t["nodes"], t["x_back_pair"], t["y_back"]
    )
    got = exchanged(message.reshape(256, 2, 128), AXES).reshape(512, 128)
    message = call(back_kernel, [(8, 64, 128)], [VMEM] * 5, cells, "back")(
        got, t["z_tile_back"], t["twiddle"], t["z_back_pair"], t["z_last_back"]
    )
    got = exchanged(message, "gz").reshape(8, 2, 2, 16, 128)
    place = call(place_kernel, [(8, 2, 16, 128)] * 2, [VMEM], [pltpu.SemaphoreType.DMA((2,))], "place", HBM)
    return tuple(out.reshape(16, 16, 128) for out in place(got))


def solution(mesh):
    return jax.shard_map(
        per_device,
        mesh=mesh,
        in_specs=(
            P("gx", "gy", "gz"),
            P(None, "gx", "gy", "gz", None),
            P("gx", "gy", "gz", None),
            P("gx", "gy", "gz", None, None),
            P("gx", "gy", "gz", None, None),
            P(None, "gx", "gy", "gz", None, None),
        ),
        out_specs=(P("gx", "gy", "gz"), P("gx", "gy", "gz")),
        check_vma=False,
    )
```

```python
import functools

import jax
import jax.numpy as jnp
import ml_dtypes
import numpy as np
from jax import lax
from jax.experimental import pallas as pl
from jax.experimental.pallas import tpu as pltpu
from jax.sharding import PartitionSpec as P


METRIC = np.array([[3.24, 0.972, 0.648], [0.972, 3.2157, 0.9639], [0.648, 0.9639, 2.9565]])
INVERSE = np.array(
    [
        [0.3450043297, -0.0904572938, -0.0461258313],
        [-0.0904572938, 0.3683733435, -0.1002735462],
        [-0.0461258313, -0.1002735462, 0.3810394757],
    ]
)
FIRST_WEIGHTS = np.array([6.0 / 7.0, -15.0 / 56.0, 5.0 / 63.0, -1.0 / 56.0, 2.0 / 385.0, -1.0 / 5544.0])
SECOND_WEIGHTS = 2.0 * FIRST_WEIGHTS / np.arange(1, 7)
CENTER_WEIGHT = -2.0 * SECOND_WEIGHTS.sum()
JACOBI_SCALE = float(-CENTER_WEIGHT * np.trace(INVERSE))
STEP = 0.3
WIDTH_SQUARED = 9.0
RIDGE_SHARE = 0.01
NX, NY, NZ = 128, 64, 1024
AXES = ("gx", "gy", "gz")
LOG2E = float(np.log2(np.e))
NODES = 16
LARGEST = STEP * 2.3721


def cos_sin(n, rows, columns):
    angle = 2.0 * np.pi * (np.outer(rows, columns) % n) / n
    return np.cos(angle), np.sin(angle)


def first_symbol(n):
    angle = 2.0 * np.pi * np.arange(n) / n
    return 2.0 * sum(w * np.sin((o + 1) * angle) for o, w in enumerate(FIRST_WEIGHTS))


def second_symbol(n):
    angle = 2.0 * np.pi * np.arange(n) / n
    return CENTER_WEIGHT + 2.0 * sum(w * np.cos((o + 1) * angle) for o, w in enumerate(SECOND_WEIGHTS))


def halves_of(table):
    high = table.astype(ml_dtypes.bfloat16)
    return high, (table - high.astype(np.float64)).astype(ml_dtypes.bfloat16)


ON_THE_RIGHT = ("z_even", "z_odd", "y", "y_back", "z_even_back", "z_odd_back", "z_last_back")
ON_THE_LEFT = ("x_even", "x_odd", "x_even_back", "x_odd_back")
ON_THE_LEFT += ("z_tile_even", "z_tile_odd", "z_tile_back")


@functools.lru_cache(maxsize=None)
def tables():
    eye = np.eye(32)
    freq = np.arange(128)
    short = np.arange(64)
    by_row = np.concatenate([2 * short, 2 * short + 1])
    some = np.concatenate([2 * short[:32], 2 * short[:32] + 1])
    t = {}
    for odd, name in enumerate(("z_tile_even", "z_tile_odd")):
        c, s = cos_sin(128, 2 * short + odd, short)
        t[name] = np.concatenate([c, -s], 0) / 32.0 / JACOBI_SCALE
    c, s = cos_sin(128, freq, by_row)
    t["z_tile_back"] = np.concatenate([c, -s], 1) / 32.0
    t["twiddle"] = np.stack(cos_sin(1024, by_row, np.arange(256) // 32))
    c, s = cos_sin(8, np.arange(4), np.arange(4))
    half_eye = np.eye(16)
    for odd, name in enumerate(("z_even", "z_odd")):
        ahead = np.zeros((2, 4, 32, 2, 2, 32))
        back = np.zeros((2, 2, 2, 16, 2, 4, 2, 16))
        for k in range(4):
            for n in range(2):
                cc, ss = c[k, 2 * n + odd], s[k, 2 * n + odd]
                ahead[0, k, :, n, 0], ahead[1, k, :, n, 0] = cc * eye, ss * eye
                ahead[0, k, :, n, 1], ahead[1, k, :, n, 1] = -ss * eye, cc * eye
                for x in range(2):
                    back[x, n, 0, :, 0, k, x], back[x, n, 1, :, 0, k, x] = 2.0 * cc * half_eye, -2.0 * ss * half_eye
                    back[x, n, 0, :, 1, k, x], back[x, n, 1, :, 1, k, x] = 2.0 * ss * half_eye, 2.0 * cc * half_eye
        t[name], t[name + "_back"] = ahead.reshape(256, 128), back.reshape(128, 256)
    last = np.zeros((2, 2, 2, 16, 4, 2, 16))
    for k in range(4):
        for x in range(2):
            last[x, 0, 1, :, k, x] = (-1.0) ** k * half_eye
    t["z_last_back"] = last.reshape(128, 128)
    half, b, j = np.meshgrid(np.arange(2), np.arange(4), np.arange(8), indexing="ij")
    c, s = cos_sin(64, (16 * b + 8 * half + j).reshape(-1), np.arange(64))
    c, s = c.reshape(2, 4, 8, 64) / 8.0, s.reshape(2, 4, 8, 64) / 8.0
    ahead = np.zeros((2, 2, 2, 4, 8, 2, 4, 64))
    for f in range(2):
        ahead[:, f, 0, :, :, 0, f], ahead[:, f, 1, :, :, 0, f] = c, s
        ahead[:, f, 0, :, :, 1, f], ahead[:, f, 1, :, :, 1, f] = -s, c
    ahead[:, 0, 1, :, :, 0, 2], ahead[:, 0, 1, :, :, 1, 2] = c, -s
    t["y"] = ahead.reshape(256, 512)
    c, s = cos_sin(64, np.arange(64), np.arange(64))
    c, s = c.reshape(64, 4, 16) / 8.0, s.reshape(64, 4, 16) / 8.0
    back = np.zeros((2, 2, 64, 4, 2, 2, 16))
    for f in range(2):
        back[0, f, :, :, f, 0], back[1, f, :, :, f, 0] = c, -s
        back[0, f, :, :, f, 1], back[1, f, :, :, f, 1] = s, c
    t["y_back"] = back.reshape(256, 256)
    for odd, name in enumerate(("x_even", "x_odd")):
        c, s = cos_sin(128, 2 * short + odd, short)
        t[name] = np.block([[c, s], [-s, c]]) / np.sqrt(128.0)
        c, s = cos_sin(128, 2 * short + odd, some)
        t[name + "_back"] = np.block([[c, -s], [s, c]]) / np.sqrt(128.0)
    d1x, d1y, d1z = first_symbol(NX), first_symbol(NY), first_symbol(NZ)
    d2x, d2y, d2z = second_symbol(NX), second_symbol(NY), second_symbol(NZ)
    column = np.zeros((128, 128))
    column[:, 0], column[:, 1] = -INVERSE[0, 0] * d2x[by_row] / JACOBI_SCALE, d1x[by_row]
    by_ky = np.zeros((8, 256))
    by_ky[0] = np.tile(-INVERSE[1, 1] * d2y / JACOBI_SCALE, 4)
    by_ky[1] = np.tile(2.0 * INVERSE[1, 2] * d1y / JACOBI_SCALE, 4)
    by_ky[2] = np.tile(2.0 * INVERSE[0, 1] * d1y / JACOBI_SCALE, 4)
    by_kz = np.zeros((256, 128))
    low = np.concatenate([by_row, by_row + 128])
    for f, kz in enumerate((low, low + 256, 0 * low + 512)):
        by_kz[:, 2 * f], by_kz[:, 2 * f + 1] = -INVERSE[2, 2] * d2z[kz] / JACOBI_SCALE, d1z[kz]
    t["column"], t["by_ky"], t["by_kz"] = column, by_ky, by_kz
    angle = (np.arange(NODES) + 0.5) * np.pi / NODES
    nodes = np.zeros((24, 128))
    nodes[:NODES, :NODES] = 2.0 / NODES * np.cos(np.outer(np.arange(NODES), angle))
    nodes[0, :NODES] = 1.0 / NODES
    nodes[NODES, :NODES] = 0.5 * LARGEST * (1.0 + np.cos(angle))
    t["nodes"] = nodes
    for name in ON_THE_RIGHT:
        high, low = halves_of(t[name])
        t[name] = np.concatenate([high, low], 0)
    for name in ON_THE_LEFT:
        high, low = halves_of(t[name])
        t[name] = np.concatenate([high, low], 1)
    for name in ("z_tile", "x", "z", "x_back", "z_back"):
        end = "_back" if name.endswith("_back") else ""
        even, odd = [t.pop(name.removesuffix("_back") + side + end) for side in ("_even", "_odd")]
        t[name + "_pair"] = np.concatenate([even, odd], 0)
    t["line"] = np.concatenate([t.pop("z_tile_pair"), t.pop("z_pair")], 0)
    t["cycle"] = np.concatenate([t.pop("x_back_pair"), t.pop("y_back")], 0)
    t["by_row"] = np.concatenate([t.pop("column"), t.pop("by_kz")], 0)
    return {n: v if v.dtype == ml_dtypes.bfloat16 else v.astype(np.float32) for n, v in t.items()}


def index_of(shape, dim):
    return lax.broadcasted_iota(jnp.int32, shape, dim)


def solve(gram):
    ff, fc, cc, fs, cs = gram
    ridge = RIDGE_SHARE * 0.5 * (ff + cc)
    ff, cc = ff + ridge, cc + ridge
    determinant = ff * cc - fc * fc
    return (cc * fs - fc * cs) / determinant, (ff * cs - fc * fs) / determinant


def stack_rows(rows, count):
    at = index_of((count, 128), 0)
    stacked = jnp.zeros((count, 128), jnp.float32)
    for n, row in enumerate(rows):
        stacked = jnp.where(at == n, row, stacked)
    return stacked


def sums_of(arrays):
    rows = []
    for array in arrays:
        row = jnp.sum(array, axis=0, keepdims=True)
        rows.append(row[:, :128] + row[:, 128:])
    count = -(-len(rows) // 8) * 8
    return jnp.sum(stack_rows(rows, count), axis=1, keepdims=True)


def parts_of(array):
    high = array.astype(jnp.bfloat16)
    return high, (array - high.astype(jnp.float32)).astype(jnp.bfloat16)


def bf16_dot(a, b, contract=((1,), (0,))):
    return lax.dot_general(a, b, (contract, ((), ())), preferred_element_type=jnp.float32)


def in_two(array, axis):
    high, low = parts_of(array)
    return jnp.concatenate([high, high, low], axis)


def times(data, table):
    return bf16_dot(in_two(data, 1), jnp.concatenate([table[...], table[0 : table.shape[0] // 2, :]], 0))


def applied(table, data):
    return bf16_dot(jnp.concatenate([table[...], table[:, 0 : table.shape[1] // 2]], 1), in_two(data, 0))


def blank_kernel(out):
    out[...] = jnp.zeros((8, 128), jnp.float32)


def slots_kernel(blank, site, charge, atom, tile, shift, out):
    wide = jnp.concatenate([atom[...], jnp.zeros((2, 96), jnp.int32)], 1)
    wide = jnp.concatenate([wide, jnp.zeros((6, 128), jnp.int32)], 0)
    values = []
    for row in [site[0], site[1], site[2], charge[...]]:
        row = jnp.broadcast_to(jnp.concatenate([row, jnp.zeros((1, 112), jnp.float32)], 1), (8, 128))
        chosen = jnp.take_along_axis(row, wide, axis=1, mode="promise_in_bounds")
        values.append(chosen[0:2, 0:32])
    for p in range(3):
        values[p] = values[p] + 4.0 * shift[p].astype(jnp.float32)
    code = tile[...]
    values.append(((code & 15) + 16 * (index_of((2, 32), 1) & 7)).astype(jnp.float32))
    values.append((code >> 4).astype(jnp.float32))
    ux, uy, uz, peak, at, side = values
    nothing = jnp.zeros((2, 32), jnp.float32)
    ordered = [ux, uz, at, nothing, uy, peak, side, nothing]
    lane = index_of((8, 128), 1)
    packed = blank[...]
    for e in range(2):
        rows = [jnp.concatenate([v[e : e + 1], jnp.zeros((1, 96), jnp.float32)], 1) for v in ordered]
        rows = stack_rows(rows, 8)
        for b in range(4):
            moved = pltpu.roll(rows, 8 * b + 8 * e, 1)
            packed = jnp.where((lane >> 3) == 2 * b + e, moved, packed)
    packed = jnp.where(lane < 64, packed, pltpu.roll(pltpu.roll(packed, 4, 0), 64, 1))
    packed = jnp.where(index_of((8, 128), 0) < 4, packed, pltpu.roll(packed, 4, 0))
    place = ((lax.axis_index("gy") * 8 + lax.axis_index("gz")) >> 1) & 7
    out[...] = pltpu.roll(packed, 16 * place, 1)


def send_kernel(density, packed, out):
    above = index_of((8, 128), 0) < 4
    slots = packed[...]
    for n in range(16):
        half, x = n // 8, 2 * n % 16
        even, odd = [density[x + m, 8 * half : 8 * half + 8, :] for m in range(2)]
        odd = pltpu.roll(odd, 4, 0)
        out[24 * n : 24 * n + 8, :] = even
        out[24 * n + 8 : 24 * n + 16, :] = jnp.where(above, slots, odd)
        out[24 * n + 16 : 24 * n + 24, :] = jnp.where(above, odd, slots)


def even_odd(pair):
    rows = pair.shape[0] // 2
    return pair.at[0:rows], pair.at[rows : 2 * rows]


def line_kernel(got, tables_in, twiddle, out, cells):
    z_tile_even, z_tile_odd = tables_in.at[0:128], tables_in.at[128:256]
    z_even, z_odd = tables_in.at[256:768], tables_in.at[768:1280]
    rank = lax.axis_index("gy") * 8 + lax.axis_index("gz")
    x, half = rank & 15, rank >> 4
    own = ((x >> 3) * 2 + half).astype(jnp.float32)
    along = (x & 7).astype(jnp.float32)
    lane = index_of((8, 128), 1)
    at_j = index_of((8, 512), 0).astype(jnp.float32) - 3.5
    tile_at = index_of((128, 512), 0).astype(jnp.float32)
    scale = -LOG2E / WIDTH_SQUARED
    crossed = [jnp.exp2(2.0 * scale * METRIC[1, 2] * (k - 3.5) * at_j) for k in range(8)]
    above = index_of((8, 128), 0) < 4
    bricks, pairs = [], []
    for n in range(16):
        middle, last = got[24 * n + 8 : 24 * n + 16, :], got[24 * n + 16 : 24 * n + 24, :]
        bricks += [got[24 * n : 24 * n + 8, :], pltpu.roll(jnp.where(above, last, middle), 4, 0)]
        pairs.append(jnp.where(above, middle, last))
    charge = []
    for b in range(4):
        sides = []
        for side in range(2):
            parts = []
            for g in range(2):
                part = jnp.zeros((8, 128), jnp.float32)
                for r in range(8):
                    part = jnp.where((lane >> 4) == (r + b + 4 * side) % 8, pairs[8 * g + r], part)
                parts.append(pltpu.roll(part, 64, 1) if side else part)
            parts += [pltpu.roll(part, 4, 0) for part in parts]
            sides.append(jnp.concatenate(parts, 1))
        one, two = sides
        slots = [one[0:1], two[0:1], one[1:2], two[1:2], one[2:3], two[2:3]]
        ex = along - slots[0]
        vy, vz = slots[1] - 3.5, slots[2] - 3.5
        m = METRIC
        fixed = m[0, 0] * ex * ex + m[1, 1] * vy * vy + m[2, 2] * vz * vz
        fixed = fixed - 2.0 * m[0, 1] * ex * vy - 2.0 * m[0, 2] * ex * vz + 2.0 * m[1, 2] * vy * vz
        by_j = -2.0 * m[1, 1] * vy + 2.0 * m[0, 1] * ex - 2.0 * m[1, 2] * vz
        by_k = -2.0 * m[2, 2] * vz + 2.0 * m[0, 2] * ex - 2.0 * m[1, 2] * vy
        peak = jnp.where(slots[5] == own, slots[3], 0.0)
        by_row = peak * jnp.exp2(scale * (fixed + at_j * by_k + m[2, 2] * at_j * at_j))
        by_cell = jnp.exp2(scale * at_j * (by_j + m[1, 1] * at_j))
        blocks = jnp.concatenate([by_row[k : k + 1] * (by_cell * crossed[k]) for k in range(8)], 0)
        placed = jnp.where(slots[4] == tile_at, 1.0, 0.0).astype(jnp.bfloat16)
        parts = jnp.concatenate(parts_of(blocks), 0)
        sums = bf16_dot(parts, placed, ((1,), (1,)))
        charge.append(sums[0:64] + sums[64:128])
    charge = [charge[b][8 * k : 8 * k + 8] for k in range(8) for b in range(4)]
    charge = [jnp.transpose(jnp.concatenate(charge[16 * n : 16 * n + 16], 0)) for n in range(2)]
    charge = jnp.concatenate(charge, 1)
    for c in range(8):
        piece = jnp.concatenate([bricks[8 * b + c] for b in range(4)], 0)
        cells[128 * c : 128 * c + 128, :] = jnp.transpose(jnp.concatenate([piece] * 4, 0))
    group = index_of((128, 128), 1) >> 5
    sides = []
    for side in range(2):
        total = jnp.zeros((128, 128), jnp.float32)
        for n in range(4):
            total = jnp.where(group == n, cells[pl.ds(4 * side + n, 128, stride=8), :], total)
        sides.append(total)
    field = jnp.concatenate(sides, 1) + charge
    even = applied(z_tile_even, field[:64] + field[64:])
    odd = applied(z_tile_odd, field[:64] - field[64:])
    re, im = [jnp.concatenate([even[n : n + 64], odd[n : n + 64]], 0) for n in (0, 64)]
    re, im = re * twiddle[0] + im * twiddle[1], im * twiddle[0] - re * twiddle[1]
    even = jnp.concatenate([re[:, :128] + re[:, 128:], im[:, :128] + im[:, 128:]], 1)
    odd = jnp.concatenate([re[:, :128] - re[:, 128:], im[:, :128] - im[:, 128:]], 1)
    out[0:128, :] = times(even, z_even)
    out[128:256, :] = times(odd, z_odd)
    last = jnp.where((lane >> 5) & 1 == 0, even[0:8, 0:128], -even[0:8, 0:128])
    last = last + pltpu.roll(last, 64, 1)
    last = last + pltpu.roll(last, 32, 1)
    here = (index_of((8, 128), 0) == 0) & ((lane >> 5) == 1)
    out[0:8, :] = jnp.where(here, last, out[0:8, :])


def own_rank():
    return (lax.axis_index("gx") * 4 + lax.axis_index("gy")) * 8 + lax.axis_index("gz")


def eigenvalues(column, by_ky, by_kz):
    rank = own_rank()
    mine = by_kz[pl.ds(rank, 1), :]
    field = index_of((1, 256), 1) >> 6
    second, first = [
        jnp.where(field == 0, mine[:, n : n + 1], jnp.where(field == 1, mine[:, n + 2 : n + 3], mine[:, n + 4 : n + 5]))
        for n in range(2)
    ]
    row = by_ky[0:1, :] + second + by_ky[1:2, :] * first
    other = by_ky[2:3, :] + (2.0 * INVERSE[0, 2] / JACOBI_SCALE) * first
    return column[:, 0:1] + row + column[:, 1:2] * other, rank


def weights_of(rank):
    field = index_of((1, 256), 1) >> 6
    first = jnp.where(field == 1, 2.0, jnp.where(field == 3, 0.0, 1.0))
    other = jnp.where(field < 2, 2.0, 0.0)
    return jnp.where(rank == 0, first, other)


def plane_kernel(got, y, x_pair, by_row, by_ky, nodes, out_re, out_im, out_a, out):
    x_even, x_odd = even_odd(x_pair)
    column, by_kz = by_row.at[0:128], by_row.at[128:384]
    lam, rank = eigenvalues(column, by_ky, by_kz)
    first = jnp.where(rank == 0, 1.0, 0.0).astype(jnp.float32)
    halves = [jnp.concatenate([got[32 * a + 16 * h : 32 * a + 16 * h + 16, :] for a in range(8)], 0) for h in range(2)]
    lines = times(jnp.concatenate(halves, 1), y)
    even = applied(x_even, jnp.concatenate([lines[:64, n : n + 256] + lines[64:, n : n + 256] for n in (0, 256)], 0))
    odd = applied(x_odd, jnp.concatenate([lines[:64, n : n + 256] - lines[64:, n : n + 256] for n in (0, 256)], 0))
    re, im = [jnp.concatenate([even[n : n + 64], odd[n : n + 64]], 0) for n in (0, 64)]
    re, im = (
        jnp.concatenate([re[:, :128] + first * im[:, 128:], re[:, 128:]], 1),
        jnp.concatenate([im[:, :128] - first * re[:, 128:], im[:, 128:]], 1),
    )
    out_re[...] = re
    out_im[...] = im
    a = STEP * lam
    out_a[...] = a
    power = (re * re + im * im) * weights_of(rank) * a
    double = a * (4.0 / LARGEST) - 2.0
    moments = [power, 0.5 * double * power]
    while len(moments) < NODES:
        moments.append(double * moments[-1] - moments[-2])
    weight = jnp.sum(sums_of(moments) * nodes[0:NODES, :], axis=0, keepdims=True)
    out[...] = jnp.broadcast_to(weight, (256, 128))


def cycle_kernel(got, re_in, im_in, a_in, nodes, tables_in, out):
    x_even_back, x_odd_back, y_back = tables_in.at[0:128], tables_in.at[128:256], tables_in.at[256:768]
    weight = jnp.sum(got[...], axis=0, keepdims=True)
    node = nodes[NODES : NODES + 1, :]
    fine = a_in[...]
    first = jnp.where(own_rank() == 0, 1.0, 0.0).astype(jnp.float32)
    sides = [(node, 1.0 - node), (fine, 1.0 - fine)]
    scaled, potential = [1.0, 1.0], 0.0
    for cycle in range(3):
        a, mu = sides[0]
        low = weight * scaled[0] * scaled[0]
        products = [low * a, low * a * mu, low * a * mu * mu, -low * mu * mu, -low * mu * mu * mu]
        g0, g1 = solve([jnp.sum(p, axis=1, keepdims=True) for p in products])
        a, mu = sides[1]
        potential = potential + STEP * scaled[1] * (1.0 + mu * ((1.0 - g0) + (1.0 - g1) * mu))
        if cycle < 2:
            scaled = [s * mu * (mu * mu + a * (g0 + mu * g1)) for s, (a, mu) in zip(scaled, sides)]
    residual = JACOBI_SCALE * scaled[1] * mu * mu
    re, im = re_in[...], im_in[...]
    columns = []
    for multiplier in (potential, residual):
        fr, fi = multiplier * re, multiplier * im
        columns.append(
            jnp.concatenate([fr[:, :128] - first * fi[:, 128:], fi[:, :128] + first * fr[:, 128:]], 0)
        )
    columns = jnp.concatenate(columns, 1)
    low = jnp.concatenate([columns[n : n + 32] for n in range(0, 256, 64)], 0)
    high = jnp.concatenate([columns[n + 32 : n + 64] for n in range(0, 256, 64)], 0)
    planes = jnp.concatenate([applied(x_even_back, low + high), applied(x_odd_back, low - high)], 0)
    lines = []
    for f in range(2):
        for odd in range(2):
            at = 128 * odd
            pair = [planes[at + n : at + n + 64, 128 * f : 128 * f + 128] for n in (0, 64)]
            lines.append(jnp.concatenate(pair, 1))
    lines = times(jnp.concatenate(lines, 0), y_back)
    left = index_of((64, 128), 1) < 64
    for f in range(2):
        for b in range(4):
            side = slice(128 * (b // 2), 128 * (b // 2) + 128)
            even, odd = lines[128 * f : 128 * f + 64, side], lines[128 * f + 64 : 128 * f + 128, side]
            if b % 2 == 0:
                odd = pltpu.roll(odd, 64, 1)
            else:
                even = pltpu.roll(even, 64, 1)
            message = jnp.where(left, even, odd)
            for n in range(8):
                out[pl.ds((32 * n + 8 * b) * 2 + f, 8, stride=2), :] = message[8 * n : 8 * n + 8]


def back_kernel(got, z_tile_back, twiddle, z_back_pair, z_last_back, out, cells):
    z_even_back, z_odd_back = even_odd(z_back_pair)
    spectra = [got[pl.ds(f, 256, stride=2), :] for f in range(2)]
    low = jnp.concatenate([v[:128] for v in spectra], 0)
    high = jnp.concatenate([v[128:] for v in spectra], 0)
    top = index_of((256, 128), 0) & 127 == 0
    part = (index_of((256, 128), 1) & 63) >> 4
    last = jnp.where(top & (part == 1), low, 0.0)
    low = jnp.where(top & (part < 2), jnp.where(part == 0, 0.5 * low, 0.0), low)
    last = times(jnp.concatenate([last[0:8], last[128:136]], 0), z_last_back)
    even, odd = times(low, z_even_back), times(high, z_odd_back)
    turned = []
    for f in range(2):
        e, o = even[128 * f : 128 * f + 128], odd[128 * f : 128 * f + 128]
        real = jnp.concatenate([e[0:8, :128] + last[8 * f : 8 * f + 8], e[8:, :128]], 0)
        re = jnp.concatenate([real + o[:, :128], real - o[:, :128]], 1)
        im = jnp.concatenate([e[:, 128:] + o[:, 128:], e[:, 128:] - o[:, 128:]], 1)
        turned.append(
            jnp.concatenate([re * twiddle[0] - im * twiddle[1], im * twiddle[0] + re * twiddle[1]], 0)
        )
    fields = applied(z_tile_back, jnp.concatenate(turned, 1))
    group = index_of((128, 128), 1) >> 5
    for side in range(2):
        one = fields[:, 128 * side : 128 * side + 128]
        two = pltpu.roll(fields[:, 256 + 128 * side : 384 + 128 * side], 64, 1)
        for n in range(4):
            cells[pl.ds(4 * side + n, 128, stride=8), :] = jnp.where(group == n, one, two)
    turn = index_of((32, 128), 1) & 3
    for c in range(8):
        piece = jnp.transpose(cells[128 * c : 128 * c + 128, :])
        rows = [piece[32 * n : 32 * n + 32] for n in range(4)]
        for f in range(2):
            low = jnp.where(turn == 0, rows[2 * f], rows[(2 * f + 1) % 4])
            high = jnp.where(turn == 2, rows[(2 * f + 2) % 4], rows[(2 * f + 3) % 4])
            out[c, 32 * f : 32 * f + 32, :] = jnp.where(turn < 2, low, high)


def place_kernel(got, potential, residual, done):
    copies = [
        pltpu.make_async_copy(got.at[:, f], out, done.at[f]) for f, out in enumerate((potential, residual))
    ]
    for copy in copies:
        copy.start()
    for copy in copies:
        copy.wait()


VMEM = pl.BlockSpec(memory_space=pltpu.VMEM)
HBM = pl.BlockSpec(memory_space=pltpu.HBM)
SMEM = pl.BlockSpec(memory_space=pltpu.SMEM)


def call(kernel, out_shapes, specs, scratch=(), name=None, result=VMEM, limit=16, cost=None):
    shapes = [jax.ShapeDtypeStruct(s, jnp.float32) for s in out_shapes]
    single = len(shapes) == 1
    return pl.pallas_call(
        kernel,
        out_shape=shapes[0] if single else shapes,
        in_specs=specs,
        out_specs=result if single else [result] * len(shapes),
        scratch_shapes=list(scratch),
        compiler_params=pltpu.CompilerParams(vmem_limit_bytes=limit * 1024 * 1024),
        name=name,
        cost_estimate=cost and pl.CostEstimate(flops=cost, bytes_accessed=cost, transcendentals=0),
    )


def exchanged(array, axes):
    return lax.all_to_all(array, axes, 0, 0, tiled=True)


def per_device(density, atom_site, atom_charge, slot_atom, slot_tile, slot_shift):
    t = {name: jnp.asarray(value) for name, value in tables().items()}
    packed = call(slots_kernel, [(8, 128)], [VMEM] * 6, name="slots")(
        call(blank_kernel, [(8, 128)], [], name="blank", cost=10**8)(),
        atom_site.reshape(3, 1, 16),
        atom_charge.reshape(1, 16),
        slot_atom.reshape(32, 2).T,
        slot_tile.reshape(32, 2).T,
        jnp.swapaxes(slot_shift.reshape(3, 32, 2), 1, 2),
    )
    message = call(send_kernel, [(384, 128)], [VMEM] * 2, name="send")(density, packed)
    got = exchanged(message.reshape(32, 1, 1536), ("gy", "gz")).reshape(384, 128)
    cells = [pltpu.VMEM((1024, 128), jnp.float32)]
    message = call(line_kernel, [(256, 128)], [VMEM] * 3, cells, "line")(
        got, t["line"], t["twiddle"]
    )
    got = exchanged(message, AXES)
    re, im, a, message = call(plane_kernel, [(128, 256)] * 3 + [(256, 128)], [VMEM] * 6, name="plane")(
        got, t["y"], t["x_pair"], t["by_row"], t["by_ky"], t["nodes"]
    )
    got = exchanged(message, AXES)
    message = call(cycle_kernel, [(512, 128)], [VMEM] * 6, name="cycle")(
        got, re, im, a, t["nodes"], t["cycle"]
    )
    got = exchanged(message.reshape(256, 2, 128), AXES).reshape(512, 128)
    message = call(back_kernel, [(8, 64, 128)], [VMEM] * 5, cells, "back")(
        got, t["z_tile_back"], t["twiddle"], t["z_back_pair"], t["z_last_back"]
    )
    got = exchanged(message, "gz").reshape(8, 2, 2, 16, 128)
    place = call(place_kernel, [(8, 2, 16, 128)] * 2, [VMEM], [pltpu.SemaphoreType.DMA((2,))], "place", HBM)
    return tuple(out.reshape(16, 16, 128) for out in place(got))


def solution(mesh):
    return jax.shard_map(
        per_device,
        mesh=mesh,
        in_specs=(
            P("gx", "gy", "gz"),
            P(None, "gx", "gy", "gz", None),
            P("gx", "gy", "gz", None),
            P("gx", "gy", "gz", None, None),
            P("gx", "gy", "gz", None, None),
            P(None, "gx", "gy", "gz", None, None),
        ),
        out_specs=(P("gx", "gy", "gz"), P("gx", "gy", "gz")),
        check_vma=False,
    )
```
